128 devices in a mesh: ty: 8 (over y, x_lo), tx: 16 (over z, x_hi, core).
Axes of the slice: x: 4 (x_hi: 2, x_lo: 2; x = x_hi * 2 + x_lo), y: 4, z: 4, core: 2. Of those that a mesh axis runs over, the one named last changes fastest.
Arguments:
- object_planes: float32 [2, 8192, 8192], P(None, 'ty', 'tx'), may hold values from -6 to 6
- probe: float32 [2, 2, 128, 128], replicated, may hold values from -6 to 6
- positions: int32 [8, 16, 96, 2], P('ty', 'tx'), may hold values from -64 to 8127, as said below
- counts: int32 [8, 16], P('ty', 'tx'), may hold values from 1 to 96, as said below
- amplitudes: float32 [8, 16, 96, 128, 128], P('ty', 'tx'), may hold values from 0.5 to 6
Outputs:
- object_grad: float32 [2, 8192, 8192], P(None, 'ty', 'tx')
- probe_grad: float32 [2, 2, 128, 128], replicated
The draws below stay inside these ranges and needn't reach their ends.
Inputs may be any that keep to these rules, and one draw needn't show every extreme that they name: `counts`: each tile holds 1 to 96 live positions, some tile exactly 96. `positions`: every slot of tile (i, j), live or not, has its window centre (row + 64, column + 64) inside that tile: rows i * 1024 to (i + 1) * 1024 - 1, columns j * 512 to (j + 1) * 512 - 1.
All inputs are finite; a program needn't handle non-finite values.
Results may differ from the reference program's by a relative error of at most 0.0003.
Values sent between devices are 32-bit elements; how exact they have to be, the bound alone decides.
A program may use at most 192 MiB of HBM per device.

```python
import math
import jax
import jax.numpy as jnp
from jax import lax

WIN = 128
MODES = 2
TH = 1024
TW = 512
CAP = 96
BLOCK = 16
TILES_Y = 8
TILES_X = 16
NY = 8192
NX = 8192


def draw_counts(key, part):
    key = jax.random.fold_in(key, 11)
    first_key, second_key, third_key = jax.random.split(key, 3)
    draw_one = jax.random.randint(first_key, (TILES_Y, TILES_X), 1, CAP + 1)
    draw_two = jax.random.randint(second_key, (TILES_Y, TILES_X), 1, CAP + 1)
    chosen = jax.random.randint(third_key, (), 0, TILES_Y * TILES_X)
    tile_number = jnp.arange(TILES_Y * TILES_X, dtype=jnp.int32).reshape(TILES_Y, TILES_X)
    return jnp.where(tile_number == chosen, CAP, jnp.minimum(draw_one, draw_two)).astype(jnp.int32)


def draw_positions(key, part):
    key = jax.random.fold_in(key, 23)
    row_key, col_key = jax.random.split(key, 2)
    row_offset = jax.random.randint(row_key, (TILES_Y, TILES_X, CAP), 0, TH)
    col_offset = jax.random.randint(col_key, (TILES_Y, TILES_X, CAP), 0, TW)
    row_base = jnp.arange(TILES_Y, dtype=jnp.int32)[:, None, None] * TH
    col_base = jnp.arange(TILES_X, dtype=jnp.int32)[None, :, None] * TW
    row_place = row_base + row_offset - WIN // 2
    col_place = col_base + col_offset - WIN // 2
    return jnp.stack([row_place, col_place], axis=-1).astype(jnp.int32)


def block_levels(rng, shape, shards, smallest, largest):
    factor_of, own = 1.0, jax.random.fold_in(rng, 6)
    for position, shards_of in shards:
        heights = jnp.exp(jax.random.uniform(jax.random.fold_in(own, position), (shards_of,), jnp.float32, smallest / len(shards), largest / len(shards)))
        factor_of = factor_of * jnp.repeat(heights, shape[position] // shards_of).reshape([-1 if axis == position else 1 for axis in range(len(shape))])
    return factor_of


def gaussian(own_key, dims, spread, limit, cuts=(), kind=jnp.bfloat16):
    entries = jax.random.normal(own_key, dims, jnp.float32) * spread
    if len(cuts) > 0:
        entries = block_levels(own_key, dims, cuts, -0.22, 0.18) * entries
    return jnp.clip(entries, min=-limit, max=limit).astype(kind)


def setup_inputs(seed: int = 0) -> dict:
    arg_keys = jax.random.split(jax.random.key(seed), 6)
    object_planes = gaussian(arg_keys[0], (2, NY, NX), 1.0, 6.0, ((1, 8), (2, 16)), jnp.float32)
    probe = gaussian(arg_keys[1], (MODES, 2, WIN, WIN), 1.0, 6.0, (), jnp.float32)
    positions = draw_positions(jax.random.fold_in(arg_keys[5], 71), 0)
    counts = draw_counts(jax.random.fold_in(arg_keys[5], 71), 0)
    amplitudes = jnp.clip(jnp.exp(math.log(6.0) - 2.4849066 * jax.random.uniform(arg_keys[4], (TILES_Y, TILES_X, CAP, WIN, WIN), jnp.float32) ** block_levels(arg_keys[4], (TILES_Y, TILES_X, CAP, WIN, WIN), ((0, 8), (1, 16)), -0.2, 0.2)), 0.5, 6.0)
    return dict(object_planes=object_planes, probe=probe, positions=positions, counts=counts, amplitudes=amplitudes)


INTENSITY_FLOOR = 0.25
HIGHEST_PRECISION = lax.Precision.HIGHEST

def tables(window):
    index_line = jnp.arange(window, dtype=jnp.int32)
    product = index_line[:, None] * index_line[None, :] % window
    angle = 2.0 * math.pi / window * product.astype(jnp.float32)
    scale = 1.0 / math.sqrt(window)
    return (jnp.cos(angle) * scale, jnp.sin(angle) * scale)

def transform(real_part, imag_part, cosine_table, sine_table, direction):
    left_re = jnp.einsum('jk,bmkl->bmjl', cosine_table, real_part, precision=HIGHEST_PRECISION) + direction * jnp.einsum('jk,bmkl->bmjl', sine_table, imag_part, precision=HIGHEST_PRECISION)
    left_im = jnp.einsum('jk,bmkl->bmjl', cosine_table, imag_part, precision=HIGHEST_PRECISION) - direction * jnp.einsum('jk,bmkl->bmjl', sine_table, real_part, precision=HIGHEST_PRECISION)
    out_re = jnp.einsum('bmjk,kl->bmjl', left_re, cosine_table, precision=HIGHEST_PRECISION) + direction * jnp.einsum('bmjk,kl->bmjl', left_im, sine_table, precision=HIGHEST_PRECISION)
    out_im = jnp.einsum('bmjk,kl->bmjl', left_im, cosine_table, precision=HIGHEST_PRECISION) - direction * jnp.einsum('bmjk,kl->bmjl', left_re, sine_table, precision=HIGHEST_PRECISION)
    return (out_re, out_im)

def position_block(patches, measured, live_mask, probe, cosine_table, sine_table):
    object_re = patches[:, 0][:, None]
    object_im = patches[:, 1][:, None]
    probe_re = probe[:, 0][None]
    probe_im = probe[:, 1][None]
    wave_re = probe_re * object_re - probe_im * object_im
    wave_im = probe_re * object_im + probe_im * object_re
    far_re, far_im = transform(wave_re, wave_im, cosine_table, sine_table, 1.0)
    intensity = lax.optimization_barrier(jnp.sum(far_re * far_re + far_im * far_im, axis=1))
    weight = (1.0 - measured / jnp.sqrt(jnp.maximum(intensity, INTENSITY_FLOOR))) * live_mask[:, None, None]
    back_re, back_im = transform(weight[:, None] * far_re, weight[:, None] * far_im, cosine_table, sine_table, -1.0)
    grad_re = lax.optimization_barrier(jnp.sum(probe_re * back_re + probe_im * back_im, axis=1))
    grad_im = lax.optimization_barrier(jnp.sum(probe_re * back_im - probe_im * back_re, axis=1))
    term_re = lax.optimization_barrier(jnp.sum(object_re * back_re + object_im * back_im, axis=0))
    term_im = lax.optimization_barrier(jnp.sum(object_re * back_im - object_im * back_re, axis=0))
    return (jnp.stack([grad_re, grad_im], axis=1), jnp.stack([term_re, term_im], axis=1))

def run_blocks(patches, measured, live_mask, probe, cosine_table, sine_table, block_trips, choose_block):
    patch_grads = jnp.zeros_like(patches)
    probe_sum = jnp.zeros(probe.shape, jnp.float32)

    def advance(turn_index, state_pair):
        grads_now, sum_now = state_pair
        start_row = (choose_block(turn_index) * BLOCK).astype(jnp.int32)
        block_patches = lax.dynamic_slice_in_dim(patches, start_row, BLOCK, 0)
        block_measured = lax.dynamic_slice_in_dim(measured, start_row, BLOCK, 0)
        block_live = lax.dynamic_slice_in_dim(live_mask, start_row, BLOCK, 0)
        block_grads, block_term = position_block(block_patches, block_measured, block_live, probe, cosine_table, sine_table)
        grads_now = lax.dynamic_update_slice_in_dim(grads_now, block_grads, start_row, 0)
        return (grads_now, sum_now + block_term)
    return lax.fori_loop(jnp.int32(0), block_trips.astype(jnp.int32), advance, (patch_grads, probe_sum))

def extract(planes, row_start, col_start, window):
    anchor = jnp.zeros((), jnp.int32)

    def take_one(row_one, col_one):
        return lax.dynamic_slice(planes, (anchor, row_one, col_one), (planes.shape[0], window, window))
    return jax.vmap(take_one)(row_start, col_start)

def deposit(gradient, patch_grads, row_start, col_start):
    anchor = jnp.zeros((), jnp.int32)
    window = patch_grads.shape[2]

    def deposit_one(slot_number, current):
        corner = (anchor, row_start[slot_number], col_start[slot_number])
        present = lax.dynamic_slice(current, corner, (2, window, window))
        return lax.dynamic_update_slice(current, present + patch_grads[slot_number], corner)
    return lax.fori_loop(0, patch_grads.shape[0], deposit_one, gradient)

def reference(object_planes, probe, positions, counts, amplitudes):
    rim_width = WIN // 2
    cosine_table, sine_table = tables(WIN)
    padded = jnp.pad(object_planes, ((0, 0), (rim_width, rim_width), (rim_width, rim_width)))
    gradient = jnp.zeros_like(padded)
    probe_start = jnp.zeros(probe.shape, jnp.float32)
    tile_places = positions.reshape(TILES_Y * TILES_X, CAP, 2)
    tile_counts = counts.reshape(TILES_Y * TILES_X)
    tile_measured = amplitudes.reshape(TILES_Y * TILES_X, CAP, WIN, WIN)

    def one_tile(state_pair, tile_item):
        gradient_now, probe_now = state_pair
        places, live_count, measured = tile_item
        row_start = places[:, 0] + rim_width
        col_start = places[:, 1] + rim_width
        patches = extract(padded, row_start, col_start, WIN)
        slot_index = jnp.arange(CAP, dtype=jnp.int32)
        live_mask = (slot_index < live_count).astype(jnp.float32)
        block_trips = (live_count + BLOCK - 1) // BLOCK
        patch_grads, probe_part = run_blocks(patches, measured, live_mask, probe, cosine_table, sine_table, block_trips, lambda turn_index: turn_index)
        gradient_now = deposit(gradient_now, patch_grads, row_start, col_start)
        return ((gradient_now, probe_now + probe_part), None)
    (gradient, probe_sum), _ = lax.scan(one_tile, (gradient, probe_start), (tile_places, tile_counts, tile_measured))
    object_grad = gradient[:, rim_width:rim_width + NY, rim_width:rim_width + NX]
    probe_grad = probe_sum / float(TILES_Y * TILES_X * CAP)
    return (object_grad, probe_grad)
```

```python
import functools
import math

import jax
import jax.numpy as jnp
import numpy as np
from jax import lax
from jax.experimental import pallas as pl
from jax.experimental.pallas import tpu as pltpu
from jax.sharding import PartitionSpec as P

WIN = 128
RIM = WIN // 2
FLOOR = 0.25
AHEAD = 4


def matrices():
    index = np.arange(WIN)
    angle = 2.0 * math.pi / WIN * ((index[:, None] * index[None, :]) % WIN)
    cosine = np.cos(angle) / math.sqrt(WIN)
    sine = np.sin(angle) / math.sqrt(WIN)
    right = np.block([[cosine, -sine], [sine, cosine]])
    both = np.stack([right, right.T]).astype(np.float32)
    high = both.astype(jnp.bfloat16)
    low = (both - high.astype(np.float32)).astype(jnp.bfloat16)
    return np.stack([high, low], axis=1)


def split(value):
    high = value.astype(jnp.bfloat16)
    low = (value - high.astype(jnp.float32)).astype(jnp.bfloat16)
    return high, low


def dot(a, b):
    return lax.dot_general(a, b, (((1,), (0,)), ((), ())), preferred_element_type=jnp.float32)


def right_product(value, high_w, low_w):
    high, low = split(value)
    return dot(high, high_w) + dot(low, high_w) + dot(high, low_w)


def left_product(value, high_w, low_w):
    high, low = split(value)
    return dot(high_w, high) + dot(high_w, low) + dot(low_w, high)


def blocks(value):
    n = WIN
    return value[:n, :n], value[:n, n:], value[n:, :n], value[n:, n:]


def assemble(a, b, c, d):
    top = jnp.concatenate([a, b], axis=1)
    bottom = jnp.concatenate([c, d], axis=1)
    return jnp.concatenate([top, bottom], axis=0)


def slot_gradient(window_re, window_im, probe_ref, measured, live, w_ref):
    p0r, p0i = probe_ref[0, 0], probe_ref[0, 1]
    p1r, p1i = probe_ref[1, 0], probe_ref[1, 1]
    wave = assemble(
        p0r * window_re - p0i * window_im,
        p0r * window_im + p0i * window_re,
        p1r * window_re - p1i * window_im,
        p1r * window_im + p1i * window_re,
    )
    half = right_product(wave, w_ref[0, 0], w_ref[0, 1])
    m0r, m0i, m1r, m1i = blocks(half)
    far = left_product(assemble(m0r, m1r, m0i, m1i), w_ref[1, 0], w_ref[1, 1])
    f0r, f1r, f0i, f1i = blocks(far)
    intensity = f0r * f0r + f0i * f0i + (f1r * f1r + f1i * f1i)
    weight = live - (live * measured) * lax.rsqrt(jnp.maximum(intensity, FLOOR))
    half = left_product(
        assemble(weight * f0r, weight * f1r, weight * f0i, weight * f1i), w_ref[0, 0], w_ref[0, 1]
    )
    m0r, m1r, m0i, m1i = blocks(half)
    back = right_product(assemble(m0r, m0i, m1r, m1i), w_ref[1, 0], w_ref[1, 1])
    b0r, b0i, b1r, b1i = blocks(back)
    grad_re = p0r * b0r + p0i * b0i + (p1r * b1r + p1i * b1i)
    grad_im = p0r * b0i - p0i * b0r + (p1r * b1i - p1i * b1r)
    terms = (
        window_re * b0r + window_im * b0i,
        window_re * b0i - window_im * b0r,
        window_re * b1r + window_im * b1i,
        window_re * b1i - window_im * b1r,
    )
    return grad_re, grad_im, terms


def body(
    count_ref, place_ref, probe_ref, w_ref, tile_ref, left_ref, right_ref, top_ref, bottom_ref, measured_ref,
    grad_tile, grad_left, grad_right, grad_top, grad_bottom, probe_out,
    obj, grad, held, in_sems, held_sems,
):
    rows = tile_ref.shape[1]
    cols = tile_ref.shape[2]
    tiles = cols // WIN
    count = count_ref[0, 0]
    lane = lax.broadcasted_iota(jnp.int32, (WIN, WIN), 1)

    def fetch(slot):
        return pltpu.make_async_copy(
            measured_ref.at[slot], held.at[lax.rem(slot, AHEAD)], held_sems.at[lax.rem(slot, AHEAD)]
        )

    for ahead in range(AHEAD):
        @pl.when(ahead < count)
        def _(ahead=ahead):
            fetch(jnp.int32(ahead)).start()

    loads = []
    for q in range(tiles):
        span = pl.ds(q * WIN, WIN)
        loads.append((tile_ref.at[:, :, span], obj.at[:, q + 1, pl.ds(RIM, rows), :]))
        loads.append((top_ref.at[:, :, span], obj.at[:, q + 1, pl.ds(0, RIM), :]))
        loads.append((bottom_ref.at[:, :, span], obj.at[:, q + 1, pl.ds(RIM + rows, RIM), :]))
    loads.append((left_ref, obj.at[:, 0]))
    loads.append((right_ref, obj.at[:, tiles + 1]))
    loads = [pltpu.make_async_copy(a, b, in_sems.at[i]) for i, (a, b) in enumerate(loads)]
    for copy in loads:
        copy.start()
    grad[...] = jnp.zeros_like(grad)
    probe_out[...] = jnp.zeros_like(probe_out)
    for copy in loads:
        copy.wait()

    @pl.loop(0, count)
    def _(slot):
        row = place_ref[slot, 0]
        col = place_ref[slot, 1]
        q = col // WIN
        shift = lax.rem(col, WIN)
        here = pl.ds(row, WIN)
        keep = lane < WIN - shift
        window = []
        for plane in range(2):
            first = pltpu.roll(obj[plane, q, here, :], WIN - shift, 1)
            second = pltpu.roll(obj[plane, q + 1, here, :], WIN - shift, 1)
            window.append(jnp.where(keep, first, second))
        fetch(slot).wait()
        measured = held[lax.rem(slot, AHEAD)]
        grad_re, grad_im, terms = slot_gradient(window[0], window[1], probe_ref, measured, 1.0, w_ref)

        @pl.when(slot + AHEAD < count)
        def _():
            fetch(slot + AHEAD).start()

        after = lane >= shift
        for plane, value in enumerate((grad_re, grad_im)):
            turned = pltpu.roll(value, shift, 1)
            grad[plane, q, here, :] += jnp.where(after, turned, 0.0)
            grad[plane, q + 1, here, :] += jnp.where(after, 0.0, turned)
        for i, term in enumerate(terms):
            probe_out[i // 2, i % 2] += term

    stores = []
    for q in range(tiles):
        span = pl.ds(q * WIN, WIN)
        stores.append((grad.at[:, q + 1, pl.ds(RIM, rows), :], grad_tile.at[:, :, span]))
        stores.append((grad.at[:, q + 1, pl.ds(0, RIM), :], grad_top.at[:, :, span]))
        stores.append((grad.at[:, q + 1, pl.ds(RIM + rows, RIM), :], grad_bottom.at[:, :, span]))
    stores.append((grad.at[:, 0], grad_left))
    stores.append((grad.at[:, tiles + 1], grad_right))
    stores = [pltpu.make_async_copy(a, b, in_sems.at[i]) for i, (a, b) in enumerate(stores)]
    for copy in stores:
        copy.start()
    for copy in stores:
        copy.wait()


def tile_gradient(count, places, probe, tile, left, right, top, bottom, measured):
    planes, rows, cols = tile.shape
    tiles = cols // WIN
    f32 = jnp.float32
    smem = pl.BlockSpec(memory_space=pltpu.SMEM)
    vmem = pl.BlockSpec(memory_space=pltpu.VMEM)
    hbm = pl.BlockSpec(memory_space=pl.ANY)
    extent = (planes, tiles + 2, rows + WIN, WIN)
    copies = 3 * tiles + 2
    return pl.pallas_call(
        body,
        out_shape=(
            jax.ShapeDtypeStruct(tile.shape, f32),
            jax.ShapeDtypeStruct(left.shape, f32),
            jax.ShapeDtypeStruct(right.shape, f32),
            jax.ShapeDtypeStruct(top.shape, f32),
            jax.ShapeDtypeStruct(bottom.shape, f32),
            jax.ShapeDtypeStruct(probe.shape, f32),
        ),
        in_specs=[smem, smem, vmem, vmem, hbm, hbm, hbm, hbm, hbm, hbm],
        out_specs=(hbm, hbm, hbm, hbm, hbm, vmem),
        scratch_shapes=[
            pltpu.VMEM(extent, f32),
            pltpu.VMEM(extent, f32),
            pltpu.VMEM((AHEAD, WIN, WIN), f32),
            pltpu.SemaphoreType.DMA((copies,)),
            pltpu.SemaphoreType.DMA((AHEAD,)),
        ],
        compiler_params=pltpu.CompilerParams(vmem_limit_bytes=48 * 1024 * 1024),
        name="tile_gradient",
    )(count, places, probe, jnp.asarray(matrices()), tile, left, right, top, bottom, measured)


def shifted(value, axis, by):
    devices = lax.axis_size(axis)
    pairs = [(i, i + by) for i in range(devices) if 0 <= i + by < devices]
    return lax.ppermute(value, axis, pairs)


def shards(object_planes, probe, positions, counts, amplitudes):
    planes, rows, cols = object_planes.shape
    top = shifted(object_planes[:, rows - RIM :], "ty", 1)
    bottom = shifted(object_planes[:, :RIM], "ty", -1)
    tall_last = jnp.concatenate(
        [top[:, :, cols - RIM :], object_planes[:, :, cols - RIM :], bottom[:, :, cols - RIM :]], axis=1
    )
    tall_first = jnp.concatenate([top[:, :, :RIM], object_planes[:, :, :RIM], bottom[:, :, :RIM]], axis=1)
    left = jnp.pad(shifted(tall_last, "tx", 1), ((0, 0), (0, 0), (RIM, 0)))
    right = jnp.pad(shifted(tall_first, "tx", -1), ((0, 0), (0, 0), (0, RIM)))
    base = jnp.stack([lax.axis_index("ty") * rows - RIM, lax.axis_index("tx") * cols - WIN]).astype(jnp.int32)
    places = positions[0, 0] - base
    g_tile, g_left, g_right, g_top, g_bottom, probe_part = tile_gradient(
        counts, places, probe, object_planes, left, right, top, bottom, amplitudes[0, 0]
    )
    from_right = shifted(g_left[:, :, RIM:], "tx", -1)
    from_left = shifted(g_right[:, :, :RIM], "tx", 1)
    g_top = g_top.at[:, :, cols - RIM :].add(from_right[:, :RIM]).at[:, :, :RIM].add(from_left[:, :RIM])
    g_bottom = g_bottom.at[:, :, cols - RIM :].add(from_right[:, RIM + rows :])
    g_bottom = g_bottom.at[:, :, :RIM].add(from_left[:, RIM + rows :])
    from_below = shifted(g_top, "ty", -1)
    from_above = shifted(g_bottom, "ty", 1)
    out = g_tile.at[:, :, cols - RIM :].add(from_right[:, RIM : RIM + rows])
    out = out.at[:, :, :RIM].add(from_left[:, RIM : RIM + rows])
    out = out.at[:, rows - RIM :].add(from_below).at[:, :RIM].add(from_above)
    total = lax.psum(probe_part, ("ty", "tx"))
    slots = lax.axis_size("ty") * lax.axis_size("tx") * positions.shape[2]
    return out, total / float(slots)


def solution(mesh):
    in_specs = (
        P(None, "ty", "tx"),
        P(),
        P("ty", "tx", None, None),
        P("ty", "tx"),
        P("ty", "tx", None, None, None),
    )
    out_specs = (P(None, "ty", "tx"), P())
    return jax.shard_map(shards, mesh=mesh, in_specs=in_specs, out_specs=out_specs, check_vma=False)
```

```python
import math

import jax
import jax.numpy as jnp
import numpy as np
from jax import lax
from jax.experimental import pallas as pl
from jax.experimental.pallas import tpu as pltpu
from jax.sharding import PartitionSpec as P

WIN = 128
RIM = WIN // 2
FLOOR = 0.25
AHEAD = 16
MESH = pl.DeviceIdType.MESH
SLOTS_ALL = 8 * 16 * 96
U = 8
SLOTS = 96


def matrices():
    index = np.arange(WIN)
    angle = 2.0 * math.pi / WIN * ((index[:, None] * index[None, :]) % WIN)
    cosine = np.cos(angle) / math.sqrt(WIN)
    sine = np.sin(angle) / math.sqrt(WIN)
    right = np.block([[cosine, -sine], [sine, cosine]])
    both = np.stack([right, right.T]).astype(np.float32)
    high = both.astype(jnp.bfloat16)
    low = (both - high.astype(np.float32)).astype(jnp.bfloat16)
    return np.stack([high, low], axis=1)


def split(value):
    high = value.astype(jnp.bfloat16)
    low = (value - high.astype(jnp.float32)).astype(jnp.bfloat16)
    return high, low


def dot(a, b):
    return lax.dot_general(a, b, (((1,), (0,)), ((), ())), preferred_element_type=jnp.float32)


def blocks(value):
    n = WIN
    return value[:n, :n], value[:n, n:], value[n:, :n], value[n:, n:]


def assemble(a, b, c, d):
    top = jnp.concatenate([a, b], axis=1)
    bottom = jnp.concatenate([c, d], axis=1)
    return jnp.concatenate([top, bottom], axis=0)


def right_product(value, w_ref, k):
    high, low = split(value)
    return dot(high, w_ref[k, 0]) + dot(low, w_ref[k, 0]) + dot(high, w_ref[k, 1])


def left_product(value, w_ref, k):
    high, low = split(value)
    return dot(w_ref[k, 0], high) + dot(w_ref[k, 0], low) + dot(w_ref[k, 1], high)


def forward(wins, probe_ref, measured, live, w_ref):
    p0r, p0i = probe_ref[0, 0], probe_ref[0, 1]
    p1r, p1i = probe_ref[1, 0], probe_ref[1, 1]
    waves = [assemble(
        p0r * a - p0i * b,
        p0r * b + p0i * a,
        p1r * a - p1i * b,
        p1r * b + p1i * a,
    ) for a, b in wins]
    xs = []
    for half in [right_product(v, w_ref, 0) for v in waves]:
        m0r, m0i, m1r, m1i = blocks(half)
        xs.append(assemble(m0r, m1r, m0i, m1i))
    out = []
    for k, far in enumerate([left_product(v, w_ref, 1) for v in xs]):
        f0r, f1r, f0i, f1i = blocks(far)
        intensity = f0r * f0r + f0i * f0i + (f1r * f1r + f1i * f1i)
        weight = live[k] - (live[k] * measured[k]) * lax.rsqrt(jnp.maximum(intensity, FLOOR))
        out.append(assemble(weight * f0r, weight * f1r, weight * f0i, weight * f1i))
    return out


def inverse(values, wins, probe_ref, w_ref):
    p0r, p0i = probe_ref[0, 0], probe_ref[0, 1]
    p1r, p1i = probe_ref[1, 0], probe_ref[1, 1]
    xs = []
    for half in [left_product(v, w_ref, 0) for v in values]:
        m0r, m1r, m0i, m1i = blocks(half)
        xs.append(assemble(m0r, m0i, m1r, m1i))
    out = []
    for (a, b), back in zip(wins, [right_product(v, w_ref, 1) for v in xs]):
        b0r, b0i, b1r, b1i = blocks(back)
        grad_re = p0r * b0r + p0i * b0i + (p1r * b1r + p1i * b1i)
        grad_im = p0r * b0i - p0i * b0r + (p1r * b1i - p1i * b1r)
        out.append((grad_re, grad_im, (a * b0r + b * b0i, a * b0i - b * b0r, a * b1r + b * b1i, a * b1i - b * b1r)))
    return out


def body(
    count_ref, place_ref, probe_ref, w_ref, tile_ref, left_ref, right_ref, top_ref, bottom_ref, corner_ref, measured_ref,
    grad_tile, grad_left, grad_right, grad_top, grad_bottom, grad_corner, probe_out,
    obj, grad, held, sides, in_sems, held_sems,
):
    rows = tile_ref.shape[1]
    cols = tile_ref.shape[2]
    tiles = cols // WIN
    count = count_ref[0, 0]
    lane = lax.broadcasted_iota(jnp.int32, (WIN, WIN), 1)

    def fetch(slot):
        return pltpu.make_async_copy(
            measured_ref.at[slot], held.at[lax.rem(slot, AHEAD)], held_sems.at[lax.rem(slot, AHEAD)]
        )

    for ahead in range(AHEAD):
        @pl.when(ahead < count)
        def _(ahead=ahead):
            fetch(jnp.int32(ahead)).start()

    last = tiles + 1
    low = RIM + rows
    middle = RIM + rows // 2
    loads = []
    for q in range(tiles):
        span = pl.ds(q * WIN, WIN)
        loads.append((tile_ref.at[:, :, span], obj.at[:, q + 1, pl.ds(RIM, rows), :]))
        loads.append((top_ref.at[:, :, span], obj.at[:, q + 1, pl.ds(0, RIM), :]))
        loads.append((bottom_ref.at[:, :, span], obj.at[:, q + 1, pl.ds(low, RIM), :]))
    for i, (q, start) in enumerate(((0, 0), (last, 0), (0, low), (last, low))):
        loads.append((corner_ref.at[i], obj.at[:, q, pl.ds(start, RIM), :]))
    loads.append((left_ref, sides.at[0]))
    loads.append((right_ref, sides.at[1]))
    loads = [pltpu.make_async_copy(a, b, in_sems.at[i]) for i, (a, b) in enumerate(loads)]
    for copy in loads:
        copy.start()
    grad[...] = jnp.zeros_like(grad)
    probe_out[...] = jnp.zeros_like(probe_out)
    for copy in loads:
        copy.wait()
    first_half = pl.ds(RIM, rows // 2)
    second_half = pl.ds(middle, rows // 2)
    for plane in range(2):
        obj[plane, 0, first_half, :] = pltpu.roll(sides[0, plane], RIM, 1)
        obj[plane, 0, second_half, :] = sides[0, plane]
        obj[plane, last, first_half, :] = sides[1, plane]
        obj[plane, last, second_half, :] = pltpu.roll(sides[1, plane], RIM, 1)
    ty, tx = lax.axis_index("ty"), lax.axis_index("tx")

    @pl.when(ty == 0)
    def _():
        obj[:, :, pl.ds(0, RIM), :] = jnp.zeros((2, tiles + 2, RIM, WIN), jnp.float32)

    @pl.when(ty == lax.axis_size("ty") - 1)
    def _():
        obj[:, :, pl.ds(low, RIM), :] = jnp.zeros((2, tiles + 2, RIM, WIN), jnp.float32)

    @pl.when(tx == 0)
    def _():
        obj[:, 0] = jnp.zeros((2, rows + WIN, WIN), jnp.float32)

    @pl.when(tx == lax.axis_size("tx") - 1)
    def _():
        obj[:, last] = jnp.zeros((2, rows + WIN, WIN), jnp.float32)


    def info_of(slot):
        safe = jnp.minimum(slot, SLOTS - 1)
        row = place_ref[safe, 0]
        col = place_ref[safe, 1]
        return row, col // WIN, lax.rem(col, WIN)

    def take(slot):
        row, q, shift = info_of(slot)
        here = pl.ds(row, WIN)
        keep = lane < WIN - shift
        window = []
        for plane in range(2):
            first = pltpu.roll(obj[plane, q, here, :], WIN - shift, 1)
            second = pltpu.roll(obj[plane, q + 1, here, :], WIN - shift, 1)
            window.append(jnp.where(keep, first, second))
        return window

    def put(slot, grad_re, grad_im):
        row, q, shift = info_of(slot)
        here = pl.ds(row, WIN)
        after = lane >= shift
        for plane, value in enumerate((grad_re, grad_im)):
            turned = pltpu.roll(value, shift, 1)
            grad[plane, q, here, :] += jnp.where(after, turned, 0.0)
            grad[plane, q + 1, here, :] += jnp.where(after, 0.0, turned)

    def run_forward(slots):
        wins = [take(s) for s in slots]
        for s in slots:
            @pl.when(s < count)
            def _():
                fetch(s).wait()
        return wins, forward(wins, probe_ref, [held[lax.rem(s, AHEAD)] for s in slots], [jnp.where(s < count, 1.0, 0.0) for s in slots], w_ref)

    def run_inverse(slots, wins, values):
        results = inverse(values, wins, probe_ref, w_ref)
        for s, (grad_re, grad_im, terms) in zip(slots, results):
            put(s, grad_re, grad_im)
        for i in range(4):
            probe_out[i // 2, i % 2] += sum(r[2][i] for r in results)

    def refill(slots):
        for s in slots:
            @pl.when(s + AHEAD < count)
            def _():
                fetch(s + AHEAD).start()

    groups = (count + U - 1) // U
    @pl.loop(0, groups)
    def _(group):
        slots = [group * U + u for u in range(U)]
        wins, values = run_forward(slots)
        run_inverse(slots, wins, values)
        refill(slots)

    stores = []
    for q in range(tiles):
        span = pl.ds(q * WIN, WIN)
        stores.append((grad.at[:, q + 1, pl.ds(RIM, rows), :], grad_tile.at[:, :, span]))
        stores.append((grad.at[:, q + 1, pl.ds(0, RIM), :], grad_top.at[:, :, span]))
        stores.append((grad.at[:, q + 1, pl.ds(low, RIM), :], grad_bottom.at[:, :, span]))
    for i, (q, start) in enumerate(((0, 0), (last, 0), (0, low), (last, low))):
        stores.append((grad.at[:, q, pl.ds(start, RIM), :], grad_corner.at[i]))
    stores.append((sides.at[0], grad_left))
    stores.append((sides.at[1], grad_right))
    stores = [pltpu.make_async_copy(a, b, in_sems.at[i]) for i, (a, b) in enumerate(stores)]
    for copy in stores[:-2]:
        copy.start()
    near = lax.broadcasted_iota(jnp.int32, (rows // 2, WIN), 1) < RIM
    for plane in range(2):
        sides[0, plane] = jnp.where(near, pltpu.roll(grad[plane, 0, first_half, :], RIM, 1), grad[plane, 0, second_half, :])
        sides[1, plane] = jnp.where(
            near, grad[plane, last, first_half, :], pltpu.roll(grad[plane, last, second_half, :], RIM, 1)
        )
    for copy in stores[-2:]:
        copy.start()
    for copy in stores:
        copy.wait()


def tile_gradient(count, places, probe, tile, halo, measured):
    planes, rows, cols = tile.shape
    tiles = cols // WIN
    f32 = jnp.float32
    smem = pl.BlockSpec(memory_space=pltpu.SMEM)
    vmem = pl.BlockSpec(memory_space=pltpu.VMEM)
    hbm = pl.BlockSpec(memory_space=pl.ANY)
    extent = (planes, tiles + 2, rows + WIN, WIN)
    copies = 3 * tiles + 6
    return pl.pallas_call(
        body,
        out_shape=(
            jax.ShapeDtypeStruct(tile.shape, f32),
            *(jax.ShapeDtypeStruct(h.shape, f32) for h in halo),
            jax.ShapeDtypeStruct(probe.shape, f32),
        ),
        in_specs=[smem, smem, vmem, vmem] + [hbm] * 7,
        out_specs=(*[hbm] * 6, vmem),
        scratch_shapes=[
            pltpu.VMEM(extent, f32),
            pltpu.VMEM(extent, f32),
            pltpu.VMEM((AHEAD, WIN, WIN), f32),
            pltpu.VMEM((2, planes, rows // 2, WIN), f32),
            pltpu.SemaphoreType.DMA((copies,)),
            pltpu.SemaphoreType.DMA((AHEAD,)),
        ],
        compiler_params=pltpu.CompilerParams(vmem_limit_bytes=48 * 1024 * 1024),
        name="tile_gradient",
    )(count, places, probe, jnp.asarray(matrices()), tile, *halo, measured)


AROUND = ((-1, 0), (1, 0), (0, -1), (0, 1), (-1, -1), (-1, 1), (1, -1), (1, 1))


def ring(axis, by):
    size = lax.axis_size(axis)
    return lax.rem(lax.axis_index(axis) + (by + size), size)


def around(dy, dx):
    return {"ty": ring("ty", dy), "tx": ring("tx", dx)}


def greet(partners):
    barrier = pltpu.get_barrier_semaphore()
    for partner in partners:
        pl.semaphore_signal(barrier, inc=1, device_id=partner, device_id_type=MESH)


def halo_body(
    tile_ref, left_out, right_out, top_out, bottom_out, corner_out, edge, packed, in_sems, send_sems, recv_sems
):
    rows, cols = tile_ref.shape[1:]
    greet([around(*step) for step in AROUND])
    firsts = pltpu.make_async_copy(tile_ref.at[:, :, pl.ds(0, WIN)], edge.at[0], in_sems.at[0])
    lasts = pltpu.make_async_copy(tile_ref.at[:, :, pl.ds(cols - WIN, WIN)], edge.at[1], in_sems.at[1])
    firsts.start()
    lasts.start()
    half = rows // 2
    near = lax.broadcasted_iota(jnp.int32, (half, WIN), 1) < RIM
    firsts.wait()
    for plane in range(2):
        packed[0, plane] = jnp.where(
            near, edge[0, plane, pl.ds(0, half), :], pltpu.roll(edge[0, plane, pl.ds(half, half), :], RIM, 1)
        )
    lasts.wait()
    for plane in range(2):
        packed[1, plane] = jnp.where(
            near, pltpu.roll(edge[1, plane, pl.ds(0, half), :], RIM, 1), edge[1, plane, pl.ds(half, half), :]
        )
    pl.semaphore_wait(pltpu.get_barrier_semaphore(), len(AROUND))
    above, below = pl.ds(0, RIM), pl.ds(rows - RIM, RIM)
    start, stop = pl.ds(0, WIN), pl.ds(cols - WIN, WIN)
    moves = (
        (packed.at[0], right_out, (0, -1)),
        (packed.at[1], left_out, (0, 1)),
        (tile_ref.at[:, above, :], bottom_out, (-1, 0)),
        (tile_ref.at[:, below, :], top_out, (1, 0)),
        (tile_ref.at[:, below, stop], corner_out.at[0], (1, 1)),
        (tile_ref.at[:, below, start], corner_out.at[1], (1, -1)),
        (tile_ref.at[:, above, stop], corner_out.at[2], (-1, 1)),
        (tile_ref.at[:, above, start], corner_out.at[3], (-1, -1)),
    )
    send(moves, send_sems, recv_sems)


def send(moves, send_sems, recv_sems, wait=True):
    copies = [
        pltpu.make_async_remote_copy(
            src_ref=source,
            dst_ref=target,
            send_sem=send_sems.at[i],
            recv_sem=recv_sems.at[i],
            device_id=around(*step),
            device_id_type=MESH,
        )
        for i, (source, target, step) in enumerate(moves)
    ]
    for copy in copies:
        copy.start()
    if wait:
        for copy in copies:
            copy.wait()
    return copies


def halo_shapes(tile):
    planes, rows, cols = tile.shape
    shapes = [(planes, rows // 2, WIN)] * 2 + [(planes, RIM, cols)] * 2 + [(4, planes, RIM, WIN)]
    return tuple(jax.ShapeDtypeStruct(s, jnp.float32) for s in shapes)


def gather_halo(tile):
    planes, rows, cols = tile.shape
    hbm = pl.BlockSpec(memory_space=pl.ANY)
    return pl.pallas_call(
        halo_body,
        out_shape=halo_shapes(tile),
        in_specs=[hbm],
        out_specs=(hbm,) * 5,
        scratch_shapes=[
            pltpu.VMEM((2, planes, rows, WIN), jnp.float32),
            pltpu.VMEM((2, planes, rows // 2, WIN), jnp.float32),
            pltpu.SemaphoreType.DMA((2,)),
            pltpu.SemaphoreType.DMA((8,)),
            pltpu.SemaphoreType.DMA((8,)),
        ],
        compiler_params=pltpu.CompilerParams(
            collective_id=0, has_side_effects=True, vmem_limit_bytes=16 * 1024 * 1024
        ),
        name="gather_halo",
    )(tile)


def tail_body(
    left_ref, right_ref, top_ref, bottom_ref, corner_ref, part_ref,
    left_out, right_out, top_out, bottom_out, corner_out, total_out,
    gathered, stage, send_sems, recv_sems, tx_send, tx_recv, ty_send, ty_recv, out_send, out_recv,
):
    ty, tx = lax.axis_index("ty"), lax.axis_index("tx")
    ny, nx = lax.axis_size("ty"), lax.axis_size("tx")
    diagonal = [around(*step) for step in AROUND if 0 not in step]
    greet(diagonal)
    barrier = pltpu.get_barrier_semaphore()

    @pl.loop(1, nx)
    def _(k):
        pl.semaphore_signal(barrier, inc=1, device_id={"tx": lax.rem(tx + k, nx)}, device_id_type=MESH)

    @pl.loop(1, ny)
    def _(k):
        pl.semaphore_signal(barrier, inc=1, device_id={"ty": lax.rem(ty + k, ny)}, device_id_type=MESH)

    pl.semaphore_wait(barrier, len(diagonal) + nx - 1 + ny - 1)

    def to_column(k, source, target, sends, receives):
        return pltpu.make_async_remote_copy(
            src_ref=source,
            dst_ref=target,
            send_sem=sends.at[k],
            recv_sem=receives.at[tx],
            device_id={"tx": lax.rem(tx + k, nx)},
            device_id_type=MESH,
        )

    def to_row(k):
        return pltpu.make_async_remote_copy(
            src_ref=stage.at[ty],
            dst_ref=stage.at[ty],
            send_sem=ty_send.at[k],
            recv_sem=ty_recv.at[ty],
            device_id={"ty": lax.rem(ty + k, ny)},
            device_id_type=MESH,
        )

    def arrived(target, semaphore):
        pltpu.make_async_copy(target, target, semaphore).wait()

    def spread(k):
        return to_column(k, part_ref.at[lax.rem(tx + k, nx)], gathered.at[tx], tx_send, tx_recv)

    def share(k):
        return to_column(k, total_out.at[tx], total_out.at[tx], out_send, out_recv)

    @pl.loop(1, nx)
    def _(k):
        spread(k).start()

    moves = (
        (left_ref, right_out, (0, -1)),
        (right_ref, left_out, (0, 1)),
        (top_ref, bottom_out, (-1, 0)),
        (bottom_ref, top_out, (1, 0)),
        (corner_ref.at[0], corner_out.at[3], (-1, -1)),
        (corner_ref.at[1], corner_out.at[2], (-1, 1)),
        (corner_ref.at[2], corner_out.at[1], (1, -1)),
        (corner_ref.at[3], corner_out.at[0], (1, 1)),
    )
    halo = send(moves, send_sems, recv_sems, wait=False)

    stage[ty] = part_ref[tx]

    @pl.loop(1, nx)
    def _(k):
        source = lax.rem(tx + k, nx)
        arrived(gathered.at[source], tx_recv.at[source])
        stage[ty] += gathered[source]

    @pl.loop(1, ny)
    def _(k):
        to_row(k).start()

    @pl.loop(1, ny)
    def _(k):
        source = lax.rem(ty + k, ny)
        arrived(stage.at[source], ty_recv.at[source])

    total = stage[0]
    for i in range(1, stage.shape[0]):
        total += stage[i]
    total_out[tx] = total * (1.0 / SLOTS_ALL)

    @pl.loop(1, nx)
    def _(k):
        share(k).start()

    @pl.loop(1, nx)
    def _(k):
        source = lax.rem(tx + k, nx)
        arrived(total_out.at[source], out_recv.at[source])

    for copy in halo:
        copy.wait()

    @pl.loop(1, nx)
    def _(k):
        spread(k).wait_send()
        share(k).wait_send()

    @pl.loop(1, ny)
    def _(k):
        to_row(k).wait_send()


def exchange(halo, part):
    hbm = pl.BlockSpec(memory_space=pl.ANY)
    vmem = pl.BlockSpec(memory_space=pltpu.VMEM)
    ny, nx = lax.axis_size("ty"), lax.axis_size("tx")
    chunk = (part.size // (nx * WIN), WIN)
    return pl.pallas_call(
        tail_body,
        out_shape=(
            *(jax.ShapeDtypeStruct(h.shape, jnp.float32) for h in halo),
            jax.ShapeDtypeStruct((nx, *chunk), jnp.float32),
        ),
        in_specs=[hbm] * 5 + [vmem],
        out_specs=(*[hbm] * 5, vmem),
        scratch_shapes=[
            pltpu.VMEM((nx, *chunk), jnp.float32),
            pltpu.VMEM((ny, *chunk), jnp.float32),
            pltpu.SemaphoreType.DMA((8,)),
            pltpu.SemaphoreType.DMA((8,)),
            pltpu.SemaphoreType.DMA((nx,)),
            pltpu.SemaphoreType.DMA((nx,)),
            pltpu.SemaphoreType.DMA((ny,)),
            pltpu.SemaphoreType.DMA((ny,)),
            pltpu.SemaphoreType.DMA((nx,)),
            pltpu.SemaphoreType.DMA((nx,)),
        ],
        compiler_params=pltpu.CompilerParams(
            collective_id=1, has_side_effects=True, vmem_limit_bytes=16 * 1024 * 1024
        ),
        name="exchange",
    )(*halo, part.reshape(nx, *chunk))


def finish_body(
    tile_ref, left_ref, right_ref, top_ref, bottom_ref, corner_ref, total_ref, out_ref, total_out, edge, strip, in_sems
):
    planes, rows, cols = tile_ref.shape
    ty, tx = lax.axis_index("ty"), lax.axis_index("tx")
    ny, nx = lax.axis_size("ty"), lax.axis_size("tx")
    half = rows // 2
    ends = (pl.ds(0, RIM), pl.ds(rows - RIM, RIM))
    sides = (pl.ds(0, WIN), pl.ds(cols - WIN, WIN))
    inner = pl.ds(WIN, cols - 2 * WIN)
    parts = [(out_ref.at[:, :, span], edge.at[i]) for i, span in enumerate(sides)]
    parts += [(out_ref.at[:, span, inner], strip.at[i]) for i, span in enumerate(ends)]
    reads = [pltpu.make_async_copy(a, b, in_sems.at[i]) for i, (a, b) in enumerate(parts)]
    for copy in reads:
        copy.start()
    total_out[...] = total_ref[...]
    lane = lax.broadcasted_iota(jnp.int32, (half, WIN), 1)
    near = lane < RIM
    lane = lane[:RIM]
    no_side = (tx == 0, tx == nx - 1)
    no_end = (ty == 0, ty == ny - 1)
    for copy in reads:
        copy.wait()
    for plane in range(2):
        for i, packed in enumerate((left_ref, right_ref)):
            value = jnp.where(no_side[i], 0.0, packed[plane])
            turned = pltpu.roll(value, RIM, 1)
            mine = near if i == 0 else jnp.logical_not(near)
            first, second = (value, turned) if i == 0 else (turned, value)
            edge[i, plane, pl.ds(0, half), :] += jnp.where(mine, first, 0.0)
            edge[i, plane, pl.ds(half, half), :] += jnp.where(mine, second, 0.0)
        for j, rim in enumerate((top_ref, bottom_ref)):
            for i in range(2):
                value = jnp.where(no_end[j], 0.0, rim[plane, :, sides[i]])
                gone = jnp.logical_or(no_side[i], no_end[j])
                value += jnp.where(gone, 0.0, corner_ref[2 * j + i, plane])
                edge[i, plane, ends[j], :] += value
            strip[j, plane] += jnp.where(no_end[j], 0.0, rim[plane, :, inner])
    writes = [pltpu.make_async_copy(b, a, in_sems.at[i]) for i, (a, b) in enumerate(parts)]
    for copy in writes:
        copy.start()
    for copy in writes:
        copy.wait()


def finish(tile, halo, total):
    planes, rows, cols = tile.shape
    hbm = pl.BlockSpec(memory_space=pl.ANY)
    vmem = pl.BlockSpec(memory_space=pltpu.VMEM)
    return pl.pallas_call(
        finish_body,
        out_shape=(jax.ShapeDtypeStruct(tile.shape, jnp.float32), jax.ShapeDtypeStruct(total.shape, jnp.float32)),
        in_specs=[hbm] + [vmem] * 6,
        out_specs=(hbm, vmem),
        scratch_shapes=[
            pltpu.VMEM((2, planes, rows, WIN), jnp.float32),
            pltpu.VMEM((2, planes, RIM, cols - 2 * WIN), jnp.float32),
            pltpu.SemaphoreType.DMA((4,)),
        ],
        input_output_aliases={0: 0},
        compiler_params=pltpu.CompilerParams(vmem_limit_bytes=16 * 1024 * 1024),
        name="finish",
    )(tile, *halo, total)


def shards(object_planes, probe, positions, counts, amplitudes):
    planes, rows, cols = object_planes.shape
    halo = gather_halo(object_planes)
    base = jnp.stack([lax.axis_index("ty") * rows - RIM, lax.axis_index("tx") * cols - WIN]).astype(jnp.int32)
    places = positions[0, 0] - base
    tile, *outer, part = tile_gradient(counts, places, probe, object_planes, halo, amplitudes[0, 0])
    *outer, total = exchange(outer, part)
    tile, total = finish(tile, outer, total)
    return tile, total.reshape(probe.shape)


def solution(mesh):
    in_specs = (
        P(None, "ty", "tx"),
        P(),
        P("ty", "tx", None, None),
        P("ty", "tx"),
        P("ty", "tx", None, None, None),
    )
    out_specs = (P(None, "ty", "tx"), P())
    return jax.shard_map(shards, mesh=mesh, in_specs=in_specs, out_specs=out_specs, check_vma=False)
```

```python
import math

import jax
import jax.numpy as jnp
import numpy as np
from jax import lax
from jax.experimental import pallas as pl
from jax.experimental.pallas import tpu as pltpu
from jax.sharding import PartitionSpec as P

WIN = 128
RIM = WIN // 2
FLOOR = 0.25
AHEAD = 16
MESH = pl.DeviceIdType.MESH
SLOTS_ALL = 8 * 16 * 96
U = 8
EARLY = 48


def matrices():
    index = np.arange(WIN)
    angle = 2.0 * math.pi / WIN * ((index[:, None] * index[None, :]) % WIN)
    cosine = np.cos(angle) / math.sqrt(WIN)
    sine = np.sin(angle) / math.sqrt(WIN)
    right = np.block([[cosine, -sine], [sine, cosine]])
    both = np.stack([right, right.T]).astype(np.float32)
    high = both.astype(jnp.bfloat16)
    low = (both - high.astype(np.float32)).astype(jnp.bfloat16)
    return np.stack([high, low], axis=1)


def split(value):
    high = value.astype(jnp.bfloat16)
    low = (value - high.astype(jnp.float32)).astype(jnp.bfloat16)
    return high, low


def dot(a, b):
    return lax.dot_general(a, b, (((1,), (0,)), ((), ())), preferred_element_type=jnp.float32)


def blocks(value):
    n = WIN
    return value[:n, :n], value[:n, n:], value[n:, :n], value[n:, n:]


def assemble(a, b, c, d):
    top = jnp.concatenate([a, b], axis=1)
    bottom = jnp.concatenate([c, d], axis=1)
    return jnp.concatenate([top, bottom], axis=0)


def right_product(value, w_ref, k):
    high, low = split(value)
    return dot(high, w_ref[k, 0]) + dot(low, w_ref[k, 0]) + dot(high, w_ref[k, 1])


def left_product(value, w_ref, k):
    high, low = split(value)
    return dot(w_ref[k, 0], high) + dot(w_ref[k, 0], low) + dot(w_ref[k, 1], high)


def forward(wins, probe_ref, measured, live, w_ref):
    p0r, p0i = probe_ref[0, 0], probe_ref[0, 1]
    p1r, p1i = probe_ref[1, 0], probe_ref[1, 1]
    waves = [assemble(
        p0r * a - p0i * b,
        p0r * b + p0i * a,
        p1r * a - p1i * b,
        p1r * b + p1i * a,
    ) for a, b in wins]
    xs = []
    for half in [right_product(v, w_ref, 0) for v in waves]:
        m0r, m0i, m1r, m1i = blocks(half)
        xs.append(assemble(m0r, m1r, m0i, m1i))
    out = []
    for k, far in enumerate([left_product(v, w_ref, 1) for v in xs]):
        f0r, f1r, f0i, f1i = blocks(far)
        intensity = f0r * f0r + f0i * f0i + (f1r * f1r + f1i * f1i)
        weight = live[k] - (live[k] * measured[k]) * lax.rsqrt(jnp.maximum(intensity, FLOOR))
        out.append(assemble(weight * f0r, weight * f1r, weight * f0i, weight * f1i))
    return out


def inverse(values, wins, probe_ref, w_ref):
    p0r, p0i = probe_ref[0, 0], probe_ref[0, 1]
    p1r, p1i = probe_ref[1, 0], probe_ref[1, 1]
    xs = []
    for half in [left_product(v, w_ref, 0) for v in values]:
        m0r, m1r, m0i, m1i = blocks(half)
        xs.append(assemble(m0r, m0i, m1r, m1i))
    out = []
    for (a, b), back in zip(wins, [right_product(v, w_ref, 1) for v in xs]):
        b0r, b0i, b1r, b1i = blocks(back)
        grad_re = p0r * b0r + p0i * b0i + (p1r * b1r + p1i * b1i)
        grad_im = p0r * b0i - p0i * b0r + (p1r * b1i - p1i * b1r)
        out.append((grad_re, grad_im, (a * b0r + b * b0i, a * b0i - b * b0r, a * b1r + b * b1i, a * b1i - b * b1r)))
    return out


def take(obj, row, q, q_next, shift):
    here = pl.ds(row, WIN)
    keep = lax.broadcasted_iota(jnp.int32, (WIN, WIN), 1) < WIN - shift
    window = []
    for plane in range(2):
        first = pltpu.roll(obj[plane, q, here, :], WIN - shift, 1)
        second = pltpu.roll(obj[plane, q_next, here, :], WIN - shift, 1)
        window.append(jnp.where(keep, first, second))
    return window


def put(grad, row, q, shift, values):
    here = pl.ds(row, WIN)
    after = lax.broadcasted_iota(jnp.int32, (WIN, WIN), 1) >= shift
    for plane, value in enumerate(values):
        turned = pltpu.roll(value, shift, 1)
        grad[plane, q, here, :] += jnp.where(after, turned, 0.0)
        grad[plane, q + 1, here, :] += jnp.where(after, 0.0, turned)


def body(
    place_ref, number_ref, probe_ref, w_ref, tile_ref, left_ref, right_ref, top_ref, bottom_ref, corner_ref,
    measured_ref, patch_ref, part_ref,
    grad_tile, grad_left, grad_right, grad_top, grad_bottom, grad_corner, probe_out,
    obj, grad, held, sides, patches, in_sems, held_sems, patch_sem,
):
    rows = tile_ref.shape[1]
    cols = tile_ref.shape[2]
    tiles = cols // WIN
    begin, count = number_ref[0], number_ref[1]
    slots_max = place_ref.shape[1]

    def fetch(place):
        turn = lax.rem(place - begin, AHEAD)
        return pltpu.make_async_copy(measured_ref.at[place_ref[0, place]], held.at[turn], held_sems.at[turn])

    for ahead in range(AHEAD):
        @pl.when(begin + ahead < count)
        def _(ahead=ahead):
            fetch(begin + ahead).start()

    last = tiles + 1
    low = RIM + rows
    middle = RIM + rows // 2
    loads = []
    for q in range(tiles):
        span = pl.ds(q * WIN, WIN)
        loads.append((tile_ref.at[:, :, span], obj.at[:, q + 1, pl.ds(RIM, rows), :]))
        loads.append((top_ref.at[:, :, span], obj.at[:, q + 1, pl.ds(0, RIM), :]))
        loads.append((bottom_ref.at[:, :, span], obj.at[:, q + 1, pl.ds(low, RIM), :]))
    for i, (q, start) in enumerate(((0, 0), (last, 0), (0, low), (last, low))):
        loads.append((corner_ref.at[i], obj.at[:, q, pl.ds(start, RIM), :]))
    loads.append((left_ref, sides.at[0]))
    loads.append((right_ref, sides.at[1]))
    loads = [pltpu.make_async_copy(a, b, in_sems.at[i]) for i, (a, b) in enumerate(loads)]
    early = pltpu.make_async_copy(patch_ref, patches, patch_sem)
    early.start()
    for copy in loads:
        copy.start()
    grad[...] = jnp.zeros_like(grad)
    probe_out[...] = part_ref[...]
    for copy in loads:
        copy.wait()
    first_half = pl.ds(RIM, rows // 2)
    second_half = pl.ds(middle, rows // 2)
    for plane in range(2):
        obj[plane, 0, first_half, :] = pltpu.roll(sides[0, plane], RIM, 1)
        obj[plane, 0, second_half, :] = sides[0, plane]
        obj[plane, last, first_half, :] = sides[1, plane]
        obj[plane, last, second_half, :] = pltpu.roll(sides[1, plane], RIM, 1)
    ty, tx = lax.axis_index("ty"), lax.axis_index("tx")

    @pl.when(ty == 0)
    def _():
        obj[:, :, pl.ds(0, RIM), :] = jnp.zeros((2, tiles + 2, RIM, WIN), jnp.float32)

    @pl.when(ty == lax.axis_size("ty") - 1)
    def _():
        obj[:, :, pl.ds(low, RIM), :] = jnp.zeros((2, tiles + 2, RIM, WIN), jnp.float32)

    @pl.when(tx == 0)
    def _():
        obj[:, 0] = jnp.zeros((2, rows + WIN, WIN), jnp.float32)

    @pl.when(tx == lax.axis_size("tx") - 1)
    def _():
        obj[:, last] = jnp.zeros((2, rows + WIN, WIN), jnp.float32)


    def info_of(place):
        safe = jnp.minimum(place, slots_max - 1)
        row, col = place_ref[1, safe], place_ref[2, safe]
        return row, col // WIN, lax.rem(col, WIN)

    early.wait()

    @pl.loop(0, begin)
    def _(place):
        put(grad, *info_of(place), (patches[place, 0], patches[place, 1]))

    @pl.loop(0, (count - begin + U - 1) // U)
    def _(group):
        places = [begin + group * U + u for u in range(U)]
        wins = []
        for place in places:
            row, q, shift = info_of(place)
            wins.append(take(obj, row, q, q + 1, shift))
        for place in places:
            @pl.when(place < count)
            def _():
                fetch(place).wait()
        held_now = [held[lax.rem(place - begin, AHEAD)] for place in places]
        live = [jnp.where(place < count, 1.0, 0.0) for place in places]
        results = inverse(forward(wins, probe_ref, held_now, live, w_ref), wins, probe_ref, w_ref)
        for place, (grad_re, grad_im, terms) in zip(places, results):
            put(grad, *info_of(place), (grad_re, grad_im))
        for i in range(4):
            probe_out[i // 2, i % 2] += sum(r[2][i] for r in results)
        for place in places:
            @pl.when(place + AHEAD < count)
            def _():
                fetch(place + AHEAD).start()

    stores = []
    for q in range(tiles):
        span = pl.ds(q * WIN, WIN)
        stores.append((grad.at[:, q + 1, pl.ds(RIM, rows), :], grad_tile.at[:, :, span]))
        stores.append((grad.at[:, q + 1, pl.ds(0, RIM), :], grad_top.at[:, :, span]))
        stores.append((grad.at[:, q + 1, pl.ds(low, RIM), :], grad_bottom.at[:, :, span]))
    for i, (q, start) in enumerate(((0, 0), (last, 0), (0, low), (last, low))):
        stores.append((grad.at[:, q, pl.ds(start, RIM), :], grad_corner.at[i]))
    stores.append((sides.at[0], grad_left))
    stores.append((sides.at[1], grad_right))
    stores = [pltpu.make_async_copy(a, b, in_sems.at[i]) for i, (a, b) in enumerate(stores)]
    for copy in stores[:-2]:
        copy.start()
    near = lax.broadcasted_iota(jnp.int32, (rows // 2, WIN), 1) < RIM
    for plane in range(2):
        sides[0, plane] = jnp.where(near, pltpu.roll(grad[plane, 0, first_half, :], RIM, 1), grad[plane, 0, second_half, :])
        sides[1, plane] = jnp.where(
            near, grad[plane, last, first_half, :], pltpu.roll(grad[plane, last, second_half, :], RIM, 1)
        )
    for copy in stores[-2:]:
        copy.start()
    for copy in stores:
        copy.wait()


def tile_gradient(places, numbers, probe, tile, halo, measured, patches, part):
    planes, rows, cols = tile.shape
    tiles = cols // WIN
    f32 = jnp.float32
    smem = pl.BlockSpec(memory_space=pltpu.SMEM)
    vmem = pl.BlockSpec(memory_space=pltpu.VMEM)
    hbm = pl.BlockSpec(memory_space=pl.ANY)
    extent = (planes, tiles + 2, rows + WIN, WIN)
    copies = 3 * tiles + 6
    return pl.pallas_call(
        body,
        out_shape=(
            jax.ShapeDtypeStruct(tile.shape, f32),
            *(jax.ShapeDtypeStruct(h.shape, f32) for h in halo),
            jax.ShapeDtypeStruct(probe.shape, f32),
        ),
        in_specs=[smem, smem, vmem, vmem] + [hbm] * 8 + [vmem],
        out_specs=(*[hbm] * 6, vmem),
        scratch_shapes=[
            pltpu.VMEM(extent, f32),
            pltpu.VMEM(extent, f32),
            pltpu.VMEM((AHEAD, WIN, WIN), f32),
            pltpu.VMEM((2, planes, rows // 2, WIN), f32),
            pltpu.VMEM(patches.shape, f32),
            pltpu.SemaphoreType.DMA((copies,)),
            pltpu.SemaphoreType.DMA((AHEAD,)),
            pltpu.SemaphoreType.DMA,
        ],
        compiler_params=pltpu.CompilerParams(vmem_limit_bytes=56 * 1024 * 1024),
        name="tile_gradient",
    )(places, numbers, probe, jnp.asarray(matrices()), tile, *halo, measured, patches, part)


AROUND = ((-1, 0), (1, 0), (0, -1), (0, 1), (-1, -1), (-1, 1), (1, -1), (1, 1))


def ring(axis, by):
    size = lax.axis_size(axis)
    return lax.rem(lax.axis_index(axis) + (by + size), size)


def around(dy, dx):
    return {"ty": ring("ty", dy), "tx": ring("tx", dx)}


def greet(partners):
    barrier = pltpu.get_barrier_semaphore()
    for partner in partners:
        pl.semaphore_signal(barrier, inc=1, device_id=partner, device_id_type=MESH)


def halo_body(
    place_ref, live_ref, probe_ref, w_ref, tile_ref, measured_ref,
    left_out, right_out, top_out, bottom_out, corner_out, patch_out, part_out,
    obj, held, packed, patches, in_sems, held_sem, send_sems, recv_sems, patch_sems,
):
    rows, cols = tile_ref.shape[1:]
    tiles = cols // WIN
    greet([around(*step) for step in AROUND])
    loads = [
        pltpu.make_async_copy(tile_ref.at[:, :, pl.ds(q * WIN, WIN)], obj.at[:, q], in_sems.at[q])
        for q in range(tiles)
    ]
    for q in (0, tiles - 1, *range(1, tiles - 1)):
        loads[q].start()
    measures = pltpu.make_async_copy(measured_ref, held, held_sem)
    measures.start()
    part_out[...] = jnp.zeros_like(part_out)
    half = rows // 2
    first, second = pl.ds(0, half), pl.ds(half, half)
    near = lax.broadcasted_iota(jnp.int32, (half, WIN), 1) < RIM
    loads[0].wait()
    for plane in range(2):
        packed[0, plane] = jnp.where(near, obj[plane, 0, first, :], pltpu.roll(obj[plane, 0, second, :], RIM, 1))
    loads[tiles - 1].wait()
    for plane in range(2):
        packed[1, plane] = jnp.where(
            near, pltpu.roll(obj[plane, tiles - 1, first, :], RIM, 1), obj[plane, tiles - 1, second, :]
        )
    pl.semaphore_wait(pltpu.get_barrier_semaphore(), len(AROUND))
    above, below = pl.ds(0, RIM), pl.ds(rows - RIM, RIM)
    start, stop = pl.ds(0, WIN), pl.ds(cols - WIN, WIN)
    moves = (
        (packed.at[0], right_out, (0, -1)),
        (packed.at[1], left_out, (0, 1)),
        (tile_ref.at[:, above, :], bottom_out, (-1, 0)),
        (tile_ref.at[:, below, :], top_out, (1, 0)),
        (tile_ref.at[:, below, stop], corner_out.at[0], (1, 1)),
        (tile_ref.at[:, below, start], corner_out.at[1], (1, -1)),
        (tile_ref.at[:, above, stop], corner_out.at[2], (-1, 1)),
        (tile_ref.at[:, above, start], corner_out.at[3], (-1, -1)),
    )
    halo = send(moves, send_sems, recv_sems, wait=False)
    for q in range(1, tiles - 1):
        loads[q].wait()
    measures.wait()

    def store(group):
        turn = lax.rem(group, 2)
        return pltpu.make_async_copy(patches.at[turn], patch_out.at[pl.ds(group * U, U)], patch_sems.at[turn])

    groups = patch_out.shape[0] // U

    @pl.loop(0, groups)
    def _(group):
        turn = lax.rem(group, 2)

        @pl.when(group >= 2)
        def _():
            store(group - 2).wait()

        places = [group * U + u for u in range(U)]
        wins = [
            take(obj, place_ref[3, p], place_ref[4, p], place_ref[5, p], place_ref[6, p]) for p in places
        ]
        held_now = [held[place_ref[0, p]] for p in places]
        live = [live_ref[p] for p in places]
        results = inverse(forward(wins, probe_ref, held_now, live, w_ref), wins, probe_ref, w_ref)
        for u, (grad_re, grad_im, terms) in enumerate(results):
            patches[turn, u, 0] = grad_re
            patches[turn, u, 1] = grad_im
        for i in range(4):
            part_out[i // 2, i % 2] += sum(r[2][i] for r in results)
        store(group).start()

    for group in range(max(groups - 2, 0), groups):
        store(group).wait()
    for copy in halo:
        copy.wait()


def send(moves, send_sems, recv_sems, wait=True):
    copies = [
        pltpu.make_async_remote_copy(
            src_ref=source,
            dst_ref=target,
            send_sem=send_sems.at[i],
            recv_sem=recv_sems.at[i],
            device_id=around(*step),
            device_id_type=MESH,
        )
        for i, (source, target, step) in enumerate(moves)
    ]
    for copy in copies:
        copy.start()
    if wait:
        for copy in copies:
            copy.wait()
    return copies


def halo_shapes(tile):
    planes, rows, cols = tile.shape
    shapes = [(planes, rows // 2, WIN)] * 2 + [(planes, RIM, cols)] * 2 + [(4, planes, RIM, WIN)]
    return tuple(jax.ShapeDtypeStruct(s, jnp.float32) for s in shapes)


def gather_halo(places, live, probe, tile, measured):
    planes, rows, cols = tile.shape
    hbm = pl.BlockSpec(memory_space=pl.ANY)
    smem = pl.BlockSpec(memory_space=pltpu.SMEM)
    vmem = pl.BlockSpec(memory_space=pltpu.VMEM)
    f32 = jnp.float32
    return pl.pallas_call(
        halo_body,
        out_shape=(
            *halo_shapes(tile),
            jax.ShapeDtypeStruct((EARLY, planes, WIN, WIN), f32),
            jax.ShapeDtypeStruct(probe.shape, f32),
        ),
        in_specs=[smem, smem, vmem, vmem, hbm, hbm],
        out_specs=(*[hbm] * 6, vmem),
        scratch_shapes=[
            pltpu.VMEM((planes, cols // WIN, rows, WIN), f32),
            pltpu.VMEM(measured.shape, f32),
            pltpu.VMEM((2, planes, rows // 2, WIN), f32),
            pltpu.VMEM((2, U, planes, WIN, WIN), f32),
            pltpu.SemaphoreType.DMA((cols // WIN,)),
            pltpu.SemaphoreType.DMA,
            pltpu.SemaphoreType.DMA((8,)),
            pltpu.SemaphoreType.DMA((8,)),
            pltpu.SemaphoreType.DMA((2,)),
        ],
        compiler_params=pltpu.CompilerParams(
            collective_id=0, has_side_effects=True, vmem_limit_bytes=56 * 1024 * 1024
        ),
        name="gather_halo",
    )(places, live, probe, jnp.asarray(matrices()), tile, measured)


def ordered(positions, count, rows, cols):
    slots = positions.shape[0]
    row = positions[:, 0] - lax.axis_index("ty") * rows
    col = positions[:, 1] - lax.axis_index("tx") * cols
    slot = jnp.arange(slots, dtype=jnp.int32)
    inside = (row >= 0) & (row <= rows - WIN) & (col >= 0) & (col <= cols - WIN)
    key = jnp.where(slot < count, jnp.where(inside, 0, 1), 2) * slots + slot
    rank = jnp.sum((key[None, :] < key[:, None]).astype(jnp.int32), axis=1)
    safe_row = jnp.clip(row, 0, rows - WIN)
    safe_col = jnp.clip(col, 0, cols - WIN)
    q = safe_col // WIN
    table = jnp.stack(
        [slot, row + RIM, col + WIN, safe_row, q, jnp.minimum(q + 1, cols // WIN - 1), safe_col % WIN, slot * 0]
    )
    hit = rank[None, :] == slot[:, None]
    table = jnp.sum(jnp.where(hit[None], table[:, None, :], 0), axis=2)
    inner = jnp.sum((inside & (slot < count)).astype(jnp.int32))
    live = (slot < inner).astype(jnp.float32)
    return table, live, jnp.stack([jnp.minimum(inner, EARLY), count])


def tail_body(
    left_ref, right_ref, top_ref, bottom_ref, corner_ref, part_ref,
    left_out, right_out, top_out, bottom_out, corner_out, total_out,
    gathered, stage, send_sems, recv_sems, tx_send, tx_recv, ty_send, ty_recv, out_send, out_recv,
):
    ty, tx = lax.axis_index("ty"), lax.axis_index("tx")
    ny, nx = lax.axis_size("ty"), lax.axis_size("tx")
    diagonal = [around(*step) for step in AROUND if 0 not in step]
    greet(diagonal)
    barrier = pltpu.get_barrier_semaphore()

    @pl.loop(1, nx)
    def _(k):
        pl.semaphore_signal(barrier, inc=1, device_id={"tx": lax.rem(tx + k, nx)}, device_id_type=MESH)

    @pl.loop(1, ny)
    def _(k):
        pl.semaphore_signal(barrier, inc=1, device_id={"ty": lax.rem(ty + k, ny)}, device_id_type=MESH)

    pl.semaphore_wait(barrier, len(diagonal) + nx - 1 + ny - 1)

    def to_column(k, source, target, sends, receives):
        return pltpu.make_async_remote_copy(
            src_ref=source,
            dst_ref=target,
            send_sem=sends.at[k],
            recv_sem=receives.at[tx],
            device_id={"tx": lax.rem(tx + k, nx)},
            device_id_type=MESH,
        )

    def to_row(k):
        return pltpu.make_async_remote_copy(
            src_ref=stage.at[ty],
            dst_ref=stage.at[ty],
            send_sem=ty_send.at[k],
            recv_sem=ty_recv.at[ty],
            device_id={"ty": lax.rem(ty + k, ny)},
            device_id_type=MESH,
        )

    def arrived(target, semaphore):
        pltpu.make_async_copy(target, target, semaphore).wait()

    def spread(k):
        return to_column(k, part_ref.at[lax.rem(tx + k, nx)], gathered.at[tx], tx_send, tx_recv)

    def share(k):
        return to_column(k, total_out.at[tx], total_out.at[tx], out_send, out_recv)

    @pl.loop(1, nx)
    def _(k):
        spread(k).start()

    moves = (
        (left_ref, right_out, (0, -1)),
        (right_ref, left_out, (0, 1)),
        (top_ref, bottom_out, (-1, 0)),
        (bottom_ref, top_out, (1, 0)),
        (corner_ref.at[0], corner_out.at[3], (-1, -1)),
        (corner_ref.at[1], corner_out.at[2], (-1, 1)),
        (corner_ref.at[2], corner_out.at[1], (1, -1)),
        (corner_ref.at[3], corner_out.at[0], (1, 1)),
    )
    halo = send(moves, send_sems, recv_sems, wait=False)

    stage[ty] = part_ref[tx]

    @pl.loop(1, nx)
    def _(k):
        source = lax.rem(tx + k, nx)
        arrived(gathered.at[source], tx_recv.at[source])
        stage[ty] += gathered[source]

    @pl.loop(1, ny)
    def _(k):
        to_row(k).start()

    @pl.loop(1, ny)
    def _(k):
        source = lax.rem(ty + k, ny)
        arrived(stage.at[source], ty_recv.at[source])

    total = stage[0]
    for i in range(1, stage.shape[0]):
        total += stage[i]
    total_out[tx] = total * (1.0 / SLOTS_ALL)

    @pl.loop(1, nx)
    def _(k):
        share(k).start()

    @pl.loop(1, nx)
    def _(k):
        source = lax.rem(tx + k, nx)
        arrived(total_out.at[source], out_recv.at[source])

    for copy in halo:
        copy.wait()

    @pl.loop(1, nx)
    def _(k):
        spread(k).wait_send()
        share(k).wait_send()

    @pl.loop(1, ny)
    def _(k):
        to_row(k).wait_send()


def exchange(halo, part):
    hbm = pl.BlockSpec(memory_space=pl.ANY)
    vmem = pl.BlockSpec(memory_space=pltpu.VMEM)
    ny, nx = lax.axis_size("ty"), lax.axis_size("tx")
    chunk = (part.size // (nx * WIN), WIN)
    return pl.pallas_call(
        tail_body,
        out_shape=(
            *(jax.ShapeDtypeStruct(h.shape, jnp.float32) for h in halo),
            jax.ShapeDtypeStruct((nx, *chunk), jnp.float32),
        ),
        in_specs=[hbm] * 5 + [vmem],
        out_specs=(*[hbm] * 5, vmem),
        scratch_shapes=[
            pltpu.VMEM((nx, *chunk), jnp.float32),
            pltpu.VMEM((ny, *chunk), jnp.float32),
            pltpu.SemaphoreType.DMA((8,)),
            pltpu.SemaphoreType.DMA((8,)),
            pltpu.SemaphoreType.DMA((nx,)),
            pltpu.SemaphoreType.DMA((nx,)),
            pltpu.SemaphoreType.DMA((ny,)),
            pltpu.SemaphoreType.DMA((ny,)),
            pltpu.SemaphoreType.DMA((nx,)),
            pltpu.SemaphoreType.DMA((nx,)),
        ],
        compiler_params=pltpu.CompilerParams(
            collective_id=1, has_side_effects=True, vmem_limit_bytes=56 * 1024 * 1024
        ),
        name="exchange",
    )(*halo, part.reshape(nx, *chunk))


def finish_body(
    tile_ref, left_ref, right_ref, top_ref, bottom_ref, corner_ref, total_ref, out_ref, total_out, edge, strip, in_sems
):
    planes, rows, cols = tile_ref.shape
    ty, tx = lax.axis_index("ty"), lax.axis_index("tx")
    ny, nx = lax.axis_size("ty"), lax.axis_size("tx")
    half = rows // 2
    ends = (pl.ds(0, RIM), pl.ds(rows - RIM, RIM))
    sides = (pl.ds(0, WIN), pl.ds(cols - WIN, WIN))
    inner = pl.ds(WIN, cols - 2 * WIN)
    parts = [(out_ref.at[:, :, span], edge.at[i]) for i, span in enumerate(sides)]
    parts += [(out_ref.at[:, span, inner], strip.at[i]) for i, span in enumerate(ends)]
    reads = [pltpu.make_async_copy(a, b, in_sems.at[i]) for i, (a, b) in enumerate(parts)]
    for copy in reads:
        copy.start()
    total_out[...] = total_ref[...]
    lane = lax.broadcasted_iota(jnp.int32, (half, WIN), 1)
    near = lane < RIM
    lane = lane[:RIM]
    no_side = (tx == 0, tx == nx - 1)
    no_end = (ty == 0, ty == ny - 1)
    for copy in reads:
        copy.wait()
    for plane in range(2):
        for i, packed in enumerate((left_ref, right_ref)):
            value = jnp.where(no_side[i], 0.0, packed[plane])
            turned = pltpu.roll(value, RIM, 1)
            mine = near if i == 0 else jnp.logical_not(near)
            first, second = (value, turned) if i == 0 else (turned, value)
            edge[i, plane, pl.ds(0, half), :] += jnp.where(mine, first, 0.0)
            edge[i, plane, pl.ds(half, half), :] += jnp.where(mine, second, 0.0)
        for j, rim in enumerate((top_ref, bottom_ref)):
            for i in range(2):
                value = jnp.where(no_end[j], 0.0, rim[plane, :, sides[i]])
                gone = jnp.logical_or(no_side[i], no_end[j])
                value += jnp.where(gone, 0.0, corner_ref[2 * j + i, plane])
                edge[i, plane, ends[j], :] += value
            strip[j, plane] += jnp.where(no_end[j], 0.0, rim[plane, :, inner])
    writes = [pltpu.make_async_copy(b, a, in_sems.at[i]) for i, (a, b) in enumerate(parts)]
    for copy in writes:
        copy.start()
    for copy in writes:
        copy.wait()


def finish(tile, halo, total):
    planes, rows, cols = tile.shape
    hbm = pl.BlockSpec(memory_space=pl.ANY)
    vmem = pl.BlockSpec(memory_space=pltpu.VMEM)
    return pl.pallas_call(
        finish_body,
        out_shape=(jax.ShapeDtypeStruct(tile.shape, jnp.float32), jax.ShapeDtypeStruct(total.shape, jnp.float32)),
        in_specs=[hbm] + [vmem] * 6,
        out_specs=(hbm, vmem),
        scratch_shapes=[
            pltpu.VMEM((2, planes, rows, WIN), jnp.float32),
            pltpu.VMEM((2, planes, RIM, cols - 2 * WIN), jnp.float32),
            pltpu.SemaphoreType.DMA((4,)),
        ],
        input_output_aliases={0: 0},
        compiler_params=pltpu.CompilerParams(vmem_limit_bytes=56 * 1024 * 1024),
        name="finish",
    )(tile, *halo, total)


def shards(object_planes, probe, positions, counts, amplitudes):
    planes, rows, cols = object_planes.shape
    places, live, numbers = ordered(positions[0, 0], counts[0, 0], rows, cols)
    measured = amplitudes[0, 0]
    *halo, patches, early_part = gather_halo(places, live, probe, object_planes, measured)
    tile, *outer, part = tile_gradient(places, numbers, probe, object_planes, halo, measured, patches, early_part)
    *outer, total = exchange(outer, part)
    tile, total = finish(tile, outer, total)
    return tile, total.reshape(probe.shape)


def solution(mesh):
    in_specs = (
        P(None, "ty", "tx"),
        P(),
        P("ty", "tx", None, None),
        P("ty", "tx"),
        P("ty", "tx", None, None, None),
    )
    out_specs = (P(None, "ty", "tx"), P())
    return jax.shard_map(shards, mesh=mesh, in_specs=in_specs, out_specs=out_specs, check_vma=False)
```

```python
import math

import jax
import jax.numpy as jnp
import numpy as np
from jax import lax
from jax.experimental import pallas as pl
from jax.experimental.pallas import tpu as pltpu
from jax.sharding import PartitionSpec as P

WIN = 128
RIM = WIN // 2
FLOOR = 0.25
AHEAD = 16
MESH = pl.DeviceIdType.MESH
SLOTS_ALL = 8 * 16 * 96
U = 8
EARLY = 48
LATE = 16


def matrices():
    index = np.arange(WIN)
    angle = 2.0 * math.pi / WIN * ((index[:, None] * index[None, :]) % WIN)
    cosine = np.cos(angle) / math.sqrt(WIN)
    sine = np.sin(angle) / math.sqrt(WIN)
    right = np.block([[cosine, -sine], [sine, cosine]])
    both = np.stack([right, right.T]).astype(np.float32)
    high = both.astype(jnp.bfloat16)
    low = (both - high.astype(np.float32)).astype(jnp.bfloat16)
    return np.stack([high, low], axis=1)


def split(value):
    high = value.astype(jnp.bfloat16)
    low = (value - high.astype(jnp.float32)).astype(jnp.bfloat16)
    return high, low


def dot(a, b):
    return lax.dot_general(a, b, (((1,), (0,)), ((), ())), preferred_element_type=jnp.float32)


def blocks(value):
    n = WIN
    return value[:n, :n], value[:n, n:], value[n:, :n], value[n:, n:]


def assemble(a, b, c, d):
    top = jnp.concatenate([a, b], axis=1)
    bottom = jnp.concatenate([c, d], axis=1)
    return jnp.concatenate([top, bottom], axis=0)


def right_product(value, w_ref, k):
    high, low = split(value)
    return dot(high, w_ref[k, 0]) + dot(low, w_ref[k, 0]) + dot(high, w_ref[k, 1])


def left_product(value, w_ref, k):
    high, low = split(value)
    return dot(w_ref[k, 0], high) + dot(w_ref[k, 0], low) + dot(w_ref[k, 1], high)


def forward(wins, probe_ref, measured, live, w_ref):
    p0r, p0i = probe_ref[0, 0], probe_ref[0, 1]
    p1r, p1i = probe_ref[1, 0], probe_ref[1, 1]
    waves = [assemble(
        p0r * a - p0i * b,
        p0r * b + p0i * a,
        p1r * a - p1i * b,
        p1r * b + p1i * a,
    ) for a, b in wins]
    xs = []
    for half in [right_product(v, w_ref, 0) for v in waves]:
        m0r, m0i, m1r, m1i = blocks(half)
        xs.append(assemble(m0r, m1r, m0i, m1i))
    out = []
    for k, far in enumerate([left_product(v, w_ref, 1) for v in xs]):
        f0r, f1r, f0i, f1i = blocks(far)
        intensity = f0r * f0r + f0i * f0i + (f1r * f1r + f1i * f1i)
        weight = live[k] - (live[k] * measured[k]) * lax.rsqrt(jnp.maximum(intensity, FLOOR))
        out.append(assemble(weight * f0r, weight * f1r, weight * f0i, weight * f1i))
    return out


def inverse(values, wins, probe_ref, w_ref):
    p0r, p0i = probe_ref[0, 0], probe_ref[0, 1]
    p1r, p1i = probe_ref[1, 0], probe_ref[1, 1]
    xs = []
    for half in [left_product(v, w_ref, 0) for v in values]:
        m0r, m1r, m0i, m1i = blocks(half)
        xs.append(assemble(m0r, m0i, m1r, m1i))
    out = []
    for (a, b), back in zip(wins, [right_product(v, w_ref, 1) for v in xs]):
        b0r, b0i, b1r, b1i = blocks(back)
        grad_re = p0r * b0r + p0i * b0i + (p1r * b1r + p1i * b1i)
        grad_im = p0r * b0i - p0i * b0r + (p1r * b1i - p1i * b1r)
        out.append((grad_re, grad_im, (a * b0r + b * b0i, a * b0i - b * b0r, a * b1r + b * b1i, a * b1i - b * b1r)))
    return out


def take(obj, row, q, q_next, shift):
    here = pl.ds(row, WIN)
    keep = lax.broadcasted_iota(jnp.int32, (WIN, WIN), 1) < WIN - shift
    window = []
    for plane in range(2):
        first = pltpu.roll(obj[plane, q, here, :], WIN - shift, 1)
        second = pltpu.roll(obj[plane, q_next, here, :], WIN - shift, 1)
        window.append(jnp.where(keep, first, second))
    return window


def put(grad, row, q, shift, values, q_next=None):
    here = pl.ds(row, WIN)
    after = lax.broadcasted_iota(jnp.int32, (WIN, WIN), 1) >= shift
    q_next = q + 1 if q_next is None else q_next
    for plane, value in enumerate(values):
        turned = pltpu.roll(value, shift, 1)
        grad[plane, q, here, :] += jnp.where(after, turned, 0.0)
        grad[plane, q_next, here, :] += jnp.where(after, 0.0, turned)


def pack(value, high):
    half = value.shape[0] // 2
    first, second = value[:half], value[half:]
    near = lax.broadcasted_iota(jnp.int32, first.shape, 1) < RIM
    if high:
        first = pltpu.roll(first, RIM, 1)
    else:
        second = pltpu.roll(second, RIM, 1)
    return jnp.where(near, first, second)


def unpack(packed, high):
    turned = pltpu.roll(packed, RIM, 1)
    return (turned, packed) if high else (packed, turned)


def deposit(grad, patches, info_of, first, end):
    for u in range(U):
        @pl.when(first + u < end)
        def _(place=first + u):
            row, q, shift, q_next = info_of(place)
            put(grad, row, q, shift, (patches[place, 0], patches[place, 1]), q_next)


def body(
    place_ref, number_ref, probe_ref, w_ref, tile_ref, left_ref, right_ref, top_ref, bottom_ref, corner_ref,
    measured_ref, patch_ref, part_ref,
    grad_tile, grad_left, grad_right, grad_top, grad_bottom, grad_corner, probe_out,
    obj, grad, held, sides, corners, patches, in_sems, held_sems, patch_sems,
):
    rows = tile_ref.shape[1]
    cols = tile_ref.shape[2]
    tiles = cols // WIN
    begin, count, early = number_ref[0], number_ref[1], number_ref[2]
    slots_max = place_ref.shape[1]

    def fetch(place):
        turn = lax.rem(place - begin, AHEAD)
        return pltpu.make_async_copy(measured_ref.at[place_ref[0, place]], held.at[turn], held_sems.at[turn])

    for ahead in range(AHEAD):
        @pl.when(begin + ahead < count)
        def _(ahead=ahead):
            fetch(begin + ahead).start()

    last = tiles + 1
    low = RIM + rows
    middle = RIM + rows // 2
    loads = []
    for q in range(tiles):
        span = pl.ds(q * WIN, WIN)
        loads.append((tile_ref.at[:, :, span], obj.at[:, q + 1, pl.ds(RIM, rows), :]))
        loads.append((top_ref.at[:, :, span], obj.at[:, q + 1, pl.ds(0, RIM), :]))
        loads.append((bottom_ref.at[:, :, span], obj.at[:, q + 1, pl.ds(low, RIM), :]))
    loads.append((corner_ref, corners))
    loads.append((left_ref, sides.at[0]))
    loads.append((right_ref, sides.at[1]))
    loads = [pltpu.make_async_copy(a, b, in_sems.at[i]) for i, (a, b) in enumerate(loads)]
    pieces = patch_ref.shape[0] // U
    chunks = [
        pltpu.make_async_copy(patch_ref.at[pl.ds(i * U, U)], patches.at[pl.ds(i * U, U)], patch_sems.at[i])
        for i in range(pieces)
    ]
    for copy in chunks[:2] + loads + chunks[2:]:
        copy.start()
    grad[...] = jnp.zeros_like(grad)
    probe_out[...] = part_ref[...]

    def info_of(place):
        safe = jnp.minimum(place, slots_max - 1)
        row, col = place_ref[1, safe], place_ref[2, safe]
        return row, col // WIN, lax.rem(col, WIN), col // WIN + 1

    for i, copy in enumerate(chunks):
        copy.wait()
        deposit(grad, patches, info_of, i * U, early)
    for copy in loads:
        copy.wait()
    for plane in range(2):
        for q, high in ((0, True), (last, False)):
            side = 0 if high else 1
            pieces = ((corners[side, plane], 0), (sides[side, plane], RIM), (corners[2 + side, plane], low))
            for packed, start in pieces:
                half = packed.shape[0]
                for i, value in enumerate(unpack(packed, high)):
                    obj[plane, q, pl.ds(start + i * half, half), :] = value
    ty, tx = lax.axis_index("ty"), lax.axis_index("tx")

    @pl.when(ty == 0)
    def _():
        obj[:, :, pl.ds(0, RIM), :] = jnp.zeros((2, tiles + 2, RIM, WIN), jnp.float32)

    @pl.when(ty == lax.axis_size("ty") - 1)
    def _():
        obj[:, :, pl.ds(low, RIM), :] = jnp.zeros((2, tiles + 2, RIM, WIN), jnp.float32)

    @pl.when(tx == 0)
    def _():
        obj[:, 0] = jnp.zeros((2, rows + WIN, WIN), jnp.float32)

    @pl.when(tx == lax.axis_size("tx") - 1)
    def _():
        obj[:, last] = jnp.zeros((2, rows + WIN, WIN), jnp.float32)


    @pl.loop(0, (count - begin + U - 1) // U)
    def _(group):
        places = [begin + group * U + u for u in range(U)]
        wins = []
        for place in places:
            row, q, shift, q_next = info_of(place)
            wins.append(take(obj, row, q, q_next, shift))
        for place in places:
            @pl.when(place < count)
            def _():
                fetch(place).wait()
        held_now = [held[lax.rem(place - begin, AHEAD)] for place in places]
        live = [jnp.where(place < count, 1.0, 0.0) for place in places]
        results = inverse(forward(wins, probe_ref, held_now, live, w_ref), wins, probe_ref, w_ref)
        for place, (grad_re, grad_im, terms) in zip(places, results):
            row, q, shift, q_next = info_of(place)
            put(grad, row, q, shift, (grad_re, grad_im), q_next)
        for i in range(4):
            probe_out[i // 2, i % 2] += sum(r[2][i] for r in results)
        for place in places:
            @pl.when(place + AHEAD < count)
            def _():
                fetch(place + AHEAD).start()

    stores = []
    for q in range(tiles):
        span = pl.ds(q * WIN, WIN)
        stores.append((grad.at[:, q + 1, pl.ds(RIM, rows), :], grad_tile.at[:, :, span]))
        stores.append((grad.at[:, q + 1, pl.ds(0, RIM), :], grad_top.at[:, :, span]))
        stores.append((grad.at[:, q + 1, pl.ds(low, RIM), :], grad_bottom.at[:, :, span]))
    stores.append((corners, grad_corner))
    stores.append((sides.at[0], grad_left))
    stores.append((sides.at[1], grad_right))
    stores = [pltpu.make_async_copy(a, b, in_sems.at[i]) for i, (a, b) in enumerate(stores)]
    for copy in stores[:-3]:
        copy.start()
    for plane in range(2):
        for q, high in ((0, True), (last, False)):
            side = 0 if high else 1
            corners[side, plane] = pack(grad[plane, q, pl.ds(0, RIM), :], high)
            corners[2 + side, plane] = pack(grad[plane, q, pl.ds(low, RIM), :], high)
            sides[side, plane] = pack(grad[plane, q, pl.ds(RIM, rows), :], high)
    for copy in stores[-3:]:
        copy.start()
    for copy in stores:
        copy.wait()


def tile_gradient(places, numbers, probe, tile, halo, measured, patches, part):
    planes, rows, cols = tile.shape
    tiles = cols // WIN
    f32 = jnp.float32
    smem = pl.BlockSpec(memory_space=pltpu.SMEM)
    vmem = pl.BlockSpec(memory_space=pltpu.VMEM)
    hbm = pl.BlockSpec(memory_space=pl.ANY)
    extent = (planes, tiles + 2, rows + WIN, WIN)
    copies = 3 * tiles + 3
    return pl.pallas_call(
        body,
        out_shape=(
            jax.ShapeDtypeStruct(tile.shape, f32),
            *(jax.ShapeDtypeStruct(h.shape, f32) for h in halo),
            jax.ShapeDtypeStruct(probe.shape, f32),
        ),
        in_specs=[smem, smem, vmem, vmem] + [hbm] * 8 + [vmem],
        out_specs=(*[hbm] * 6, vmem),
        scratch_shapes=[
            pltpu.VMEM(extent, f32),
            pltpu.VMEM(extent, f32),
            pltpu.VMEM((AHEAD, WIN, WIN), f32),
            pltpu.VMEM((2, planes, rows // 2, WIN), f32),
            pltpu.VMEM((4, planes, RIM // 2, WIN), f32),
            pltpu.VMEM(patches.shape, f32),
            pltpu.SemaphoreType.DMA((copies,)),
            pltpu.SemaphoreType.DMA((AHEAD,)),
            pltpu.SemaphoreType.DMA((patches.shape[0] // U,)),
        ],
        compiler_params=pltpu.CompilerParams(vmem_limit_bytes=56 * 1024 * 1024),
        name="tile_gradient",
    )(places, numbers, probe, jnp.asarray(matrices()), tile, *halo, measured, patches, part)


AROUND = ((-1, 0), (1, 0), (0, -1), (0, 1), (-1, -1), (-1, 1), (1, -1), (1, 1))


def ring(axis, by):
    size = lax.axis_size(axis)
    return lax.rem(lax.axis_index(axis) + (by + size), size)


def around(dy, dx):
    return {"ty": ring("ty", dy), "tx": ring("tx", dx)}


def greet(partners):
    barrier = pltpu.get_barrier_semaphore()
    for partner in partners:
        pl.semaphore_signal(barrier, inc=1, device_id=partner, device_id_type=MESH)


def inner_patches(
    begin, place_ref, live_ref, probe_ref, w_ref, obj, held, patches, patch_out, patch_sems, add
):
    def store(group):
        turn = lax.rem(group, 2)
        return pltpu.make_async_copy(patches.at[turn], patch_out.at[pl.ds(group * U, U)], patch_sems.at[turn])

    groups = patch_out.shape[0] // U

    @pl.loop(0, groups)
    def _(group):
        turn = lax.rem(group, 2)

        @pl.when(group >= 2)
        def _():
            store(group - 2).wait()

        places = [begin + group * U + u for u in range(U)]
        wins = [
            take(obj, place_ref[3, p], place_ref[4, p], place_ref[5, p], place_ref[6, p]) for p in places
        ]
        held_now = [held[place_ref[0, p]] for p in places]
        live = [live_ref[p] for p in places]
        results = inverse(forward(wins, probe_ref, held_now, live, w_ref), wins, probe_ref, w_ref)
        for u, (grad_re, grad_im, terms) in enumerate(results):
            patches[turn, u, 0] = grad_re
            patches[turn, u, 1] = grad_im
        for i in range(4):
            add(i, sum(r[2][i] for r in results))
        store(group).start()

    for group in range(max(groups - 2, 0), groups):
        store(group).wait()


def halo_body(
    place_ref, live_ref, probe_ref, w_ref, tile_ref, measured_ref,
    left_out, right_out, top_out, bottom_out, corner_out, patch_out, part_out,
    obj, held, packed, corners, patches, in_sems, held_sem, send_sems, recv_sems, patch_sems,
):
    rows, cols = tile_ref.shape[1:]
    tiles = cols // WIN
    greet([around(*step) for step in AROUND])
    loads = [
        pltpu.make_async_copy(tile_ref.at[:, :, pl.ds(q * WIN, WIN)], obj.at[:, q], in_sems.at[q])
        for q in range(tiles)
    ]
    for q in (0, tiles - 1, *range(1, tiles - 1)):
        loads[q].start()
    measures = pltpu.make_async_copy(measured_ref, held, held_sem)
    measures.start()
    part_out[...] = jnp.zeros_like(part_out)
    above, below = pl.ds(0, RIM), pl.ds(rows - RIM, RIM)
    for side, q in enumerate((0, tiles - 1)):
        loads[q].wait()
        for plane in range(2):
            packed[side, plane] = pack(obj[plane, q], side == 1)
            corners[side, plane] = pack(obj[plane, q, above, :], side == 1)
            corners[2 + side, plane] = pack(obj[plane, q, below, :], side == 1)
    pl.semaphore_wait(pltpu.get_barrier_semaphore(), len(AROUND))
    moves = (
        (packed.at[0], right_out, (0, -1)),
        (packed.at[1], left_out, (0, 1)),
        (tile_ref.at[:, above, :], bottom_out, (-1, 0)),
        (tile_ref.at[:, below, :], top_out, (1, 0)),
        (corners.at[3], corner_out.at[0], (1, 1)),
        (corners.at[2], corner_out.at[1], (1, -1)),
        (corners.at[1], corner_out.at[2], (-1, 1)),
        (corners.at[0], corner_out.at[3], (-1, -1)),
    )
    halo = send(moves, send_sems, recv_sems, wait=False)
    for q in range(1, tiles - 1):
        loads[q].wait()
    measures.wait()

    def add(i, term):
        part_out[i // 2, i % 2] += term

    inner_patches(0, place_ref, live_ref, probe_ref, w_ref, obj, held, patches, patch_out, patch_sems, add)
    for copy in halo:
        copy.wait()


def send(moves, send_sems, recv_sems, wait=True):
    copies = [
        pltpu.make_async_remote_copy(
            src_ref=source,
            dst_ref=target,
            send_sem=send_sems.at[i],
            recv_sem=recv_sems.at[i],
            device_id=around(*step),
            device_id_type=MESH,
        )
        for i, (source, target, step) in enumerate(moves)
    ]
    for copy in copies:
        copy.start()
    if wait:
        for copy in copies:
            copy.wait()
    return copies


def halo_shapes(tile):
    planes, rows, cols = tile.shape
    shapes = [(planes, rows // 2, WIN)] * 2 + [(planes, RIM, cols)] * 2 + [(4, planes, RIM // 2, WIN)]
    return tuple(jax.ShapeDtypeStruct(s, jnp.float32) for s in shapes)


def gather_halo(places, live, probe, tile, measured):
    planes, rows, cols = tile.shape
    hbm = pl.BlockSpec(memory_space=pl.ANY)
    smem = pl.BlockSpec(memory_space=pltpu.SMEM)
    vmem = pl.BlockSpec(memory_space=pltpu.VMEM)
    f32 = jnp.float32
    return pl.pallas_call(
        halo_body,
        out_shape=(
            *halo_shapes(tile),
            jax.ShapeDtypeStruct((EARLY, planes, WIN, WIN), f32),
            jax.ShapeDtypeStruct(probe.shape, f32),
        ),
        in_specs=[smem, smem, vmem, vmem, hbm, hbm],
        out_specs=(*[hbm] * 6, vmem),
        scratch_shapes=[
            pltpu.VMEM((planes, cols // WIN, rows, WIN), f32),
            pltpu.VMEM(measured.shape, f32),
            pltpu.VMEM((2, planes, rows // 2, WIN), f32),
            pltpu.VMEM((4, planes, RIM // 2, WIN), f32),
            pltpu.VMEM((2, U, planes, WIN, WIN), f32),
            pltpu.SemaphoreType.DMA((cols // WIN,)),
            pltpu.SemaphoreType.DMA,
            pltpu.SemaphoreType.DMA((8,)),
            pltpu.SemaphoreType.DMA((8,)),
            pltpu.SemaphoreType.DMA((2,)),
        ],
        compiler_params=pltpu.CompilerParams(
            collective_id=0, has_side_effects=True, vmem_limit_bytes=56 * 1024 * 1024
        ),
        name="gather_halo",
    )(places, live, probe, jnp.asarray(matrices()), tile, measured)


def ordered(positions, count, rows, cols):
    slots = positions.shape[0]
    row = positions[:, 0] - lax.axis_index("ty") * rows
    col = positions[:, 1] - lax.axis_index("tx") * cols
    slot = jnp.arange(slots, dtype=jnp.int32)
    inside = (row >= 0) & (row <= rows - WIN) & (col >= 0) & (col <= cols - WIN)
    key = jnp.where(slot < count, jnp.where(inside, 0, 1), 2) * slots + slot
    rank = jnp.sum((key[None, :] < key[:, None]).astype(jnp.int32), axis=1)
    safe_row = jnp.clip(row, 0, rows - WIN)
    safe_col = jnp.clip(col, 0, cols - WIN)
    q = safe_col // WIN
    table = jnp.stack(
        [slot, row + RIM, col + WIN, safe_row, q, jnp.minimum(q + 1, cols // WIN - 1), safe_col % WIN, slot * 0]
    )
    hit = rank[None, :] == slot[:, None]
    table = jnp.sum(jnp.where(hit[None], table[:, None, :], 0), axis=2)
    inner = jnp.sum((inside & (slot < count)).astype(jnp.int32))
    live = (slot < inner).astype(jnp.float32)
    early = jnp.minimum(inner, EARLY)
    done = jnp.minimum(inner, EARLY + LATE)
    return table, live, jnp.stack([done, count, early, done - early])


def tail_body(
    place_ref, live_ref, probe_ref, w_ref, tile_ref, measured_ref,
    left_ref, right_ref, top_ref, bottom_ref, corner_ref, start_ref,
    left_out, right_out, top_out, bottom_out, corner_out, patch_out, total_out,
    obj, held, patches, part_ref, gathered, stage, in_sems, held_sem, patch_sems,
    send_sems, recv_sems, tx_send, tx_recv, ty_send, ty_recv, out_send, out_recv,
):
    ty, tx = lax.axis_index("ty"), lax.axis_index("tx")
    ny, nx = lax.axis_size("ty"), lax.axis_size("tx")
    diagonal = [around(*step) for step in AROUND if 0 not in step]
    greet(diagonal)
    barrier = pltpu.get_barrier_semaphore()

    @pl.loop(1, nx)
    def _(k):
        pl.semaphore_signal(barrier, inc=1, device_id={"tx": lax.rem(tx + k, nx)}, device_id_type=MESH)

    @pl.loop(1, ny)
    def _(k):
        pl.semaphore_signal(barrier, inc=1, device_id={"ty": lax.rem(ty + k, ny)}, device_id_type=MESH)

    tiles = tile_ref.shape[2] // WIN
    loads = [
        pltpu.make_async_copy(tile_ref.at[:, :, pl.ds(q * WIN, WIN)], obj.at[:, q], in_sems.at[q])
        for q in range(tiles)
    ]
    loads.append(pltpu.make_async_copy(measured_ref, held, held_sem))
    for copy in loads:
        copy.start()
    part_ref[...] = start_ref[...]
    pl.semaphore_wait(barrier, len(diagonal) + nx - 1 + ny - 1)

    def to_column(k, source, target, sends, receives):
        return pltpu.make_async_remote_copy(
            src_ref=source,
            dst_ref=target,
            send_sem=sends.at[k],
            recv_sem=receives.at[tx],
            device_id={"tx": lax.rem(tx + k, nx)},
            device_id_type=MESH,
        )

    def to_row(k):
        return pltpu.make_async_remote_copy(
            src_ref=stage.at[ty],
            dst_ref=stage.at[ty],
            send_sem=ty_send.at[k],
            recv_sem=ty_recv.at[ty],
            device_id={"ty": lax.rem(ty + k, ny)},
            device_id_type=MESH,
        )

    def arrived(target, semaphore):
        pltpu.make_async_copy(target, target, semaphore).wait()

    def spread(k):
        return to_column(k, part_ref.at[lax.rem(tx + k, nx)], gathered.at[tx], tx_send, tx_recv)

    def share(k):
        return to_column(k, total_out.at[tx], total_out.at[tx], out_send, out_recv)

    moves = (
        (left_ref, right_out, (0, -1)),
        (right_ref, left_out, (0, 1)),
        (top_ref, bottom_out, (-1, 0)),
        (bottom_ref, top_out, (1, 0)),
        (corner_ref.at[0], corner_out.at[3], (-1, -1)),
        (corner_ref.at[1], corner_out.at[2], (-1, 1)),
        (corner_ref.at[2], corner_out.at[1], (1, -1)),
        (corner_ref.at[3], corner_out.at[0], (1, 1)),
    )
    halo = send(moves, send_sems, recv_sems, wait=False)
    for copy in loads:
        copy.wait()

    def add(i, term):
        each = part_ref.shape[0] // 4
        part_ref[pl.ds(i * each, each)] += term.reshape(each, WIN // each, WIN)

    inner_patches(EARLY, place_ref, live_ref, probe_ref, w_ref, obj, held, patches, patch_out, patch_sems, add)

    @pl.loop(1, nx)
    def _(k):
        spread(k).start()

    stage[ty] = part_ref[tx]

    @pl.loop(1, nx)
    def _(k):
        source = lax.rem(tx + k, nx)
        arrived(gathered.at[source], tx_recv.at[source])
        stage[ty] += gathered[source]

    @pl.loop(1, ny)
    def _(k):
        to_row(k).start()

    @pl.loop(1, ny)
    def _(k):
        source = lax.rem(ty + k, ny)
        arrived(stage.at[source], ty_recv.at[source])

    total = stage[0]
    for i in range(1, stage.shape[0]):
        total += stage[i]
    total_out[tx] = total * (1.0 / SLOTS_ALL)

    @pl.loop(1, nx)
    def _(k):
        share(k).start()

    @pl.loop(1, nx)
    def _(k):
        source = lax.rem(tx + k, nx)
        arrived(total_out.at[source], out_recv.at[source])

    for copy in halo:
        copy.wait()

    @pl.loop(1, nx)
    def _(k):
        spread(k).wait_send()
        share(k).wait_send()

    @pl.loop(1, ny)
    def _(k):
        to_row(k).wait_send()


def exchange(places, live, probe, tile, measured, halo, part):
    hbm = pl.BlockSpec(memory_space=pl.ANY)
    vmem = pl.BlockSpec(memory_space=pltpu.VMEM)
    smem = pl.BlockSpec(memory_space=pltpu.SMEM)
    planes, rows, cols = tile.shape
    ny, nx = lax.axis_size("ty"), lax.axis_size("tx")
    chunk = (part.size // (nx * WIN), WIN)
    return pl.pallas_call(
        tail_body,
        out_shape=(
            *(jax.ShapeDtypeStruct(h.shape, jnp.float32) for h in halo),
            jax.ShapeDtypeStruct((LATE, planes, WIN, WIN), jnp.float32),
            jax.ShapeDtypeStruct((nx, *chunk), jnp.float32),
        ),
        in_specs=[smem, smem, vmem, vmem] + [hbm] * 7 + [vmem],
        out_specs=(*[hbm] * 6, vmem),
        scratch_shapes=[
            pltpu.VMEM((planes, cols // WIN, rows, WIN), jnp.float32),
            pltpu.VMEM(measured.shape, jnp.float32),
            pltpu.VMEM((2, U, planes, WIN, WIN), jnp.float32),
            pltpu.VMEM((nx, *chunk), jnp.float32),
            pltpu.VMEM((nx, *chunk), jnp.float32),
            pltpu.VMEM((ny, *chunk), jnp.float32),
            pltpu.SemaphoreType.DMA((cols // WIN,)),
            pltpu.SemaphoreType.DMA,
            pltpu.SemaphoreType.DMA((2,)),
            pltpu.SemaphoreType.DMA((8,)),
            pltpu.SemaphoreType.DMA((8,)),
            pltpu.SemaphoreType.DMA((nx,)),
            pltpu.SemaphoreType.DMA((nx,)),
            pltpu.SemaphoreType.DMA((ny,)),
            pltpu.SemaphoreType.DMA((ny,)),
            pltpu.SemaphoreType.DMA((nx,)),
            pltpu.SemaphoreType.DMA((nx,)),
        ],
        compiler_params=pltpu.CompilerParams(
            collective_id=1, has_side_effects=True, vmem_limit_bytes=56 * 1024 * 1024
        ),
        name="exchange",
    )(places, live, probe, jnp.asarray(matrices()), tile, measured, *halo, part.reshape(nx, *chunk))


def finish_body(
    place_ref, number_ref, tile_ref, left_ref, right_ref, top_ref, bottom_ref, corner_ref, patch_ref, total_ref,
    out_ref, total_out, grad, sides, rims, corners, patches, in_sems, more_sems,
):
    planes, rows, cols = tile_ref.shape
    tiles = cols // WIN
    ty, tx = lax.axis_index("ty"), lax.axis_index("tx")
    ny, nx = lax.axis_size("ty"), lax.axis_size("tx")
    late = number_ref[3]
    spans = [pl.ds(q * WIN, WIN) for q in range(tiles)]
    more = (
        (patch_ref, patches),
        (left_ref, sides.at[0]),
        (right_ref, sides.at[1]),
        (top_ref, rims.at[0]),
        (bottom_ref, rims.at[1]),
        (corner_ref, corners),
    )
    more = [pltpu.make_async_copy(a, b, more_sems.at[i]) for i, (a, b) in enumerate(more)]
    reads = [
        pltpu.make_async_copy(tile_ref.at[:, :, span], grad.at[:, q], in_sems.at[q]) for q, span in enumerate(spans)
    ]
    for copy in reads + more:
        copy.start()
    total_out[...] = total_ref[...]
    no_side = (tx == 0, tx == nx - 1)
    no_end = (ty == 0, ty == ny - 1)
    ends = (0, rows - RIM)
    for copy in reads + more:
        copy.wait()

    def info_of(place):
        at = EARLY + place
        return place_ref[3, at], place_ref[4, at], place_ref[6, at], place_ref[5, at]

    for first in range(0, patches.shape[0], U):
        deposit(grad, patches, info_of, first, late)

    def side_add(plane, side, start, packed, gone):
        high = side == 1
        half = packed.shape[0]
        far = lax.broadcasted_iota(jnp.int32, packed.shape, 1) >= RIM
        mine = far if high else jnp.logical_not(far)
        for i, value in enumerate(unpack(packed, high)):
            here = pl.ds(start + i * half, half)
            value = jnp.where(gone, 0.0, value)
            grad[plane, side * (tiles - 1), here, :] += jnp.where(mine, value, 0.0)

    for plane in range(2):
        for side in range(2):
            side_add(plane, side, 0, sides[side, plane], no_side[side])
            for end in range(2):
                gone = jnp.logical_or(no_side[side], no_end[end])
                side_add(plane, side, ends[end], corners[2 * end + side, plane], gone)
        for end in range(2):
            for q in range(tiles):
                value = jnp.where(no_end[end], 0.0, rims[end, plane, :, spans[q]])
                grad[plane, q, pl.ds(ends[end], RIM), :] += value
    writes = [
        pltpu.make_async_copy(grad.at[:, q], out_ref.at[:, :, span], in_sems.at[q]) for q, span in enumerate(spans)
    ]
    for copy in writes:
        copy.start()
    for copy in writes:
        copy.wait()


def finish(places, numbers, tile, halo, patches, total):
    planes, rows, cols = tile.shape
    hbm = pl.BlockSpec(memory_space=pl.ANY)
    vmem = pl.BlockSpec(memory_space=pltpu.VMEM)
    smem = pl.BlockSpec(memory_space=pltpu.SMEM)
    f32 = jnp.float32
    return pl.pallas_call(
        finish_body,
        out_shape=(jax.ShapeDtypeStruct(tile.shape, f32), jax.ShapeDtypeStruct(total.shape, f32)),
        in_specs=[smem, smem] + [hbm] * 7 + [vmem],
        out_specs=(hbm, vmem),
        scratch_shapes=[
            pltpu.VMEM((planes, cols // WIN, rows, WIN), f32),
            pltpu.VMEM((2, planes, rows // 2, WIN), f32),
            pltpu.VMEM((2, planes, RIM, cols), f32),
            pltpu.VMEM((4, planes, RIM // 2, WIN), f32),
            pltpu.VMEM(patches.shape, f32),
            pltpu.SemaphoreType.DMA((cols // WIN,)),
            pltpu.SemaphoreType.DMA((6,)),
        ],
        compiler_params=pltpu.CompilerParams(vmem_limit_bytes=56 * 1024 * 1024),
        name="finish",
    )(places, numbers, tile, *halo, patches, total)


def shards(object_planes, probe, positions, counts, amplitudes):
    planes, rows, cols = object_planes.shape
    places, live, numbers = ordered(positions[0, 0], counts[0, 0], rows, cols)
    measured = amplitudes[0, 0]
    *halo, patches, early_part = gather_halo(places, live, probe, object_planes, measured)
    tile, *outer, part = tile_gradient(places, numbers, probe, object_planes, halo, measured, patches, early_part)
    *outer, patches, total = exchange(places, live, probe, object_planes, measured, outer, part)
    tile, total = finish(places, numbers, tile, outer, patches, total)
    return tile, total.reshape(probe.shape)


def solution(mesh):
    in_specs = (
        P(None, "ty", "tx"),
        P(),
        P("ty", "tx", None, None),
        P("ty", "tx"),
        P("ty", "tx", None, None, None),
    )
    out_specs = (P(None, "ty", "tx"), P())
    return jax.shard_map(shards, mesh=mesh, in_specs=in_specs, out_specs=out_specs, check_vma=False)
```

```python
import math

import jax
import jax.numpy as jnp
import numpy as np
from jax import lax
from jax.experimental import pallas as pl
from jax.experimental.pallas import tpu as pltpu
from jax.sharding import PartitionSpec as P

WIN = 128
RIM = WIN // 2
FLOOR = 0.25
AHEAD = 16
MESH = pl.DeviceIdType.MESH
SLOTS_ALL = 8 * 16 * 96
U = 8
SMALL = 4
WIDE = 16
STAGES = 7
EARLY = 48
LATE = 16


def matrices():
    index = np.arange(WIN)
    angle = 2.0 * math.pi / WIN * ((index[:, None] * index[None, :]) % WIN)
    cosine = np.cos(angle) / math.sqrt(WIN)
    sine = np.sin(angle) / math.sqrt(WIN)
    right = np.block([[cosine, -sine], [sine, cosine]])
    both = np.stack([right, right.T]).astype(np.float32)
    high = both.astype(jnp.bfloat16)
    low = (both - high.astype(np.float32)).astype(jnp.bfloat16)
    return np.stack([high, low], axis=1)


def split(value):
    high = value.astype(jnp.bfloat16)
    low = (value - high.astype(jnp.float32)).astype(jnp.bfloat16)
    return high, low


def dot(a, b):
    return lax.dot_general(a, b, (((1,), (0,)), ((), ())), preferred_element_type=jnp.float32)


def blocks(value):
    n = WIN
    return value[:n, :n], value[:n, n:], value[n:, :n], value[n:, n:]


def assemble(a, b, c, d):
    top = jnp.concatenate([a, b], axis=1)
    bottom = jnp.concatenate([c, d], axis=1)
    return jnp.concatenate([top, bottom], axis=0)


def right_product(value, w_ref, k):
    high, low = split(value)
    return dot(high, w_ref[k, 0]) + dot(low, w_ref[k, 0]) + dot(high, w_ref[k, 1])


def left_product(value, w_ref, k):
    high, low = split(value)
    return dot(w_ref[k, 0], high) + dot(w_ref[k, 0], low) + dot(w_ref[k, 1], high)


def slot_steps(window, probe_ref, measured, live, w_ref):
    a, b = window
    p0r, p0i = probe_ref[0, 0], probe_ref[0, 1]
    p1r, p1i = probe_ref[1, 0], probe_ref[1, 1]
    wave = assemble(
        p0r * a - p0i * b,
        p0r * b + p0i * a,
        p1r * a - p1i * b,
        p1r * b + p1i * a,
    )
    yield
    half = right_product(wave, w_ref, 0)
    yield
    m0r, m0i, m1r, m1i = blocks(half)
    far = left_product(assemble(m0r, m1r, m0i, m1i), w_ref, 1)
    yield
    f0r, f1r, f0i, f1i = blocks(far)
    intensity = f0r * f0r + f0i * f0i + (f1r * f1r + f1i * f1i)
    weight = live - (live * measured) * lax.rsqrt(jnp.maximum(intensity, FLOOR))
    value = assemble(weight * f0r, weight * f1r, weight * f0i, weight * f1i)
    yield
    half = left_product(value, w_ref, 0)
    yield
    m0r, m1r, m0i, m1i = blocks(half)
    back = right_product(assemble(m0r, m0i, m1r, m1i), w_ref, 1)
    yield
    b0r, b0i, b1r, b1i = blocks(back)
    grad_re = p0r * b0r + p0i * b0i + (p1r * b1r + p1i * b1i)
    grad_im = p0r * b0i - p0i * b0r + (p1r * b1i - p1i * b1r)
    yield grad_re, grad_im, (a * b0r + b * b0i, a * b0i - b * b0r, a * b1r + b * b1i, a * b1i - b * b1r)


def pipelined(start, finish, size):
    runs = [None] * size
    for moment in range(STAGES + size - 1):
        for u in reversed(range(size)):
            stage = moment - u
            if 0 <= stage < STAGES:
                if stage == 0:
                    runs[u] = start(u)
                result = next(runs[u])
                if stage == STAGES - 1:
                    finish(u, *result)


def take(obj, row, q, q_next, shift):
    here = pl.ds(row, WIN)
    keep = lax.broadcasted_iota(jnp.int32, (WIN, WIN), 1) < WIN - shift
    window = []
    for plane in range(2):
        first = pltpu.roll(obj[plane, q, here, :], WIN - shift, 1)
        second = pltpu.roll(obj[plane, q_next, here, :], WIN - shift, 1)
        window.append(jnp.where(keep, first, second))
    return window


def put(grad, row, q, shift, values, q_next=None):
    here = pl.ds(row, WIN)
    after = lax.broadcasted_iota(jnp.int32, (WIN, WIN), 1) >= shift
    q_next = q + 1 if q_next is None else q_next
    for plane, value in enumerate(values):
        turned = pltpu.roll(value, shift, 1)
        grad[plane, q, here, :] += jnp.where(after, turned, 0.0)
        grad[plane, q_next, here, :] += jnp.where(after, 0.0, turned)


def pack(value, high):
    half = value.shape[0] // 2
    first, second = value[:half], value[half:]
    near = lax.broadcasted_iota(jnp.int32, first.shape, 1) < RIM
    if high:
        first = pltpu.roll(first, RIM, 1)
    else:
        second = pltpu.roll(second, RIM, 1)
    return jnp.where(near, first, second)


def unpack(packed, high):
    turned = pltpu.roll(packed, RIM, 1)
    return (turned, packed) if high else (packed, turned)


def deposit(grad, patches, info_of, first, end):
    for u in range(U):
        @pl.when(first + u < end)
        def _(place=first + u):
            row, q, shift, q_next = info_of(place)
            put(grad, row, q, shift, (patches[place, 0], patches[place, 1]), q_next)


def body(
    place_ref, number_ref, probe_ref, w_ref, tile_ref, left_ref, right_ref, top_ref, bottom_ref, corner_ref,
    measured_ref, patch_ref, part_ref,
    grad_tile, grad_left, grad_right, grad_top, grad_bottom, grad_corner, probe_out,
    obj, grad, held, sides, corners, patches, in_sems, held_sems, patch_sems,
):
    rows = tile_ref.shape[1]
    cols = tile_ref.shape[2]
    tiles = cols // WIN
    begin, count, early = number_ref[0], number_ref[1], number_ref[2]
    slots_max = place_ref.shape[1]

    def fetch(place):
        turn = lax.rem(place - begin, AHEAD)
        return pltpu.make_async_copy(measured_ref.at[place_ref[0, place]], held.at[turn], held_sems.at[turn])

    for ahead in range(AHEAD):
        @pl.when(begin + ahead < count)
        def _(ahead=ahead):
            fetch(begin + ahead).start()

    last = tiles + 1
    low = RIM + rows
    middle = RIM + rows // 2
    loads = []
    for q in range(tiles):
        span = pl.ds(q * WIN, WIN)
        loads.append((tile_ref.at[:, :, span], obj.at[:, q + 1, pl.ds(RIM, rows), :]))
        loads.append((top_ref.at[:, :, span], obj.at[:, q + 1, pl.ds(0, RIM), :]))
        loads.append((bottom_ref.at[:, :, span], obj.at[:, q + 1, pl.ds(low, RIM), :]))
    loads.append((corner_ref, corners))
    loads.append((left_ref, sides.at[0]))
    loads.append((right_ref, sides.at[1]))
    loads = [pltpu.make_async_copy(a, b, in_sems.at[i]) for i, (a, b) in enumerate(loads)]
    pieces = patch_ref.shape[0] // U
    chunks = [
        pltpu.make_async_copy(patch_ref.at[pl.ds(i * U, U)], patches.at[pl.ds(i * U, U)], patch_sems.at[i])
        for i in range(pieces)
    ]
    for copy in chunks[:2] + loads + chunks[2:]:
        copy.start()
    grad[...] = jnp.zeros_like(grad)
    probe_out[...] = part_ref[...]

    def info_of(place):
        safe = jnp.minimum(place, slots_max - 1)
        row, col = place_ref[1, safe], place_ref[2, safe]
        return row, col // WIN, lax.rem(col, WIN), col // WIN + 1

    for i, copy in enumerate(chunks):
        copy.wait()
        deposit(grad, patches, info_of, i * U, early)
    for copy in loads:
        copy.wait()
    for plane in range(2):
        for q, high in ((0, True), (last, False)):
            side = 0 if high else 1
            pieces = ((corners[side, plane], 0), (sides[side, plane], RIM), (corners[2 + side, plane], low))
            for packed, start in pieces:
                half = packed.shape[0]
                for i, value in enumerate(unpack(packed, high)):
                    obj[plane, q, pl.ds(start + i * half, half), :] = value
    ty, tx = lax.axis_index("ty"), lax.axis_index("tx")

    @pl.when(ty == 0)
    def _():
        obj[:, :, pl.ds(0, RIM), :] = jnp.zeros((2, tiles + 2, RIM, WIN), jnp.float32)

    @pl.when(ty == lax.axis_size("ty") - 1)
    def _():
        obj[:, :, pl.ds(low, RIM), :] = jnp.zeros((2, tiles + 2, RIM, WIN), jnp.float32)

    @pl.when(tx == 0)
    def _():
        obj[:, 0] = jnp.zeros((2, rows + WIN, WIN), jnp.float32)

    @pl.when(tx == lax.axis_size("tx") - 1)
    def _():
        obj[:, last] = jnp.zeros((2, rows + WIN, WIN), jnp.float32)


    def run(first, size):
        places = [first + u for u in range(size)]
        for place in places:
            @pl.when(place < count)
            def _(place=place):
                fetch(place).wait()
        terms = []

        def start(u):
            row, q, shift, q_next = info_of(places[u])
            window = take(obj, row, q, q_next, shift)
            live = jnp.where(places[u] < count, 1.0, 0.0)
            return slot_steps(window, probe_ref, held[lax.rem(places[u] - begin, AHEAD)], live, w_ref)

        def finish(u, grad_re, grad_im, term):
            row, q, shift, q_next = info_of(places[u])
            put(grad, row, q, shift, (grad_re, grad_im), q_next)
            terms.append(term)

        pipelined(start, finish, size)
        for i in range(4):
            probe_out[i // 2, i % 2] += sum(term[i] for term in terms)
        for place in places:
            @pl.when(place + AHEAD < count)
            def _(place=place):
                fetch(place + AHEAD).start()

    rest = count - begin
    whole = (rest + SMALL - 1) // U

    @pl.loop(0, whole)
    def _(group):
        run(begin + group * U, U)

    @pl.when(rest > whole * U)
    def _():
        run(begin + whole * U, SMALL)

    stores = []
    for q in range(tiles):
        span = pl.ds(q * WIN, WIN)
        stores.append((grad.at[:, q + 1, pl.ds(RIM, rows), :], grad_tile.at[:, :, span]))
        stores.append((grad.at[:, q + 1, pl.ds(0, RIM), :], grad_top.at[:, :, span]))
        stores.append((grad.at[:, q + 1, pl.ds(low, RIM), :], grad_bottom.at[:, :, span]))
    stores.append((corners, grad_corner))
    stores.append((sides.at[0], grad_left))
    stores.append((sides.at[1], grad_right))
    stores = [pltpu.make_async_copy(a, b, in_sems.at[i]) for i, (a, b) in enumerate(stores)]
    for copy in stores[:-3]:
        copy.start()
    for plane in range(2):
        for q, high in ((0, True), (last, False)):
            side = 0 if high else 1
            corners[side, plane] = pack(grad[plane, q, pl.ds(0, RIM), :], high)
            corners[2 + side, plane] = pack(grad[plane, q, pl.ds(low, RIM), :], high)
            sides[side, plane] = pack(grad[plane, q, pl.ds(RIM, rows), :], high)
    for copy in stores[-3:]:
        copy.start()
    for copy in stores:
        copy.wait()


def tile_gradient(places, numbers, probe, tile, halo, measured, patches, part):
    planes, rows, cols = tile.shape
    tiles = cols // WIN
    f32 = jnp.float32
    smem = pl.BlockSpec(memory_space=pltpu.SMEM)
    vmem = pl.BlockSpec(memory_space=pltpu.VMEM)
    hbm = pl.BlockSpec(memory_space=pl.ANY)
    extent = (planes, tiles + 2, rows + WIN, WIN)
    copies = 3 * tiles + 3
    return pl.pallas_call(
        body,
        out_shape=(
            jax.ShapeDtypeStruct(tile.shape, f32),
            *(jax.ShapeDtypeStruct(h.shape, f32) for h in halo),
            jax.ShapeDtypeStruct(probe.shape, f32),
        ),
        in_specs=[smem, smem, vmem, vmem] + [hbm] * 8 + [vmem],
        out_specs=(*[hbm] * 6, vmem),
        scratch_shapes=[
            pltpu.VMEM(extent, f32),
            pltpu.VMEM(extent, f32),
            pltpu.VMEM((AHEAD, WIN, WIN), f32),
            pltpu.VMEM((2, planes, rows // 2, WIN), f32),
            pltpu.VMEM((4, planes, RIM // 2, WIN), f32),
            pltpu.VMEM(patches.shape, f32),
            pltpu.SemaphoreType.DMA((copies,)),
            pltpu.SemaphoreType.DMA((AHEAD,)),
            pltpu.SemaphoreType.DMA((patches.shape[0] // U,)),
        ],
        compiler_params=pltpu.CompilerParams(vmem_limit_bytes=56 * 1024 * 1024),
        name="tile_gradient",
    )(places, numbers, probe, jnp.asarray(matrices()), tile, *halo, measured, patches, part)


AROUND = ((-1, 0), (1, 0), (0, -1), (0, 1), (-1, -1), (-1, 1), (1, -1), (1, 1))


def ring(axis, by):
    size = lax.axis_size(axis)
    return lax.rem(lax.axis_index(axis) + (by + size), size)


def around(dy, dx):
    return {"ty": ring("ty", dy), "tx": ring("tx", dx)}


def greet(partners):
    barrier = pltpu.get_barrier_semaphore()
    for partner in partners:
        pl.semaphore_signal(barrier, inc=1, device_id=partner, device_id_type=MESH)


def inner_patches(
    begin, place_ref, live_ref, probe_ref, w_ref, obj, held, patches, patch_out, patch_sems, add
):
    size = patches.shape[1]

    def store(group):
        turn = lax.rem(group, 2)
        return pltpu.make_async_copy(patches.at[turn], patch_out.at[pl.ds(group * size, size)], patch_sems.at[turn])

    groups = patch_out.shape[0] // size

    @pl.loop(0, groups)
    def _(group):
        turn = lax.rem(group, 2)

        @pl.when(group >= 2)
        def _():
            store(group - 2).wait()

        places = [begin + group * size + u for u in range(size)]

        def start(u):
            p = places[u]
            window = take(obj, place_ref[3, p], place_ref[4, p], place_ref[5, p], place_ref[6, p])
            return slot_steps(window, probe_ref, held[place_ref[0, p]], live_ref[p], w_ref)

        def finish(u, grad_re, grad_im, terms):
            patches[turn, u, 0] = grad_re
            patches[turn, u, 1] = grad_im
            for i, term in enumerate(terms):
                add(i, term)

        pipelined(start, finish, size)
        store(group).start()

    for group in range(max(groups - 2, 0), groups):
        store(group).wait()


def halo_body(
    place_ref, live_ref, probe_ref, w_ref, tile_ref, measured_ref,
    left_out, right_out, top_out, bottom_out, corner_out, patch_out, part_out,
    obj, held, packed, corners, patches, in_sems, held_sem, send_sems, recv_sems, patch_sems,
):
    rows, cols = tile_ref.shape[1:]
    tiles = cols // WIN
    greet([around(*step) for step in AROUND])
    loads = [
        pltpu.make_async_copy(tile_ref.at[:, :, pl.ds(q * WIN, WIN)], obj.at[:, q], in_sems.at[q])
        for q in range(tiles)
    ]
    for q in (0, tiles - 1, *range(1, tiles - 1)):
        loads[q].start()
    measures = pltpu.make_async_copy(measured_ref, held, held_sem)
    measures.start()
    part_out[...] = jnp.zeros_like(part_out)
    above, below = pl.ds(0, RIM), pl.ds(rows - RIM, RIM)
    for side, q in enumerate((0, tiles - 1)):
        loads[q].wait()
        for plane in range(2):
            packed[side, plane] = pack(obj[plane, q], side == 1)
            corners[side, plane] = pack(obj[plane, q, above, :], side == 1)
            corners[2 + side, plane] = pack(obj[plane, q, below, :], side == 1)
    pl.semaphore_wait(pltpu.get_barrier_semaphore(), len(AROUND))
    moves = (
        (packed.at[0], right_out, (0, -1)),
        (packed.at[1], left_out, (0, 1)),
        (tile_ref.at[:, above, :], bottom_out, (-1, 0)),
        (tile_ref.at[:, below, :], top_out, (1, 0)),
        (corners.at[3], corner_out.at[0], (1, 1)),
        (corners.at[2], corner_out.at[1], (1, -1)),
        (corners.at[1], corner_out.at[2], (-1, 1)),
        (corners.at[0], corner_out.at[3], (-1, -1)),
    )
    halo = send(moves, send_sems, recv_sems)
    for q in range(1, tiles - 1):
        loads[q].wait()
    measures.wait()

    def add(i, term):
        part_out[i // 2, i % 2] += term

    inner_patches(0, place_ref, live_ref, probe_ref, w_ref, obj, held, patches, patch_out, patch_sems, add)
    for copy in halo:
        copy.wait()


def send(moves, send_sems, recv_sems, begin=True):
    copies = [
        pltpu.make_async_remote_copy(
            src_ref=source,
            dst_ref=target,
            send_sem=send_sems.at[i],
            recv_sem=recv_sems.at[i],
            device_id=around(*step),
            device_id_type=MESH,
        )
        for i, (source, target, step) in enumerate(moves)
    ]
    if begin:
        for copy in copies:
            copy.start()
    return copies


def halo_shapes(tile):
    planes, rows, cols = tile.shape
    shapes = [(planes, rows // 2, WIN)] * 2 + [(planes, RIM, cols)] * 2 + [(4, planes, RIM // 2, WIN)]
    return tuple(jax.ShapeDtypeStruct(s, jnp.float32) for s in shapes)


def gather_halo(places, live, probe, tile, measured):
    planes, rows, cols = tile.shape
    hbm = pl.BlockSpec(memory_space=pl.ANY)
    smem = pl.BlockSpec(memory_space=pltpu.SMEM)
    vmem = pl.BlockSpec(memory_space=pltpu.VMEM)
    f32 = jnp.float32
    return pl.pallas_call(
        halo_body,
        out_shape=(
            *halo_shapes(tile),
            jax.ShapeDtypeStruct((EARLY, planes, WIN, WIN), f32),
            jax.ShapeDtypeStruct(probe.shape, f32),
        ),
        in_specs=[smem, smem, vmem, vmem, hbm, hbm],
        out_specs=(*[hbm] * 6, vmem),
        scratch_shapes=[
            pltpu.VMEM((planes, cols // WIN, rows, WIN), f32),
            pltpu.VMEM(measured.shape, f32),
            pltpu.VMEM((2, planes, rows // 2, WIN), f32),
            pltpu.VMEM((4, planes, RIM // 2, WIN), f32),
            pltpu.VMEM((2, WIDE, planes, WIN, WIN), f32),
            pltpu.SemaphoreType.DMA((cols // WIN,)),
            pltpu.SemaphoreType.DMA,
            pltpu.SemaphoreType.DMA((8,)),
            pltpu.SemaphoreType.DMA((8,)),
            pltpu.SemaphoreType.DMA((2,)),
        ],
        compiler_params=pltpu.CompilerParams(
            collective_id=0, has_side_effects=True, vmem_limit_bytes=56 * 1024 * 1024
        ),
        name="gather_halo",
    )(places, live, probe, jnp.asarray(matrices()), tile, measured)


def ordered(positions, count, rows, cols):
    slots = positions.shape[0]
    row = positions[:, 0] - lax.axis_index("ty") * rows
    col = positions[:, 1] - lax.axis_index("tx") * cols
    slot = jnp.arange(slots, dtype=jnp.int32)
    inside = (row >= 0) & (row <= rows - WIN) & (col >= 0) & (col <= cols - WIN)
    key = jnp.where(slot < count, jnp.where(inside, 0, 1), 2) * slots + slot
    rank = jnp.sum((key[None, :] < key[:, None]).astype(jnp.int32), axis=1)
    safe_row = jnp.clip(row, 0, rows - WIN)
    safe_col = jnp.clip(col, 0, cols - WIN)
    q = safe_col // WIN
    table = jnp.stack(
        [slot, row + RIM, col + WIN, safe_row, q, jnp.minimum(q + 1, cols // WIN - 1), safe_col % WIN, slot * 0]
    )
    hit = rank[None, :] == slot[:, None]
    table = jnp.sum(jnp.where(hit[None], table[:, None, :], 0), axis=2)
    inner = jnp.sum((inside & (slot < count)).astype(jnp.int32))
    live = (slot < inner).astype(jnp.float32)
    early = jnp.minimum(inner, EARLY)
    done = jnp.minimum(inner, EARLY + LATE)
    return table, live, jnp.stack([done, count, early, done - early])


def tail_body(
    place_ref, live_ref, probe_ref, w_ref, tile_ref, measured_ref,
    left_ref, right_ref, top_ref, bottom_ref, corner_ref, start_ref,
    left_out, right_out, top_out, bottom_out, corner_out, patch_out, total_out,
    obj, held, patches, part_ref, gathered, stage, in_sems, held_sem, patch_sems,
    send_sems, recv_sems, tx_send, tx_recv, ty_send, ty_recv, out_send, out_recv,
):
    ty, tx = lax.axis_index("ty"), lax.axis_index("tx")
    ny, nx = lax.axis_size("ty"), lax.axis_size("tx")
    diagonal = [around(*step) for step in AROUND if 0 not in step]
    greet(diagonal)
    barrier = pltpu.get_barrier_semaphore()

    @pl.loop(1, nx)
    def _(k):
        pl.semaphore_signal(barrier, inc=1, device_id={"tx": lax.rem(tx + k, nx)}, device_id_type=MESH)

    @pl.loop(1, ny)
    def _(k):
        pl.semaphore_signal(barrier, inc=1, device_id={"ty": lax.rem(ty + k, ny)}, device_id_type=MESH)

    tiles = tile_ref.shape[2] // WIN
    loads = [
        pltpu.make_async_copy(tile_ref.at[:, :, pl.ds(q * WIN, WIN)], obj.at[:, q], in_sems.at[q])
        for q in range(tiles)
    ]
    loads.append(pltpu.make_async_copy(measured_ref, held, held_sem))
    for copy in loads:
        copy.start()
    part_ref[...] = start_ref[...]
    pl.semaphore_wait(barrier, len(diagonal) + nx - 1 + ny - 1)

    def to_column(k, source, target, sends, receives):
        return pltpu.make_async_remote_copy(
            src_ref=source,
            dst_ref=target,
            send_sem=sends.at[k],
            recv_sem=receives.at[tx],
            device_id={"tx": lax.rem(tx + k, nx)},
            device_id_type=MESH,
        )

    def to_row(k):
        return pltpu.make_async_remote_copy(
            src_ref=stage.at[ty],
            dst_ref=stage.at[ty],
            send_sem=ty_send.at[k],
            recv_sem=ty_recv.at[ty],
            device_id={"ty": lax.rem(ty + k, ny)},
            device_id_type=MESH,
        )

    def arrived(target, semaphore):
        pltpu.make_async_copy(target, target, semaphore).wait()

    def spread(k):
        return to_column(k, part_ref.at[lax.rem(tx + k, nx)], gathered.at[tx], tx_send, tx_recv)

    def share(k):
        return to_column(k, total_out.at[tx], total_out.at[tx], out_send, out_recv)

    moves = (
        (left_ref, right_out, (0, -1)),
        (right_ref, left_out, (0, 1)),
        (top_ref, bottom_out, (-1, 0)),
        (bottom_ref, top_out, (1, 0)),
        (corner_ref.at[0], corner_out.at[3], (-1, -1)),
        (corner_ref.at[1], corner_out.at[2], (-1, 1)),
        (corner_ref.at[2], corner_out.at[1], (1, -1)),
        (corner_ref.at[3], corner_out.at[0], (1, 1)),
    )
    halo = send(moves, send_sems, recv_sems, begin=False)
    for copy in halo[:2]:
        copy.start()
    for copy in loads:
        copy.wait()

    def add(i, term):
        each = part_ref.shape[0] // 4
        part_ref[pl.ds(i * each, each)] += term.reshape(each, WIN // each, WIN)

    inner_patches(EARLY, place_ref, live_ref, probe_ref, w_ref, obj, held, patches, patch_out, patch_sems, add)

    @pl.loop(1, nx)
    def _(k):
        spread(k).start()

    for copy in (halo[2], *halo[4:6]):
        copy.start()
    stage[ty] = part_ref[tx]

    @pl.loop(1, nx)
    def _(k):
        source = lax.rem(tx + k, nx)
        arrived(gathered.at[source], tx_recv.at[source])
        stage[ty] += gathered[source]

    @pl.loop(1, ny)
    def _(k):
        to_row(k).start()

    for copy in (halo[3], *halo[6:]):
        copy.start()

    @pl.loop(1, ny)
    def _(k):
        source = lax.rem(ty + k, ny)
        arrived(stage.at[source], ty_recv.at[source])

    total = stage[0]
    for i in range(1, stage.shape[0]):
        total += stage[i]
    total_out[tx] = total * (1.0 / SLOTS_ALL)

    @pl.loop(1, nx)
    def _(k):
        share(k).start()

    @pl.loop(1, nx)
    def _(k):
        source = lax.rem(tx + k, nx)
        arrived(total_out.at[source], out_recv.at[source])

    for copy in halo:
        copy.wait()

    @pl.loop(1, nx)
    def _(k):
        spread(k).wait_send()
        share(k).wait_send()

    @pl.loop(1, ny)
    def _(k):
        to_row(k).wait_send()


def exchange(places, live, probe, tile, measured, halo, part):
    hbm = pl.BlockSpec(memory_space=pl.ANY)
    vmem = pl.BlockSpec(memory_space=pltpu.VMEM)
    smem = pl.BlockSpec(memory_space=pltpu.SMEM)
    planes, rows, cols = tile.shape
    ny, nx = lax.axis_size("ty"), lax.axis_size("tx")
    chunk = (part.size // (nx * WIN), WIN)
    return pl.pallas_call(
        tail_body,
        out_shape=(
            *(jax.ShapeDtypeStruct(h.shape, jnp.float32) for h in halo),
            jax.ShapeDtypeStruct((LATE, planes, WIN, WIN), jnp.float32),
            jax.ShapeDtypeStruct((nx, *chunk), jnp.float32),
        ),
        in_specs=[smem, smem, vmem, vmem] + [hbm] * 7 + [vmem],
        out_specs=(*[hbm] * 6, vmem),
        scratch_shapes=[
            pltpu.VMEM((planes, cols // WIN, rows, WIN), jnp.float32),
            pltpu.VMEM(measured.shape, jnp.float32),
            pltpu.VMEM((2, WIDE, planes, WIN, WIN), jnp.float32),
            pltpu.VMEM((nx, *chunk), jnp.float32),
            pltpu.VMEM((nx, *chunk), jnp.float32),
            pltpu.VMEM((ny, *chunk), jnp.float32),
            pltpu.SemaphoreType.DMA((cols // WIN,)),
            pltpu.SemaphoreType.DMA,
            pltpu.SemaphoreType.DMA((2,)),
            pltpu.SemaphoreType.DMA((8,)),
            pltpu.SemaphoreType.DMA((8,)),
            pltpu.SemaphoreType.DMA((nx,)),
            pltpu.SemaphoreType.DMA((nx,)),
            pltpu.SemaphoreType.DMA((ny,)),
            pltpu.SemaphoreType.DMA((ny,)),
            pltpu.SemaphoreType.DMA((nx,)),
            pltpu.SemaphoreType.DMA((nx,)),
        ],
        compiler_params=pltpu.CompilerParams(
            collective_id=1, has_side_effects=True, vmem_limit_bytes=56 * 1024 * 1024
        ),
        name="exchange",
    )(places, live, probe, jnp.asarray(matrices()), tile, measured, *halo, part.reshape(nx, *chunk))


def finish_body(
    place_ref, number_ref, tile_ref, left_ref, right_ref, top_ref, bottom_ref, corner_ref, patch_ref, total_ref,
    out_ref, total_out, grad, sides, rims, corners, patches, in_sems, more_sems,
):
    planes, rows, cols = tile_ref.shape
    tiles = cols // WIN
    ty, tx = lax.axis_index("ty"), lax.axis_index("tx")
    ny, nx = lax.axis_size("ty"), lax.axis_size("tx")
    late = number_ref[3]
    spans = [pl.ds(q * WIN, WIN) for q in range(tiles)]
    more = (
        (patch_ref, patches),
        (left_ref, sides.at[0]),
        (right_ref, sides.at[1]),
        (top_ref, rims.at[0]),
        (bottom_ref, rims.at[1]),
        (corner_ref, corners),
    )
    more = [pltpu.make_async_copy(a, b, more_sems.at[i]) for i, (a, b) in enumerate(more)]
    reads = [
        pltpu.make_async_copy(tile_ref.at[:, :, span], grad.at[:, q], in_sems.at[q]) for q, span in enumerate(spans)
    ]
    for copy in reads + more:
        copy.start()
    total_out[...] = total_ref[...]
    no_side = (tx == 0, tx == nx - 1)
    no_end = (ty == 0, ty == ny - 1)
    ends = (0, rows - RIM)
    for copy in (*reads, more[0]):
        copy.wait()

    def info_of(place):
        at = EARLY + place
        return place_ref[3, at], place_ref[4, at], place_ref[6, at], place_ref[5, at]

    for first in range(0, patches.shape[0], U):
        deposit(grad, patches, info_of, first, late)

    for copy in more[1:]:
        copy.wait()

    def side_add(plane, side, start, packed, gone):
        high = side == 1
        half = packed.shape[0]
        far = lax.broadcasted_iota(jnp.int32, packed.shape, 1) >= RIM
        mine = far if high else jnp.logical_not(far)
        for i, value in enumerate(unpack(packed, high)):
            here = pl.ds(start + i * half, half)
            value = jnp.where(gone, 0.0, value)
            grad[plane, side * (tiles - 1), here, :] += jnp.where(mine, value, 0.0)

    for plane in range(2):
        for side in range(2):
            side_add(plane, side, 0, sides[side, plane], no_side[side])
            for end in range(2):
                gone = jnp.logical_or(no_side[side], no_end[end])
                side_add(plane, side, ends[end], corners[2 * end + side, plane], gone)
        for end in range(2):
            for q in range(tiles):
                value = jnp.where(no_end[end], 0.0, rims[end, plane, :, spans[q]])
                grad[plane, q, pl.ds(ends[end], RIM), :] += value
    writes = [
        pltpu.make_async_copy(grad.at[:, q], out_ref.at[:, :, span], in_sems.at[q]) for q, span in enumerate(spans)
    ]
    for copy in writes:
        copy.start()
    for copy in writes:
        copy.wait()


def finish(places, numbers, tile, halo, patches, total):
    planes, rows, cols = tile.shape
    hbm = pl.BlockSpec(memory_space=pl.ANY)
    vmem = pl.BlockSpec(memory_space=pltpu.VMEM)
    smem = pl.BlockSpec(memory_space=pltpu.SMEM)
    f32 = jnp.float32
    return pl.pallas_call(
        finish_body,
        out_shape=(jax.ShapeDtypeStruct(tile.shape, f32), jax.ShapeDtypeStruct(total.shape, f32)),
        in_specs=[smem, smem] + [hbm] * 7 + [vmem],
        out_specs=(hbm, vmem),
        scratch_shapes=[
            pltpu.VMEM((planes, cols // WIN, rows, WIN), f32),
            pltpu.VMEM((2, planes, rows // 2, WIN), f32),
            pltpu.VMEM((2, planes, RIM, cols), f32),
            pltpu.VMEM((4, planes, RIM // 2, WIN), f32),
            pltpu.VMEM(patches.shape, f32),
            pltpu.SemaphoreType.DMA((cols // WIN,)),
            pltpu.SemaphoreType.DMA((6,)),
        ],
        compiler_params=pltpu.CompilerParams(vmem_limit_bytes=56 * 1024 * 1024),
        name="finish",
    )(places, numbers, tile, *halo, patches, total)


def shards(object_planes, probe, positions, counts, amplitudes):
    planes, rows, cols = object_planes.shape
    places, live, numbers = ordered(positions[0, 0], counts[0, 0], rows, cols)
    measured = amplitudes[0, 0]
    *halo, patches, early_part = gather_halo(places, live, probe, object_planes, measured)
    tile, *outer, part = tile_gradient(places, numbers, probe, object_planes, halo, measured, patches, early_part)
    *outer, patches, total = exchange(places, live, probe, object_planes, measured, outer, part)
    tile, total = finish(places, numbers, tile, outer, patches, total)
    return tile, total.reshape(probe.shape)


def solution(mesh):
    in_specs = (
        P(None, "ty", "tx"),
        P(),
        P("ty", "tx", None, None),
        P("ty", "tx"),
        P("ty", "tx", None, None, None),
    )
    out_specs = (P(None, "ty", "tx"), P())
    return jax.shard_map(shards, mesh=mesh, in_specs=in_specs, out_specs=out_specs, check_vma=False)
```

```python
import math

import jax
import jax.numpy as jnp
import numpy as np
from jax import lax
from jax.experimental import pallas as pl
from jax.experimental.pallas import tpu as pltpu
from jax.sharding import PartitionSpec as P

WIN = 128
RIM = WIN // 2
FLOOR = 0.25
AHEAD = 16
MESH = pl.DeviceIdType.MESH
SLOTS_ALL = 8 * 16 * 96
U = 8
SMALL = 4
WIDE = 16
STAGES = 7
SLOTS = 96
EARLY = 48
LATE = 16


def matrices():
    index = np.arange(WIN)
    angle = 2.0 * math.pi / WIN * ((index[:, None] * index[None, :]) % WIN)
    cosine = np.cos(angle) / math.sqrt(WIN)
    sine = np.sin(angle) / math.sqrt(WIN)
    right = np.block([[cosine, -sine], [sine, cosine]])
    both = np.stack([right, right.T]).astype(np.float32)
    high = both.astype(jnp.bfloat16)
    low = (both - high.astype(np.float32)).astype(jnp.bfloat16)
    return np.stack([high, low], axis=1)


def split(value):
    high = value.astype(jnp.bfloat16)
    low = (value - high.astype(jnp.float32)).astype(jnp.bfloat16)
    return high, low


def dot(a, b):
    return lax.dot_general(a, b, (((1,), (0,)), ((), ())), preferred_element_type=jnp.float32)


def blocks(value):
    n = WIN
    return value[:n, :n], value[:n, n:], value[n:, :n], value[n:, n:]


def assemble(a, b, c, d):
    top = jnp.concatenate([a, b], axis=1)
    bottom = jnp.concatenate([c, d], axis=1)
    return jnp.concatenate([top, bottom], axis=0)


def right_product(value, w_ref, k):
    high, low = split(value)
    return dot(high, w_ref[k, 0]) + dot(low, w_ref[k, 0]) + dot(high, w_ref[k, 1])


def left_product(value, w_ref, k):
    high, low = split(value)
    return dot(w_ref[k, 0], high) + dot(w_ref[k, 0], low) + dot(w_ref[k, 1], high)


def slot_steps(window, probe_ref, measured, live, w_ref):
    a, b = window
    p0r, p0i = probe_ref[0, 0], probe_ref[0, 1]
    p1r, p1i = probe_ref[1, 0], probe_ref[1, 1]
    wave = assemble(
        p0r * a - p0i * b,
        p0r * b + p0i * a,
        p1r * a - p1i * b,
        p1r * b + p1i * a,
    )
    yield
    half = right_product(wave, w_ref, 0)
    yield
    m0r, m0i, m1r, m1i = blocks(half)
    far = left_product(assemble(m0r, m1r, m0i, m1i), w_ref, 1)
    yield
    f0r, f1r, f0i, f1i = blocks(far)
    intensity = f0r * f0r + f0i * f0i + (f1r * f1r + f1i * f1i)
    weight = live - (live * measured) * lax.rsqrt(jnp.maximum(intensity, FLOOR))
    value = assemble(weight * f0r, weight * f1r, weight * f0i, weight * f1i)
    yield
    half = left_product(value, w_ref, 0)
    yield
    m0r, m1r, m0i, m1i = blocks(half)
    back = right_product(assemble(m0r, m0i, m1r, m1i), w_ref, 1)
    yield
    b0r, b0i, b1r, b1i = blocks(back)
    grad_re = p0r * b0r + p0i * b0i + (p1r * b1r + p1i * b1i)
    grad_im = p0r * b0i - p0i * b0r + (p1r * b1i - p1i * b1r)
    yield grad_re, grad_im, (a * b0r + b * b0i, a * b0i - b * b0r, a * b1r + b * b1i, a * b1i - b * b1r)


def pipelined(start, finish, size):
    runs = [None] * size
    for moment in range(STAGES + size - 1):
        for u in reversed(range(size)):
            stage = moment - u
            if 0 <= stage < STAGES:
                if stage == 0:
                    runs[u] = start(u)
                result = next(runs[u])
                if stage == STAGES - 1:
                    finish(u, *result)


def take(obj, row, q, q_next, shift):
    here = pl.ds(row, WIN)
    keep = lax.broadcasted_iota(jnp.int32, (WIN, WIN), 1) < WIN - shift
    window = []
    for plane in range(2):
        first = pltpu.roll(obj[plane, q, here, :], WIN - shift, 1)
        second = pltpu.roll(obj[plane, q_next, here, :], WIN - shift, 1)
        window.append(jnp.where(keep, first, second))
    return window


def put(grad, row, q, shift, values, q_next=None):
    here = pl.ds(row, WIN)
    after = lax.broadcasted_iota(jnp.int32, (WIN, WIN), 1) >= shift
    q_next = q + 1 if q_next is None else q_next
    for plane, value in enumerate(values):
        turned = pltpu.roll(value, shift, 1)
        grad[plane, q, here, :] += jnp.where(after, turned, 0.0)
        grad[plane, q_next, here, :] += jnp.where(after, 0.0, turned)


def pack(value, high):
    half = value.shape[0] // 2
    first, second = value[:half], value[half:]
    near = lax.broadcasted_iota(jnp.int32, first.shape, 1) < RIM
    if high:
        first = pltpu.roll(first, RIM, 1)
    else:
        second = pltpu.roll(second, RIM, 1)
    return jnp.where(near, first, second)


def unpack(packed, high):
    turned = pltpu.roll(packed, RIM, 1)
    return (turned, packed) if high else (packed, turned)


def deposit(grad, patches, info_of, first, end):
    for u in range(U):
        @pl.when(first + u < end)
        def _(place=first + u):
            row, q, shift, q_next = info_of(place)
            put(grad, row, q, shift, (patches[place, 0], patches[place, 1]), q_next)


def body(
    place_ref, probe_ref, w_ref, tile_ref, left_ref, right_ref, top_ref, bottom_ref, corner_ref,
    measured_ref, patch_ref, part_ref,
    grad_tile, grad_left, grad_right, grad_top, grad_bottom, grad_corner, probe_out,
    obj, grad, held, sides, corners, patches, in_sems, held_sems, patch_sems,
):
    rows = tile_ref.shape[1]
    cols = tile_ref.shape[2]
    tiles = cols // WIN
    slots_max = measured_ref.shape[0]
    begin, count, early = (place_ref[7, slots_max + i] for i in range(3))

    def fetch(place):
        turn = lax.rem(place - begin, AHEAD)
        return pltpu.make_async_copy(measured_ref.at[place_ref[0, place]], held.at[turn], held_sems.at[turn])

    for ahead in range(AHEAD):
        @pl.when(begin + ahead < count)
        def _(ahead=ahead):
            fetch(begin + ahead).start()

    last = tiles + 1
    low = RIM + rows
    middle = RIM + rows // 2
    loads = []
    for q in range(tiles):
        span = pl.ds(q * WIN, WIN)
        loads.append((tile_ref.at[:, :, span], obj.at[:, q + 1, pl.ds(RIM, rows), :]))
        loads.append((top_ref.at[:, :, span], obj.at[:, q + 1, pl.ds(0, RIM), :]))
        loads.append((bottom_ref.at[:, :, span], obj.at[:, q + 1, pl.ds(low, RIM), :]))
    loads.append((corner_ref, corners))
    loads.append((left_ref, sides.at[0]))
    loads.append((right_ref, sides.at[1]))
    loads = [pltpu.make_async_copy(a, b, in_sems.at[i]) for i, (a, b) in enumerate(loads)]
    pieces = patch_ref.shape[0] // U
    chunks = [
        pltpu.make_async_copy(patch_ref.at[pl.ds(i * U, U)], patches.at[pl.ds(i * U, U)], patch_sems.at[i])
        for i in range(pieces)
    ]
    for copy in chunks[:2] + loads + chunks[2:]:
        copy.start()
    grad[...] = jnp.zeros_like(grad)
    probe_out[...] = part_ref[...]

    def info_of(place):
        safe = jnp.minimum(place, slots_max - 1)
        row, col = place_ref[1, safe], place_ref[2, safe]
        return row, col // WIN, lax.rem(col, WIN), col // WIN + 1

    for i, copy in enumerate(chunks):
        copy.wait()
        deposit(grad, patches, info_of, i * U, early)
    for copy in loads:
        copy.wait()
    for plane in range(2):
        for q, high in ((0, True), (last, False)):
            side = 0 if high else 1
            pieces = ((corners[side, plane], 0), (sides[side, plane], RIM), (corners[2 + side, plane], low))
            for packed, start in pieces:
                half = packed.shape[0]
                for i, value in enumerate(unpack(packed, high)):
                    obj[plane, q, pl.ds(start + i * half, half), :] = value
    ty, tx = lax.axis_index("ty"), lax.axis_index("tx")

    @pl.when(ty == 0)
    def _():
        obj[:, :, pl.ds(0, RIM), :] = jnp.zeros((2, tiles + 2, RIM, WIN), jnp.float32)

    @pl.when(ty == lax.axis_size("ty") - 1)
    def _():
        obj[:, :, pl.ds(low, RIM), :] = jnp.zeros((2, tiles + 2, RIM, WIN), jnp.float32)

    @pl.when(tx == 0)
    def _():
        obj[:, 0] = jnp.zeros((2, rows + WIN, WIN), jnp.float32)

    @pl.when(tx == lax.axis_size("tx") - 1)
    def _():
        obj[:, last] = jnp.zeros((2, rows + WIN, WIN), jnp.float32)


    def run(first, size):
        places = [first + u for u in range(size)]
        for place in places:
            @pl.when(place < count)
            def _(place=place):
                fetch(place).wait()
        terms = []

        def start(u):
            row, q, shift, q_next = info_of(places[u])
            window = take(obj, row, q, q_next, shift)
            live = jnp.where(places[u] < count, 1.0, 0.0)
            return slot_steps(window, probe_ref, held[lax.rem(places[u] - begin, AHEAD)], live, w_ref)

        def finish(u, grad_re, grad_im, term):
            row, q, shift, q_next = info_of(places[u])
            put(grad, row, q, shift, (grad_re, grad_im), q_next)
            terms.append(term)

        pipelined(start, finish, size)
        for i in range(4):
            probe_out[i // 2, i % 2] += sum(term[i] for term in terms)
        for place in places:
            @pl.when(place + AHEAD < count)
            def _(place=place):
                fetch(place + AHEAD).start()

    rest = count - begin
    whole = (rest + SMALL - 1) // U

    @pl.loop(0, whole)
    def _(group):
        run(begin + group * U, U)

    @pl.when(rest > whole * U)
    def _():
        run(begin + whole * U, SMALL)

    stores = []
    for q in range(tiles):
        span = pl.ds(q * WIN, WIN)
        stores.append((grad.at[:, q + 1, pl.ds(RIM, rows), :], grad_tile.at[:, :, span]))
        stores.append((grad.at[:, q + 1, pl.ds(0, RIM), :], grad_top.at[:, :, span]))
        stores.append((grad.at[:, q + 1, pl.ds(low, RIM), :], grad_bottom.at[:, :, span]))
    stores.append((corners, grad_corner))
    stores.append((sides.at[0], grad_left))
    stores.append((sides.at[1], grad_right))
    stores = [pltpu.make_async_copy(a, b, in_sems.at[i]) for i, (a, b) in enumerate(stores)]
    for copy in stores[:-3]:
        copy.start()
    for plane in range(2):
        for q, high in ((0, True), (last, False)):
            side = 0 if high else 1
            corners[side, plane] = pack(grad[plane, q, pl.ds(0, RIM), :], high)
            corners[2 + side, plane] = pack(grad[plane, q, pl.ds(low, RIM), :], high)
            sides[side, plane] = pack(grad[plane, q, pl.ds(RIM, rows), :], high)
    for copy in stores[-3:]:
        copy.start()
    for copy in stores:
        copy.wait()


def tile_gradient(places, probe, tile, halo, measured, patches, part):
    planes, rows, cols = tile.shape
    tiles = cols // WIN
    f32 = jnp.float32
    smem = pl.BlockSpec(memory_space=pltpu.SMEM)
    vmem = pl.BlockSpec(memory_space=pltpu.VMEM)
    hbm = pl.BlockSpec(memory_space=pl.ANY)
    extent = (planes, tiles + 2, rows + WIN, WIN)
    copies = 3 * tiles + 3
    return pl.pallas_call(
        body,
        out_shape=(
            jax.ShapeDtypeStruct(tile.shape, f32),
            *(jax.ShapeDtypeStruct(h.shape, f32) for h in halo),
            jax.ShapeDtypeStruct(probe.shape, f32),
        ),
        in_specs=[smem, vmem, vmem] + [hbm] * 8 + [vmem],
        out_specs=(*[hbm] * 6, vmem),
        scratch_shapes=[
            pltpu.VMEM(extent, f32),
            pltpu.VMEM(extent, f32),
            pltpu.VMEM((AHEAD, WIN, WIN), f32),
            pltpu.VMEM((2, planes, rows // 2, WIN), f32),
            pltpu.VMEM((4, planes, RIM // 2, WIN), f32),
            pltpu.VMEM(patches.shape, f32),
            pltpu.SemaphoreType.DMA((copies,)),
            pltpu.SemaphoreType.DMA((AHEAD,)),
            pltpu.SemaphoreType.DMA((patches.shape[0] // U,)),
        ],
        compiler_params=pltpu.CompilerParams(vmem_limit_bytes=56 * 1024 * 1024),
        name="tile_gradient",
    )(places, probe, jnp.asarray(matrices()), tile, *halo, measured, patches, part)


AROUND = ((-1, 0), (1, 0), (0, -1), (0, 1), (-1, -1), (-1, 1), (1, -1), (1, 1))


def ring(axis, by):
    size = lax.axis_size(axis)
    return lax.rem(lax.axis_index(axis) + (by + size), size)


def around(dy, dx):
    return {"ty": ring("ty", dy), "tx": ring("tx", dx)}


def greet(partners):
    barrier = pltpu.get_barrier_semaphore()
    for partner in partners:
        pl.semaphore_signal(barrier, inc=1, device_id=partner, device_id_type=MESH)


def inner_patches(
    begin, place_ref, probe_ref, w_ref, obj, held, patches, patch_out, patch_sems, add
):
    size = patches.shape[1]

    def store(group):
        turn = lax.rem(group, 2)
        return pltpu.make_async_copy(patches.at[turn], patch_out.at[pl.ds(group * size, size)], patch_sems.at[turn])

    groups = patch_out.shape[0] // size

    @pl.loop(0, groups)
    def _(group):
        turn = lax.rem(group, 2)

        @pl.when(group >= 2)
        def _():
            store(group - 2).wait()

        places = [begin + group * size + u for u in range(size)]

        def start(u):
            p = places[u]
            window = take(obj, place_ref[3, p], place_ref[4, p], place_ref[5, p], place_ref[6, p])
            return slot_steps(window, probe_ref, held[place_ref[0, p]], place_ref[7, p].astype(jnp.float32), w_ref)

        def finish(u, grad_re, grad_im, terms):
            patches[turn, u, 0] = grad_re
            patches[turn, u, 1] = grad_im
            for i, term in enumerate(terms):
                add(i, term)

        pipelined(start, finish, size)
        store(group).start()

    for group in range(max(groups - 2, 0), groups):
        store(group).wait()


def halo_body(
    count_ref, position_ref, probe_ref, w_ref, tile_ref, measured_ref,
    left_out, right_out, top_out, bottom_out, corner_out, patch_out, part_out, table_out,
    table, place_ref, table_sems, obj, held, packed, corners, patches, in_sems, held_sem, send_sems, recv_sems, patch_sems,
):
    rows, cols = tile_ref.shape[1:]
    tiles = cols // WIN
    greet([around(*step) for step in AROUND])
    loads = [
        pltpu.make_async_copy(tile_ref.at[:, :, pl.ds(q * WIN, WIN)], obj.at[:, q], in_sems.at[q])
        for q in range(tiles)
    ]
    for q in (0, tiles - 1, *range(1, tiles - 1)):
        loads[q].start()
    measures = pltpu.make_async_copy(measured_ref, held, held_sem)
    measures.start()
    part_out[...] = jnp.zeros_like(part_out)
    above, below = pl.ds(0, RIM), pl.ds(rows - RIM, RIM)
    for side, q in enumerate((0, tiles - 1)):
        loads[q].wait()
        for plane in range(2):
            packed[side, plane] = pack(obj[plane, q], side == 1)
            corners[side, plane] = pack(obj[plane, q, above, :], side == 1)
            corners[2 + side, plane] = pack(obj[plane, q, below, :], side == 1)
    pl.semaphore_wait(pltpu.get_barrier_semaphore(), len(AROUND))
    moves = (
        (packed.at[0], right_out, (0, -1)),
        (packed.at[1], left_out, (0, 1)),
        (tile_ref.at[:, above, :], bottom_out, (-1, 0)),
        (tile_ref.at[:, below, :], top_out, (1, 0)),
        (corners.at[3], corner_out.at[0], (1, 1)),
        (corners.at[2], corner_out.at[1], (1, -1)),
        (corners.at[1], corner_out.at[2], (-1, 1)),
        (corners.at[0], corner_out.at[3], (-1, -1)),
    )
    halo = send(moves, send_sems, recv_sems)
    table[...] = ordered(position_ref[...], count_ref[0, 0], rows, cols)
    keep = pltpu.make_async_copy(table, table_out, table_sems.at[0])
    keep.start()
    scalars = pltpu.make_async_copy(table, place_ref, table_sems.at[1])
    scalars.start()
    scalars.wait()
    for q in range(1, tiles - 1):
        loads[q].wait()
    measures.wait()

    def add(i, term):
        part_out[i // 2, i % 2] += term

    inner_patches(0, place_ref, probe_ref, w_ref, obj, held, patches, patch_out, patch_sems, add)
    keep.wait()
    for copy in halo:
        copy.wait()


def send(moves, send_sems, recv_sems, begin=True):
    copies = [
        pltpu.make_async_remote_copy(
            src_ref=source,
            dst_ref=target,
            send_sem=send_sems.at[i],
            recv_sem=recv_sems.at[i],
            device_id=around(*step),
            device_id_type=MESH,
        )
        for i, (source, target, step) in enumerate(moves)
    ]
    if begin:
        for copy in copies:
            copy.start()
    return copies


def halo_shapes(tile):
    planes, rows, cols = tile.shape
    shapes = [(planes, rows // 2, WIN)] * 2 + [(planes, RIM, cols)] * 2 + [(4, planes, RIM // 2, WIN)]
    return tuple(jax.ShapeDtypeStruct(s, jnp.float32) for s in shapes)


def gather_halo(count, positions, probe, tile, measured):
    planes, rows, cols = tile.shape
    hbm = pl.BlockSpec(memory_space=pl.ANY)
    smem = pl.BlockSpec(memory_space=pltpu.SMEM)
    vmem = pl.BlockSpec(memory_space=pltpu.VMEM)
    f32 = jnp.float32
    return pl.pallas_call(
        halo_body,
        out_shape=(
            *halo_shapes(tile),
            jax.ShapeDtypeStruct((EARLY, planes, WIN, WIN), f32),
            jax.ShapeDtypeStruct(probe.shape, f32),
            jax.ShapeDtypeStruct((8, WIN), jnp.int32),
        ),
        in_specs=[smem, vmem, vmem, vmem, hbm, hbm],
        out_specs=(*[hbm] * 6, vmem, hbm),
        scratch_shapes=[
            pltpu.VMEM((8, WIN), jnp.int32),
            pltpu.SMEM((8, WIN), jnp.int32),
            pltpu.SemaphoreType.DMA((2,)),
            pltpu.VMEM((planes, cols // WIN, rows, WIN), f32),
            pltpu.VMEM(measured.shape, f32),
            pltpu.VMEM((2, planes, rows // 2, WIN), f32),
            pltpu.VMEM((4, planes, RIM // 2, WIN), f32),
            pltpu.VMEM((2, WIDE, planes, WIN, WIN), f32),
            pltpu.SemaphoreType.DMA((cols // WIN,)),
            pltpu.SemaphoreType.DMA,
            pltpu.SemaphoreType.DMA((8,)),
            pltpu.SemaphoreType.DMA((8,)),
            pltpu.SemaphoreType.DMA((2,)),
        ],
        compiler_params=pltpu.CompilerParams(
            collective_id=0, has_side_effects=True, vmem_limit_bytes=56 * 1024 * 1024
        ),
        name="gather_halo",
    )(count, positions, probe, jnp.asarray(matrices()), tile, measured)


def ordered(positions, count, rows, cols):
    slots = positions.shape[0]
    row = positions[:, 0:1] - lax.axis_index("ty") * rows
    col = positions[:, 1:2] - lax.axis_index("tx") * cols
    shape = (slots, WIN)
    slot = lax.broadcasted_iota(jnp.int32, (slots, 1), 0)
    place = lax.broadcasted_iota(jnp.int32, shape, 1)
    inside = (row >= 0) & (row <= rows - WIN) & (col >= 0) & (col <= cols - WIN)
    alive = slot < count
    key = jnp.where(alive, jnp.where(inside, 0, 1), 2) * slots + slot
    wide = jnp.broadcast_to(key, shape)
    across = jnp.sum(jnp.where(place == slot, wide, 0), axis=0, keepdims=True)
    across = jnp.where(lax.broadcasted_iota(jnp.int32, (1, WIN), 1) < slots, across, 4 * slots)
    rank = jnp.sum(jnp.where(across < wide, 1, 0), axis=1, keepdims=True)
    hit = jnp.broadcast_to(rank, shape) == place
    safe_row = jnp.clip(row, 0, rows - WIN)
    safe_col = jnp.clip(col, 0, cols - WIN)
    q = safe_col // WIN
    lines = (slot, row + RIM, col + WIN, safe_row, q, jnp.minimum(q + 1, cols // WIN - 1), safe_col - q * WIN)
    lines = [jnp.sum(jnp.where(hit, line, 0), axis=0, keepdims=True) for line in lines]
    inner = jnp.sum(jnp.where(inside & alive, 1, 0), axis=0, keepdims=True)
    early = jnp.minimum(inner, EARLY)
    done = jnp.minimum(inner, EARLY + LATE)
    at = lax.broadcasted_iota(jnp.int32, (1, WIN), 1)
    last = jnp.where(at < inner, 1, 0)
    for i, number in enumerate((done, count, early, done - early)):
        last = jnp.where(at == slots + i, number, last)
    return jnp.concatenate([*lines, last], axis=0)


def tail_body(
    place_ref, probe_ref, w_ref, tile_ref, measured_ref,
    left_ref, right_ref, top_ref, bottom_ref, corner_ref, start_ref,
    left_out, right_out, top_out, bottom_out, corner_out, patch_out, total_out,
    obj, held, patches, part_ref, gathered, stage, in_sems, held_sem, patch_sems,
    send_sems, recv_sems, tx_send, tx_recv, ty_send, ty_recv, out_send, out_recv,
):
    ty, tx = lax.axis_index("ty"), lax.axis_index("tx")
    ny, nx = lax.axis_size("ty"), lax.axis_size("tx")
    diagonal = [around(*step) for step in AROUND if 0 not in step]
    greet(diagonal)
    barrier = pltpu.get_barrier_semaphore()

    @pl.loop(1, nx)
    def _(k):
        pl.semaphore_signal(barrier, inc=1, device_id={"tx": lax.rem(tx + k, nx)}, device_id_type=MESH)

    @pl.loop(1, ny)
    def _(k):
        pl.semaphore_signal(barrier, inc=1, device_id={"ty": lax.rem(ty + k, ny)}, device_id_type=MESH)

    tiles = tile_ref.shape[2] // WIN
    loads = [
        pltpu.make_async_copy(tile_ref.at[:, :, pl.ds(q * WIN, WIN)], obj.at[:, q], in_sems.at[q])
        for q in range(tiles)
    ]
    loads.append(pltpu.make_async_copy(measured_ref, held, held_sem))
    for copy in loads:
        copy.start()
    part_ref[...] = start_ref[...]
    pl.semaphore_wait(barrier, len(diagonal) + nx - 1 + ny - 1)

    def to_column(k, source, target, sends, receives):
        return pltpu.make_async_remote_copy(
            src_ref=source,
            dst_ref=target,
            send_sem=sends.at[k],
            recv_sem=receives.at[tx],
            device_id={"tx": lax.rem(tx + k, nx)},
            device_id_type=MESH,
        )

    def to_row(k):
        return pltpu.make_async_remote_copy(
            src_ref=stage.at[ty],
            dst_ref=stage.at[ty],
            send_sem=ty_send.at[k],
            recv_sem=ty_recv.at[ty],
            device_id={"ty": lax.rem(ty + k, ny)},
            device_id_type=MESH,
        )

    def arrived(target, semaphore):
        pltpu.make_async_copy(target, target, semaphore).wait()

    def spread(k):
        return to_column(k, part_ref.at[lax.rem(tx + k, nx)], gathered.at[tx], tx_send, tx_recv)

    def share(k):
        return to_column(k, total_out.at[tx], total_out.at[tx], out_send, out_recv)

    moves = (
        (left_ref, right_out, (0, -1)),
        (right_ref, left_out, (0, 1)),
        (top_ref, bottom_out, (-1, 0)),
        (bottom_ref, top_out, (1, 0)),
        (corner_ref.at[0], corner_out.at[3], (-1, -1)),
        (corner_ref.at[1], corner_out.at[2], (-1, 1)),
        (corner_ref.at[2], corner_out.at[1], (1, -1)),
        (corner_ref.at[3], corner_out.at[0], (1, 1)),
    )
    halo = send(moves, send_sems, recv_sems, begin=False)
    for copy in halo[:2]:
        copy.start()
    for copy in loads:
        copy.wait()

    def add(i, term):
        each = part_ref.shape[0] // 4
        part_ref[pl.ds(i * each, each)] += term.reshape(each, WIN // each, WIN)

    inner_patches(EARLY, place_ref, probe_ref, w_ref, obj, held, patches, patch_out, patch_sems, add)

    @pl.loop(1, nx)
    def _(k):
        spread(k).start()

    for copy in (halo[2], *halo[4:6]):
        copy.start()
    stage[ty] = part_ref[tx]

    @pl.loop(1, nx)
    def _(k):
        source = lax.rem(tx + k, nx)
        arrived(gathered.at[source], tx_recv.at[source])
        stage[ty] += gathered[source]

    @pl.loop(1, ny)
    def _(k):
        to_row(k).start()

    for copy in (halo[3], *halo[6:]):
        copy.start()

    @pl.loop(1, ny)
    def _(k):
        source = lax.rem(ty + k, ny)
        arrived(stage.at[source], ty_recv.at[source])

    total = stage[0]
    for i in range(1, stage.shape[0]):
        total += stage[i]
    total_out[tx] = total * (1.0 / SLOTS_ALL)

    @pl.loop(1, nx)
    def _(k):
        share(k).start()

    @pl.loop(1, nx)
    def _(k):
        source = lax.rem(tx + k, nx)
        arrived(total_out.at[source], out_recv.at[source])

    for copy in halo:
        copy.wait()

    @pl.loop(1, nx)
    def _(k):
        spread(k).wait_send()
        share(k).wait_send()

    @pl.loop(1, ny)
    def _(k):
        to_row(k).wait_send()


def exchange(places, probe, tile, measured, halo, part):
    hbm = pl.BlockSpec(memory_space=pl.ANY)
    vmem = pl.BlockSpec(memory_space=pltpu.VMEM)
    smem = pl.BlockSpec(memory_space=pltpu.SMEM)
    planes, rows, cols = tile.shape
    ny, nx = lax.axis_size("ty"), lax.axis_size("tx")
    chunk = (part.size // (nx * WIN), WIN)
    return pl.pallas_call(
        tail_body,
        out_shape=(
            *(jax.ShapeDtypeStruct(h.shape, jnp.float32) for h in halo),
            jax.ShapeDtypeStruct((LATE, planes, WIN, WIN), jnp.float32),
            jax.ShapeDtypeStruct((nx, *chunk), jnp.float32),
        ),
        in_specs=[smem, vmem, vmem] + [hbm] * 7 + [vmem],
        out_specs=(*[hbm] * 6, vmem),
        scratch_shapes=[
            pltpu.VMEM((planes, cols // WIN, rows, WIN), jnp.float32),
            pltpu.VMEM(measured.shape, jnp.float32),
            pltpu.VMEM((2, WIDE, planes, WIN, WIN), jnp.float32),
            pltpu.VMEM((nx, *chunk), jnp.float32),
            pltpu.VMEM((nx, *chunk), jnp.float32),
            pltpu.VMEM((ny, *chunk), jnp.float32),
            pltpu.SemaphoreType.DMA((cols // WIN,)),
            pltpu.SemaphoreType.DMA,
            pltpu.SemaphoreType.DMA((2,)),
            pltpu.SemaphoreType.DMA((8,)),
            pltpu.SemaphoreType.DMA((8,)),
            pltpu.SemaphoreType.DMA((nx,)),
            pltpu.SemaphoreType.DMA((nx,)),
            pltpu.SemaphoreType.DMA((ny,)),
            pltpu.SemaphoreType.DMA((ny,)),
            pltpu.SemaphoreType.DMA((nx,)),
            pltpu.SemaphoreType.DMA((nx,)),
        ],
        compiler_params=pltpu.CompilerParams(
            collective_id=1, has_side_effects=True, vmem_limit_bytes=56 * 1024 * 1024
        ),
        name="exchange",
    )(places, probe, jnp.asarray(matrices()), tile, measured, *halo, part.reshape(nx, *chunk))


def finish_body(
    place_ref, tile_ref, left_ref, right_ref, top_ref, bottom_ref, corner_ref, patch_ref, total_ref,
    out_ref, total_out, grad, sides, rims, corners, patches, in_sems, more_sems,
):
    planes, rows, cols = tile_ref.shape
    tiles = cols // WIN
    ty, tx = lax.axis_index("ty"), lax.axis_index("tx")
    ny, nx = lax.axis_size("ty"), lax.axis_size("tx")
    late = place_ref[7, SLOTS + 3]
    spans = [pl.ds(q * WIN, WIN) for q in range(tiles)]
    more = (
        (patch_ref, patches),
        (left_ref, sides.at[0]),
        (right_ref, sides.at[1]),
        (top_ref, rims.at[0]),
        (bottom_ref, rims.at[1]),
        (corner_ref, corners),
    )
    more = [pltpu.make_async_copy(a, b, more_sems.at[i]) for i, (a, b) in enumerate(more)]
    reads = [
        [
            pltpu.make_async_copy(tile_ref.at[p, :, span], grad.at[p, q], in_sems.at[p, q])
            for q, span in enumerate(spans)
        ]
        for p in range(planes)
    ]
    for copy in (more[0], *reads[0], *more[1:], *reads[1]):
        copy.start()
    total_out[...] = total_ref[...]
    no_side = (tx == 0, tx == nx - 1)
    no_end = (ty == 0, ty == ny - 1)
    ends = (0, rows - RIM)

    def side_add(plane, side, start, packed, gone):
        high = side == 1
        half = packed.shape[0]
        far = lax.broadcasted_iota(jnp.int32, packed.shape, 1) >= RIM
        mine = far if high else jnp.logical_not(far)
        for i, value in enumerate(unpack(packed, high)):
            here = pl.ds(start + i * half, half)
            value = jnp.where(gone, 0.0, value)
            grad[plane, side * (tiles - 1), here, :] += jnp.where(mine, value, 0.0)

    for plane in range(planes):
        for copy in reads[plane]:
            copy.wait()
        if plane == 0:
            more[0].wait()
        for place in range(patches.shape[0]):
            @pl.when(place < late)
            def _(place=place):
                at = EARLY + place
                row, q, q_next, shift = place_ref[3, at], place_ref[4, at], place_ref[5, at], place_ref[6, at]
                here = pl.ds(row, WIN)
                after = lax.broadcasted_iota(jnp.int32, (WIN, WIN), 1) >= shift
                turned = pltpu.roll(patches[place, plane], shift, 1)
                grad[plane, q, here, :] += jnp.where(after, turned, 0.0)
                grad[plane, q_next, here, :] += jnp.where(after, 0.0, turned)
        if plane == 0:
            for copy in more[1:]:
                copy.wait()
        for side in range(2):
            side_add(plane, side, 0, sides[side, plane], no_side[side])
            for end in range(2):
                gone = jnp.logical_or(no_side[side], no_end[end])
                side_add(plane, side, ends[end], corners[2 * end + side, plane], gone)
        for end in range(2):
            for q in range(tiles):
                value = jnp.where(no_end[end], 0.0, rims[end, plane, :, spans[q]])
                grad[plane, q, pl.ds(ends[end], RIM), :] += value
        for q in range(tiles):
            pltpu.make_async_copy(grad.at[plane, q], out_ref.at[plane, :, spans[q]], in_sems.at[plane, q]).start()
    for plane in range(planes):
        for q in range(tiles):
            pltpu.make_async_copy(grad.at[plane, q], out_ref.at[plane, :, spans[q]], in_sems.at[plane, q]).wait()


def finish(places, tile, halo, patches, total):
    planes, rows, cols = tile.shape
    hbm = pl.BlockSpec(memory_space=pl.ANY)
    vmem = pl.BlockSpec(memory_space=pltpu.VMEM)
    smem = pl.BlockSpec(memory_space=pltpu.SMEM)
    f32 = jnp.float32
    return pl.pallas_call(
        finish_body,
        out_shape=(jax.ShapeDtypeStruct(tile.shape, f32), jax.ShapeDtypeStruct(total.shape, f32)),
        in_specs=[smem] + [hbm] * 7 + [vmem],
        out_specs=(hbm, vmem),
        scratch_shapes=[
            pltpu.VMEM((planes, cols // WIN, rows, WIN), f32),
            pltpu.VMEM((2, planes, rows // 2, WIN), f32),
            pltpu.VMEM((2, planes, RIM, cols), f32),
            pltpu.VMEM((4, planes, RIM // 2, WIN), f32),
            pltpu.VMEM(patches.shape, f32),
            pltpu.SemaphoreType.DMA((planes, cols // WIN)),
            pltpu.SemaphoreType.DMA((6,)),
        ],
        compiler_params=pltpu.CompilerParams(vmem_limit_bytes=56 * 1024 * 1024),
        name="finish",
    )(places, tile, *halo, patches, total)


def shards(object_planes, probe, positions, counts, amplitudes):
    planes, rows, cols = object_planes.shape
    measured = amplitudes[0, 0]
    *halo, patches, early_part, places = gather_halo(counts, positions[0, 0], probe, object_planes, measured)
    tile, *outer, part = tile_gradient(places, probe, object_planes, halo, measured, patches, early_part)
    *outer, patches, total = exchange(places, probe, object_planes, measured, outer, part)
    tile, total = finish(places, tile, outer, patches, total)
    return tile, total.reshape(probe.shape)


def solution(mesh):
    in_specs = (
        P(None, "ty", "tx"),
        P(),
        P("ty", "tx", None, None),
        P("ty", "tx"),
        P("ty", "tx", None, None, None),
    )
    out_specs = (P(None, "ty", "tx"), P())
    return jax.shard_map(shards, mesh=mesh, in_specs=in_specs, out_specs=out_specs, check_vma=False)
```

```python
import math

import jax
import jax.numpy as jnp
import numpy as np
from jax import lax
from jax.experimental import pallas as pl
from jax.experimental.pallas import tpu as pltpu
from jax.sharding import PartitionSpec as P

WIN = 128
RIM = WIN // 2
FLOOR = 0.25
AHEAD = 16
MESH = pl.DeviceIdType.MESH
SLOTS_ALL = 8 * 16 * 96
U = 8
SMALL = 4
WIDE = 16
STAGES = 7
EARLY = 48
LATE = 16


def matrices():
    index = np.arange(WIN)
    angle = 2.0 * math.pi / WIN * ((index[:, None] * index[None, :]) % WIN)
    cosine = np.cos(angle) / math.sqrt(WIN)
    sine = np.sin(angle) / math.sqrt(WIN)
    right = np.block([[cosine, -sine], [sine, cosine]])
    both = np.stack([right, right.T]).astype(np.float32)
    high = both.astype(jnp.bfloat16)
    low = (both - high.astype(np.float32)).astype(jnp.bfloat16)
    return np.stack([high, low], axis=1)


def split(value):
    high = value.astype(jnp.bfloat16)
    low = (value - high.astype(jnp.float32)).astype(jnp.bfloat16)
    return high, low


def dot(a, b):
    return lax.dot_general(a, b, (((1,), (0,)), ((), ())), preferred_element_type=jnp.float32)


def blocks(value):
    n = WIN
    return value[:n, :n], value[:n, n:], value[n:, :n], value[n:, n:]


def assemble(a, b, c, d):
    top = jnp.concatenate([a, b], axis=1)
    bottom = jnp.concatenate([c, d], axis=1)
    return jnp.concatenate([top, bottom], axis=0)


def right_product(value, w_ref, k):
    high, low = split(value)
    return dot(high, w_ref[k, 0]) + dot(low, w_ref[k, 0]) + dot(high, w_ref[k, 1])


def left_product(value, w_ref, k):
    high, low = split(value)
    return dot(w_ref[k, 0], high) + dot(w_ref[k, 0], low) + dot(w_ref[k, 1], high)


def slot_steps(window, probe_ref, measured, live, w_ref):
    a, b = window
    p0r, p0i = probe_ref[0, 0], probe_ref[0, 1]
    p1r, p1i = probe_ref[1, 0], probe_ref[1, 1]
    wave = assemble(
        p0r * a - p0i * b,
        p0r * b + p0i * a,
        p1r * a - p1i * b,
        p1r * b + p1i * a,
    )
    yield
    half = right_product(wave, w_ref, 0)
    yield
    m0r, m0i, m1r, m1i = blocks(half)
    far = left_product(assemble(m0r, m1r, m0i, m1i), w_ref, 1)
    yield
    f0r, f1r, f0i, f1i = blocks(far)
    intensity = f0r * f0r + f0i * f0i + (f1r * f1r + f1i * f1i)
    weight = live - (live * measured) * lax.rsqrt(jnp.maximum(intensity, FLOOR))
    value = assemble(weight * f0r, weight * f1r, weight * f0i, weight * f1i)
    yield
    half = left_product(value, w_ref, 0)
    yield
    m0r, m1r, m0i, m1i = blocks(half)
    back = right_product(assemble(m0r, m0i, m1r, m1i), w_ref, 1)
    yield
    b0r, b0i, b1r, b1i = blocks(back)
    grad_re = p0r * b0r + p0i * b0i + (p1r * b1r + p1i * b1i)
    grad_im = p0r * b0i - p0i * b0r + (p1r * b1i - p1i * b1r)
    yield grad_re, grad_im, (a * b0r + b * b0i, a * b0i - b * b0r, a * b1r + b * b1i, a * b1i - b * b1r)


def pipelined(start, finish, size):
    runs = [None] * size
    for moment in range(STAGES + size - 1):
        for u in reversed(range(size)):
            stage = moment - u
            if 0 <= stage < STAGES:
                if stage == 0:
                    runs[u] = start(u)
                result = next(runs[u])
                if stage == STAGES - 1:
                    finish(u, *result)


def take(obj, row, q, q_next, shift):
    here = pl.ds(row, WIN)
    keep = lax.broadcasted_iota(jnp.int32, (WIN, WIN), 1) < WIN - shift
    window = []
    for plane in range(2):
        first = pltpu.roll(obj[plane, q, here, :], WIN - shift, 1)
        second = pltpu.roll(obj[plane, q_next, here, :], WIN - shift, 1)
        window.append(jnp.where(keep, first, second))
    return window


def put(grad, row, q, shift, values, q_next=None):
    here = pl.ds(row, WIN)
    after = lax.broadcasted_iota(jnp.int32, (WIN, WIN), 1) >= shift
    q_next = q + 1 if q_next is None else q_next
    for plane, value in enumerate(values):
        turned = pltpu.roll(value, shift, 1)
        grad[plane, q, here, :] += jnp.where(after, turned, 0.0)
        grad[plane, q_next, here, :] += jnp.where(after, 0.0, turned)


def pack(value, high):
    half = value.shape[0] // 2
    first, second = value[:half], value[half:]
    near = lax.broadcasted_iota(jnp.int32, first.shape, 1) < RIM
    if high:
        first = pltpu.roll(first, RIM, 1)
    else:
        second = pltpu.roll(second, RIM, 1)
    return jnp.where(near, first, second)


def unpack(packed, high):
    turned = pltpu.roll(packed, RIM, 1)
    return (turned, packed) if high else (packed, turned)


def deposit(grad, patches, info_of, first):
    for place in range(first, first + U):
        row, q, shift, q_next = info_of(place)
        put(grad, row, q, shift, (patches[place, 0], patches[place, 1]), q_next)


def body(
    place_ref, probe_ref, w_ref, tile_ref, left_ref, right_ref, top_ref, bottom_ref, corner_ref,
    measured_ref, patch_ref, part_ref,
    grad_tile, grad_left, grad_right, grad_top, grad_bottom, grad_corner, probe_out,
    obj, grad, held, sides, corners, patches, in_sems, held_sems, patch_sems,
):
    rows = tile_ref.shape[1]
    cols = tile_ref.shape[2]
    tiles = cols // WIN
    slots_max = measured_ref.shape[0]
    begin, count = (place_ref[7, slots_max + i] for i in range(2))

    def fetch(place):
        turn = lax.rem(place - begin, AHEAD)
        return pltpu.make_async_copy(measured_ref.at[place_ref[0, place]], held.at[turn], held_sems.at[turn])

    for ahead in range(AHEAD):
        @pl.when(begin + ahead < count)
        def _(ahead=ahead):
            fetch(begin + ahead).start()

    last = tiles + 1
    low = RIM + rows
    middle = RIM + rows // 2
    loads = []
    for q in range(tiles):
        span = pl.ds(q * WIN, WIN)
        loads.append((tile_ref.at[:, :, span], obj.at[:, q + 1, pl.ds(RIM, rows), :]))
        loads.append((top_ref.at[:, :, span], obj.at[:, q + 1, pl.ds(0, RIM), :]))
        loads.append((bottom_ref.at[:, :, span], obj.at[:, q + 1, pl.ds(low, RIM), :]))
    loads.append((corner_ref, corners))
    loads.append((left_ref, sides.at[0]))
    loads.append((right_ref, sides.at[1]))
    loads = [pltpu.make_async_copy(a, b, in_sems.at[i]) for i, (a, b) in enumerate(loads)]
    pieces = patch_ref.shape[0] // U
    chunks = [
        pltpu.make_async_copy(patch_ref.at[pl.ds(i * U, U)], patches.at[pl.ds(i * U, U)], patch_sems.at[i])
        for i in range(pieces)
    ]
    for copy in chunks[:2] + loads + chunks[2:]:
        copy.start()
    grad[...] = jnp.zeros_like(grad)
    probe_out[...] = part_ref[...]

    def info_of(place):
        safe = jnp.minimum(place, slots_max - 1)
        row, col = place_ref[1, safe], place_ref[2, safe]
        return row, col // WIN, lax.rem(col, WIN), col // WIN + 1

    for i, copy in enumerate(chunks):
        copy.wait()
        deposit(grad, patches, info_of, i * U)
    for copy in loads:
        copy.wait()
    for plane in range(2):
        for q, high in ((0, True), (last, False)):
            side = 0 if high else 1
            pieces = ((corners[side, plane], 0), (sides[side, plane], RIM), (corners[2 + side, plane], low))
            for packed, start in pieces:
                half = packed.shape[0]
                for i, value in enumerate(unpack(packed, high)):
                    obj[plane, q, pl.ds(start + i * half, half), :] = value
    ty, tx = lax.axis_index("ty"), lax.axis_index("tx")

    @pl.when(ty == 0)
    def _():
        obj[:, :, pl.ds(0, RIM), :] = jnp.zeros((2, tiles + 2, RIM, WIN), jnp.float32)

    @pl.when(ty == lax.axis_size("ty") - 1)
    def _():
        obj[:, :, pl.ds(low, RIM), :] = jnp.zeros((2, tiles + 2, RIM, WIN), jnp.float32)

    @pl.when(tx == 0)
    def _():
        obj[:, 0] = jnp.zeros((2, rows + WIN, WIN), jnp.float32)

    @pl.when(tx == lax.axis_size("tx") - 1)
    def _():
        obj[:, last] = jnp.zeros((2, rows + WIN, WIN), jnp.float32)


    def run(first, size):
        places = [first + u for u in range(size)]
        for place in places:
            @pl.when(place < count)
            def _(place=place):
                fetch(place).wait()
        terms = []

        def start(u):
            row, q, shift, q_next = info_of(places[u])
            window = take(obj, row, q, q_next, shift)
            live = jnp.where(places[u] < count, 1.0, 0.0)
            return slot_steps(window, probe_ref, held[lax.rem(places[u] - begin, AHEAD)], live, w_ref)

        def finish(u, grad_re, grad_im, term):
            row, q, shift, q_next = info_of(places[u])
            put(grad, row, q, shift, (grad_re, grad_im), q_next)
            terms.append(term)

        pipelined(start, finish, size)
        for i in range(4):
            probe_out[i // 2, i % 2] += sum(term[i] for term in terms)
        for place in places:
            @pl.when(place + AHEAD < count)
            def _(place=place):
                fetch(place + AHEAD).start()

    rest = count - begin
    whole = (rest + SMALL - 1) // U

    @pl.loop(0, whole)
    def _(group):
        run(begin + group * U, U)

    @pl.when(rest > whole * U)
    def _():
        run(begin + whole * U, SMALL)

    stores = []
    for q in range(tiles):
        span = pl.ds(q * WIN, WIN)
        stores.append((grad.at[:, q + 1, pl.ds(RIM, rows), :], grad_tile.at[:, :, span]))
        stores.append((grad.at[:, q + 1, pl.ds(0, RIM), :], grad_top.at[:, :, span]))
        stores.append((grad.at[:, q + 1, pl.ds(low, RIM), :], grad_bottom.at[:, :, span]))
    stores.append((corners, grad_corner))
    stores.append((sides.at[0], grad_left))
    stores.append((sides.at[1], grad_right))
    stores = [pltpu.make_async_copy(a, b, in_sems.at[i]) for i, (a, b) in enumerate(stores)]
    for copy in stores[:-3]:
        copy.start()
    for plane in range(2):
        for q, high in ((0, True), (last, False)):
            side = 0 if high else 1
            corners[side, plane] = pack(grad[plane, q, pl.ds(0, RIM), :], high)
            corners[2 + side, plane] = pack(grad[plane, q, pl.ds(low, RIM), :], high)
            sides[side, plane] = pack(grad[plane, q, pl.ds(RIM, rows), :], high)
    for copy in stores[-3:]:
        copy.start()
    for copy in stores:
        copy.wait()


def tile_gradient(places, probe, tile, halo, measured, patches, part):
    planes, rows, cols = tile.shape
    tiles = cols // WIN
    f32 = jnp.float32
    smem = pl.BlockSpec(memory_space=pltpu.SMEM)
    vmem = pl.BlockSpec(memory_space=pltpu.VMEM)
    hbm = pl.BlockSpec(memory_space=pl.ANY)
    extent = (planes, tiles + 2, rows + WIN, WIN)
    copies = 3 * tiles + 3
    return pl.pallas_call(
        body,
        out_shape=(
            jax.ShapeDtypeStruct(tile.shape, f32),
            *(jax.ShapeDtypeStruct(h.shape, f32) for h in halo),
            jax.ShapeDtypeStruct(probe.shape, f32),
        ),
        in_specs=[smem, vmem, vmem] + [hbm] * 8 + [vmem],
        out_specs=(*[hbm] * 6, vmem),
        scratch_shapes=[
            pltpu.VMEM(extent, f32),
            pltpu.VMEM(extent, f32),
            pltpu.VMEM((AHEAD, WIN, WIN), f32),
            pltpu.VMEM((2, planes, rows // 2, WIN), f32),
            pltpu.VMEM((4, planes, RIM // 2, WIN), f32),
            pltpu.VMEM(patches.shape, f32),
            pltpu.SemaphoreType.DMA((copies,)),
            pltpu.SemaphoreType.DMA((AHEAD,)),
            pltpu.SemaphoreType.DMA((patches.shape[0] // U,)),
        ],
        compiler_params=pltpu.CompilerParams(vmem_limit_bytes=56 * 1024 * 1024),
        name="tile_gradient",
    )(places, probe, jnp.asarray(matrices()), tile, *halo, measured, patches, part)


AROUND = ((-1, 0), (1, 0), (0, -1), (0, 1), (-1, -1), (-1, 1), (1, -1), (1, 1))


def ring(axis, by):
    size = lax.axis_size(axis)
    return lax.rem(lax.axis_index(axis) + (by + size), size)


def around(dy, dx):
    return {"ty": ring("ty", dy), "tx": ring("tx", dx)}


def greet(partners):
    barrier = pltpu.get_barrier_semaphore()
    for partner in partners:
        pl.semaphore_signal(barrier, inc=1, device_id=partner, device_id_type=MESH)


def inner_patches(
    begin, place_ref, probe_ref, w_ref, obj, held, patches, patch_out, patch_sems, add
):
    size = patches.shape[1]

    def store(group):
        turn = lax.rem(group, 2)
        return pltpu.make_async_copy(patches.at[turn], patch_out.at[pl.ds(group * size, size)], patch_sems.at[turn])

    groups = patch_out.shape[0] // size

    @pl.loop(0, groups)
    def _(group):
        turn = lax.rem(group, 2)

        @pl.when(group >= 2)
        def _():
            store(group - 2).wait()

        places = [begin + group * size + u for u in range(size)]

        def start(u):
            p = places[u]
            window = take(obj, place_ref[3, p], place_ref[4, p], place_ref[5, p], place_ref[6, p])
            return slot_steps(window, probe_ref, held[place_ref[0, p]], place_ref[7, p].astype(jnp.float32), w_ref)

        def finish(u, grad_re, grad_im, terms):
            patches[turn, u, 0] = grad_re
            patches[turn, u, 1] = grad_im
            for i, term in enumerate(terms):
                add(i, term)

        pipelined(start, finish, size)
        store(group).start()

    for group in range(max(groups - 2, 0), groups):
        store(group).wait()


def halo_body(
    count_ref, position_ref, probe_ref, w_ref, tile_ref, measured_ref,
    left_out, right_out, top_out, bottom_out, corner_out, patch_out, part_out, table_out,
    table, place_ref, table_sems, obj, held, packed, corners, patches, in_sems, held_sem, send_sems, recv_sems, patch_sems,
):
    rows, cols = tile_ref.shape[1:]
    tiles = cols // WIN
    greet([around(*step) for step in AROUND])
    loads = [
        pltpu.make_async_copy(tile_ref.at[:, :, pl.ds(q * WIN, WIN)], obj.at[:, q], in_sems.at[q])
        for q in range(tiles)
    ]
    for q in (0, tiles - 1, *range(1, tiles - 1)):
        loads[q].start()
    measures = pltpu.make_async_copy(measured_ref, held, held_sem)
    measures.start()
    part_out[...] = jnp.zeros_like(part_out)
    above, below = pl.ds(0, RIM), pl.ds(rows - RIM, RIM)
    pl.semaphore_wait(pltpu.get_barrier_semaphore(), len(AROUND))
    moves = (
        (packed.at[0], right_out, (0, -1)),
        (packed.at[1], left_out, (0, 1)),
        (tile_ref.at[:, above, :], bottom_out, (-1, 0)),
        (tile_ref.at[:, below, :], top_out, (1, 0)),
        (corners.at[3], corner_out.at[0], (1, 1)),
        (corners.at[2], corner_out.at[1], (1, -1)),
        (corners.at[1], corner_out.at[2], (-1, 1)),
        (corners.at[0], corner_out.at[3], (-1, -1)),
    )
    halo = send(moves, send_sems, recv_sems, begin=False)
    for copy in halo[2:4]:
        copy.start()
    for side, q in enumerate((0, tiles - 1)):
        loads[q].wait()
        for plane in range(2):
            packed[side, plane] = pack(obj[plane, q], side == 1)
            corners[side, plane] = pack(obj[plane, q, above, :], side == 1)
            corners[2 + side, plane] = pack(obj[plane, q, below, :], side == 1)
    for copy in (*halo[:2], *halo[4:]):
        copy.start()
    table[...] = ordered(position_ref[...], count_ref[0, 0], rows, cols)
    keep = pltpu.make_async_copy(table, table_out, table_sems.at[0])
    keep.start()
    scalars = pltpu.make_async_copy(table, place_ref, table_sems.at[1])
    scalars.start()
    scalars.wait()
    for q in range(1, tiles - 1):
        loads[q].wait()
    measures.wait()

    def add(i, term):
        part_out[i // 2, i % 2] += term

    inner_patches(0, place_ref, probe_ref, w_ref, obj, held, patches, patch_out, patch_sems, add)
    keep.wait()
    for copy in halo:
        copy.wait()


def send(moves, send_sems, recv_sems, begin=True):
    copies = [
        pltpu.make_async_remote_copy(
            src_ref=source,
            dst_ref=target,
            send_sem=send_sems.at[i],
            recv_sem=recv_sems.at[i],
            device_id=around(*step),
            device_id_type=MESH,
        )
        for i, (source, target, step) in enumerate(moves)
    ]
    if begin:
        for copy in copies:
            copy.start()
    return copies


def halo_shapes(tile):
    planes, rows, cols = tile.shape
    shapes = [(planes, rows // 2, WIN)] * 2 + [(planes, RIM, cols)] * 2 + [(4, planes, RIM // 2, WIN)]
    return tuple(jax.ShapeDtypeStruct(s, jnp.float32) for s in shapes)


def gather_halo(count, positions, probe, tile, measured):
    planes, rows, cols = tile.shape
    hbm = pl.BlockSpec(memory_space=pl.ANY)
    smem = pl.BlockSpec(memory_space=pltpu.SMEM)
    vmem = pl.BlockSpec(memory_space=pltpu.VMEM)
    f32 = jnp.float32
    return pl.pallas_call(
        halo_body,
        out_shape=(
            *halo_shapes(tile),
            jax.ShapeDtypeStruct((EARLY, planes, WIN, WIN), f32),
            jax.ShapeDtypeStruct(probe.shape, f32),
            jax.ShapeDtypeStruct((8, WIN), jnp.int32),
        ),
        in_specs=[smem, vmem, vmem, vmem, hbm, hbm],
        out_specs=(*[hbm] * 6, vmem, hbm),
        scratch_shapes=[
            pltpu.VMEM((8, WIN), jnp.int32),
            pltpu.SMEM((8, WIN), jnp.int32),
            pltpu.SemaphoreType.DMA((2,)),
            pltpu.VMEM((planes, cols // WIN, rows, WIN), f32),
            pltpu.VMEM(measured.shape, f32),
            pltpu.VMEM((2, planes, rows // 2, WIN), f32),
            pltpu.VMEM((4, planes, RIM // 2, WIN), f32),
            pltpu.VMEM((2, WIDE, planes, WIN, WIN), f32),
            pltpu.SemaphoreType.DMA((cols // WIN,)),
            pltpu.SemaphoreType.DMA,
            pltpu.SemaphoreType.DMA((8,)),
            pltpu.SemaphoreType.DMA((8,)),
            pltpu.SemaphoreType.DMA((2,)),
        ],
        compiler_params=pltpu.CompilerParams(
            collective_id=0, has_side_effects=True, vmem_limit_bytes=56 * 1024 * 1024
        ),
        name="gather_halo",
    )(count, positions, probe, jnp.asarray(matrices()), tile, measured)


def ordered(positions, count, rows, cols):
    slots = positions.shape[1]
    square = (slots, slots)
    same = lax.broadcasted_iota(jnp.int32, square, 0) == lax.broadcasted_iota(jnp.int32, square, 1)

    def upright(line):
        return jnp.sum(jnp.where(same, jnp.broadcast_to(line, square), 0), axis=1, keepdims=True)

    row = upright(positions[0:1]) - lax.axis_index("ty") * rows
    col = upright(positions[1:2]) - lax.axis_index("tx") * cols
    shape = (slots, WIN)
    slot = lax.broadcasted_iota(jnp.int32, (slots, 1), 0)
    place = lax.broadcasted_iota(jnp.int32, shape, 1)
    inside = (row >= 0) & (row <= rows - WIN) & (col >= 0) & (col <= cols - WIN)
    alive = slot < count
    key = jnp.where(alive, jnp.where(inside, 0, 1), 2) * slots + slot
    wide = jnp.broadcast_to(key, shape)
    across = jnp.sum(jnp.where(place == slot, wide, 0), axis=0, keepdims=True)
    across = jnp.where(lax.broadcasted_iota(jnp.int32, (1, WIN), 1) < slots, across, 4 * slots)
    rank = jnp.sum(jnp.where(across < wide, 1, 0), axis=1, keepdims=True)
    hit = jnp.broadcast_to(rank, shape) == place
    safe_row = jnp.clip(row, 0, rows - WIN)
    safe_col = jnp.clip(col, 0, cols - WIN)
    q = safe_col // WIN
    lines = (slot, row + RIM, col + WIN, safe_row, q, jnp.minimum(q + 1, cols // WIN - 1), safe_col - q * WIN)
    lines = [jnp.sum(jnp.where(hit, line, 0), axis=0, keepdims=True) for line in lines]
    inner = jnp.sum(jnp.where(inside & alive, 1, 0), axis=0, keepdims=True)
    early = jnp.minimum(inner, EARLY)
    done = jnp.minimum(inner, EARLY + LATE)
    at = lax.broadcasted_iota(jnp.int32, (1, WIN), 1)
    last = jnp.where(at < inner, 1, 0)
    for i, number in enumerate((done, count, early, done - early)):
        last = jnp.where(at == slots + i, number, last)
    return jnp.concatenate([*lines, last], axis=0)


def tail_body(
    place_ref, probe_ref, w_ref, tile_ref, measured_ref,
    left_ref, right_ref, top_ref, bottom_ref, corner_ref, start_ref,
    left_out, right_out, top_out, bottom_out, corner_out, patch_out, total_out,
    obj, held, patches, part_ref, gathered, stage, in_sems, held_sem, patch_sems,
    send_sems, recv_sems, tx_send, tx_recv, ty_send, ty_recv, out_send, out_recv,
):
    ty, tx = lax.axis_index("ty"), lax.axis_index("tx")
    ny, nx = lax.axis_size("ty"), lax.axis_size("tx")
    diagonal = [around(*step) for step in AROUND if 0 not in step]
    greet(diagonal)
    barrier = pltpu.get_barrier_semaphore()

    @pl.loop(1, nx)
    def _(k):
        pl.semaphore_signal(barrier, inc=1, device_id={"tx": lax.rem(tx + k, nx)}, device_id_type=MESH)

    @pl.loop(1, ny)
    def _(k):
        pl.semaphore_signal(barrier, inc=1, device_id={"ty": lax.rem(ty + k, ny)}, device_id_type=MESH)

    tiles = tile_ref.shape[2] // WIN
    loads = [
        pltpu.make_async_copy(tile_ref.at[:, :, pl.ds(q * WIN, WIN)], obj.at[:, q], in_sems.at[q])
        for q in range(tiles)
    ]
    loads.append(pltpu.make_async_copy(measured_ref, held, held_sem))
    for copy in loads:
        copy.start()
    part_ref[...] = start_ref[...]
    pl.semaphore_wait(barrier, len(diagonal) + nx - 1 + ny - 1)

    def to_column(k, source, target, sends, receives):
        return pltpu.make_async_remote_copy(
            src_ref=source,
            dst_ref=target,
            send_sem=sends.at[k],
            recv_sem=receives.at[tx],
            device_id={"tx": lax.rem(tx + k, nx)},
            device_id_type=MESH,
        )

    def to_row(k):
        return pltpu.make_async_remote_copy(
            src_ref=stage.at[ty],
            dst_ref=stage.at[ty],
            send_sem=ty_send.at[k],
            recv_sem=ty_recv.at[ty],
            device_id={"ty": lax.rem(ty + k, ny)},
            device_id_type=MESH,
        )

    def arrived(target, semaphore):
        pltpu.make_async_copy(target, target, semaphore).wait()

    def spread(k):
        return to_column(k, part_ref.at[lax.rem(tx + k, nx)], gathered.at[tx], tx_send, tx_recv)

    def share(k):
        return to_column(k, total_out.at[tx], total_out.at[tx], out_send, out_recv)

    moves = (
        (left_ref, right_out, (0, -1)),
        (right_ref, left_out, (0, 1)),
        (top_ref, bottom_out, (-1, 0)),
        (bottom_ref, top_out, (1, 0)),
        (corner_ref.at[0], corner_out.at[3], (-1, -1)),
        (corner_ref.at[1], corner_out.at[2], (-1, 1)),
        (corner_ref.at[2], corner_out.at[1], (1, -1)),
        (corner_ref.at[3], corner_out.at[0], (1, 1)),
    )
    halo = send(moves, send_sems, recv_sems, begin=False)
    for copy in halo[:2]:
        copy.start()
    for copy in loads:
        copy.wait()

    def add(i, term):
        each = part_ref.shape[0] // 4
        part_ref[pl.ds(i * each, each)] += term.reshape(each, WIN // each, WIN)

    inner_patches(EARLY, place_ref, probe_ref, w_ref, obj, held, patches, patch_out, patch_sems, add)

    @pl.loop(1, nx)
    def _(k):
        spread(k).start()

    for copy in (halo[2], *halo[4:6]):
        copy.start()
    stage[ty] = part_ref[tx]

    @pl.loop(1, nx)
    def _(k):
        source = lax.rem(tx + k, nx)
        arrived(gathered.at[source], tx_recv.at[source])
        stage[ty] += gathered[source]

    @pl.loop(1, ny)
    def _(k):
        to_row(k).start()

    for copy in (halo[3], *halo[6:]):
        copy.start()

    @pl.loop(1, ny)
    def _(k):
        source = lax.rem(ty + k, ny)
        arrived(stage.at[source], ty_recv.at[source])

    total = stage[0]
    for i in range(1, stage.shape[0]):
        total += stage[i]
    total_out[tx] = total * (1.0 / SLOTS_ALL)

    @pl.loop(1, nx)
    def _(k):
        share(k).start()

    @pl.loop(1, nx)
    def _(k):
        source = lax.rem(tx + k, nx)
        arrived(total_out.at[source], out_recv.at[source])

    for copy in halo:
        copy.wait()

    @pl.loop(1, nx)
    def _(k):
        spread(k).wait_send()
        share(k).wait_send()

    @pl.loop(1, ny)
    def _(k):
        to_row(k).wait_send()


def exchange(places, probe, tile, measured, halo, part):
    hbm = pl.BlockSpec(memory_space=pl.ANY)
    vmem = pl.BlockSpec(memory_space=pltpu.VMEM)
    smem = pl.BlockSpec(memory_space=pltpu.SMEM)
    planes, rows, cols = tile.shape
    ny, nx = lax.axis_size("ty"), lax.axis_size("tx")
    chunk = (part.size // (nx * WIN), WIN)
    return pl.pallas_call(
        tail_body,
        out_shape=(
            *(jax.ShapeDtypeStruct(h.shape, jnp.float32) for h in halo),
            jax.ShapeDtypeStruct((LATE, planes, WIN, WIN), jnp.float32),
            jax.ShapeDtypeStruct((nx, *chunk), jnp.float32),
        ),
        in_specs=[smem, vmem, vmem] + [hbm] * 7 + [vmem],
        out_specs=(*[hbm] * 6, vmem),
        scratch_shapes=[
            pltpu.VMEM((planes, cols // WIN, rows, WIN), jnp.float32),
            pltpu.VMEM(measured.shape, jnp.float32),
            pltpu.VMEM((2, WIDE, planes, WIN, WIN), jnp.float32),
            pltpu.VMEM((nx, *chunk), jnp.float32),
            pltpu.VMEM((nx, *chunk), jnp.float32),
            pltpu.VMEM((ny, *chunk), jnp.float32),
            pltpu.SemaphoreType.DMA((cols // WIN,)),
            pltpu.SemaphoreType.DMA,
            pltpu.SemaphoreType.DMA((2,)),
            pltpu.SemaphoreType.DMA((8,)),
            pltpu.SemaphoreType.DMA((8,)),
            pltpu.SemaphoreType.DMA((nx,)),
            pltpu.SemaphoreType.DMA((nx,)),
            pltpu.SemaphoreType.DMA((ny,)),
            pltpu.SemaphoreType.DMA((ny,)),
            pltpu.SemaphoreType.DMA((nx,)),
            pltpu.SemaphoreType.DMA((nx,)),
        ],
        compiler_params=pltpu.CompilerParams(
            collective_id=1, has_side_effects=True, vmem_limit_bytes=56 * 1024 * 1024
        ),
        name="exchange",
    )(places, probe, jnp.asarray(matrices()), tile, measured, *halo, part.reshape(nx, *chunk))


def finish_body(
    place_ref, tile_ref, left_ref, right_ref, top_ref, bottom_ref, corner_ref, patch_ref, total_ref,
    out_ref, total_out, grad, sides, rims, corners, patches, in_sems, more_sems,
):
    planes, rows, cols = tile_ref.shape
    tiles = cols // WIN
    ty, tx = lax.axis_index("ty"), lax.axis_index("tx")
    ny, nx = lax.axis_size("ty"), lax.axis_size("tx")
    spans = [pl.ds(q * WIN, WIN) for q in range(tiles)]
    more = (
        (patch_ref, patches),
        (left_ref, sides.at[0]),
        (right_ref, sides.at[1]),
        (top_ref, rims.at[0]),
        (bottom_ref, rims.at[1]),
        (corner_ref, corners),
    )
    more = [pltpu.make_async_copy(a, b, more_sems.at[i]) for i, (a, b) in enumerate(more)]
    reads = [
        [
            pltpu.make_async_copy(tile_ref.at[p, :, span], grad.at[p, q], in_sems.at[p, q])
            for q, span in enumerate(spans)
        ]
        for p in range(planes)
    ]
    for copy in (more[0], *reads[0], *more[1:], *reads[1]):
        copy.start()
    total_out[...] = total_ref[...]
    no_side = (tx == 0, tx == nx - 1)
    no_end = (ty == 0, ty == ny - 1)
    ends = (0, rows - RIM)

    def side_add(plane, side, start, packed, gone):
        high = side == 1
        half = packed.shape[0]
        far = lax.broadcasted_iota(jnp.int32, packed.shape, 1) >= RIM
        mine = far if high else jnp.logical_not(far)
        for i, value in enumerate(unpack(packed, high)):
            here = pl.ds(start + i * half, half)
            value = jnp.where(gone, 0.0, value)
            grad[plane, side * (tiles - 1), here, :] += jnp.where(mine, value, 0.0)

    for plane in range(planes):
        for copy in reads[plane]:
            copy.wait()
        if plane == 0:
            more[0].wait()
        for place in range(patches.shape[0]):
            at = EARLY + place
            row, q, q_next, shift = place_ref[3, at], place_ref[4, at], place_ref[5, at], place_ref[6, at]
            here = pl.ds(row, WIN)
            after = lax.broadcasted_iota(jnp.int32, (WIN, WIN), 1) >= shift
            turned = pltpu.roll(patches[place, plane], shift, 1)
            grad[plane, q, here, :] += jnp.where(after, turned, 0.0)
            grad[plane, q_next, here, :] += jnp.where(after, 0.0, turned)
        if plane == 0:
            for copy in more[1:]:
                copy.wait()
        for side in range(2):
            side_add(plane, side, 0, sides[side, plane], no_side[side])
            for end in range(2):
                gone = jnp.logical_or(no_side[side], no_end[end])
                side_add(plane, side, ends[end], corners[2 * end + side, plane], gone)
        for end in range(2):
            for q in range(tiles):
                value = jnp.where(no_end[end], 0.0, rims[end, plane, :, spans[q]])
                grad[plane, q, pl.ds(ends[end], RIM), :] += value
        for q in range(tiles):
            pltpu.make_async_copy(grad.at[plane, q], out_ref.at[plane, :, spans[q]], in_sems.at[plane, q]).start()
    for plane in range(planes):
        for q in range(tiles):
            pltpu.make_async_copy(grad.at[plane, q], out_ref.at[plane, :, spans[q]], in_sems.at[plane, q]).wait()


def finish(places, tile, halo, patches, total):
    planes, rows, cols = tile.shape
    hbm = pl.BlockSpec(memory_space=pl.ANY)
    vmem = pl.BlockSpec(memory_space=pltpu.VMEM)
    smem = pl.BlockSpec(memory_space=pltpu.SMEM)
    f32 = jnp.float32
    return pl.pallas_call(
        finish_body,
        out_shape=(jax.ShapeDtypeStruct(tile.shape, f32), jax.ShapeDtypeStruct(total.shape, f32)),
        in_specs=[smem] + [hbm] * 7 + [vmem],
        out_specs=(hbm, vmem),
        scratch_shapes=[
            pltpu.VMEM((planes, cols // WIN, rows, WIN), f32),
            pltpu.VMEM((2, planes, rows // 2, WIN), f32),
            pltpu.VMEM((2, planes, RIM, cols), f32),
            pltpu.VMEM((4, planes, RIM // 2, WIN), f32),
            pltpu.VMEM(patches.shape, f32),
            pltpu.SemaphoreType.DMA((planes, cols // WIN)),
            pltpu.SemaphoreType.DMA((6,)),
        ],
        compiler_params=pltpu.CompilerParams(vmem_limit_bytes=56 * 1024 * 1024),
        name="finish",
    )(places, tile, *halo, patches, total)


def shards(object_planes, probe, positions, counts, amplitudes):
    planes, rows, cols = object_planes.shape
    measured = amplitudes[0, 0]
    *halo, patches, early_part, places = gather_halo(counts, positions[0, 0].T, probe, object_planes, measured)
    tile, *outer, part = tile_gradient(places, probe, object_planes, halo, measured, patches, early_part)
    *outer, patches, total = exchange(places, probe, object_planes, measured, outer, part)
    tile, total = finish(places, tile, outer, patches, total)
    return tile, total.reshape(probe.shape)


def solution(mesh):
    in_specs = (
        P(None, "ty", "tx"),
        P(),
        P("ty", "tx", None, None),
        P("ty", "tx"),
        P("ty", "tx", None, None, None),
    )
    out_specs = (P(None, "ty", "tx"), P())
    return jax.shard_map(shards, mesh=mesh, in_specs=in_specs, out_specs=out_specs, check_vma=False)
```
